128 devices in a mesh: grp: 16 (over x, y_lo, core), dev: 8 (over y_hi, z).
Axes of the slice: x: 4, y: 4 (y_hi: 2, y_lo: 2; y = y_hi * 2 + y_lo), z: 4, core: 2. Of those that a mesh axis runs over, the one named last changes fastest.
Arguments:
- tile_patches: bfloat16 [12288, 588], P(('grp', 'dev')), may hold values from -6 to 6
- w_patch: bfloat16 [588, 1536], replicated, may hold values from -0.25 to 0.25
- w_tqkv: bfloat16 [3, 1536, 1536], P(None, None, 'dev'), may hold values from -6 to 6
- w_to: bfloat16 [1536, 1536], P('dev'), may hold values from -0.15625 to 0.15625
- w_gu: bfloat16 [2, 1536, 4096], P(None, None, 'dev'), may hold values from -0.15625 to 0.15625
- w_down: bfloat16 [4096, 1536], P('dev'), may hold values from -0.09375 to 0.09375
- tile_gain: float32 [3, 1536], replicated, may hold values from 0.1 to 1.9
- w_in: bfloat16 [1536, 768], replicated, may hold values from -0.15625 to 0.15625
- slide_tokens: bfloat16 [262144, 768], P(('grp', 'dev')), may hold values from -6 to 6
- slide_gain: float32 [768], replicated, may hold values from 0.1 to 1.9
- w_sqkv: bfloat16 [3, 768, 768], replicated, may hold values from -6 to 6
- w_so: bfloat16 [768, 768], replicated, may hold values from -1.75 to 1.75
- pattern_of_group: int32 [4], replicated, may hold values from 0 to 3, each once
- new_positions: int32 [48], replicated, may hold values from 0 to 262143, as said below
Outputs:
- tile_embed: bfloat16 [48, 768], P('grp')
- slide_out: bfloat16 [262144, 768], P(('grp', 'dev'))
The draws below stay inside these ranges and needn't reach their ends.
Inputs may be any that keep to these rules, and one draw needn't show every extreme that they name: `pattern_of_group`: each of the four patterns is used by exactly one head group. `new_positions`: distinct positions.
All inputs are finite; a program needn't handle non-finite values.
Results may differ from the reference program's by a relative error of at most 0.025.
Values may be sent and summed in bfloat16 or wider, within the bound.
A program may use at most 256 MiB of HBM per device.

```python
import jax
import jax.numpy as jnp
from jax import lax

TILE_WIDTH = 1536
TILE_HEADS = 24
TILE_HEAD = 64
TILE_HIDDEN = 4096
PATCH_VEC = 588
PATCHES = 256
TILES = 3
SLIDE_WIDTH = 768
SLIDE_HEADS = 16
SLIDE_HEAD = 48
ROWS_DEV = 2048
SEQUENCE = 262144
NEW_TILES = 48
N_GRP = 16
N_DEV = 8


def drawn_heads(seed_key, model_width):
    matrix = jax.random.normal(seed_key, (3, model_width, model_width), jnp.float32) * model_width ** (-0.5)
    return jnp.clip(matrix, -6.0, 6.0)


def draw_w_tqkv(key, part):
    return drawn_heads(jax.random.fold_in(key, 3), TILE_WIDTH).astype(jnp.bfloat16)


def draw_w_sqkv(key, part):
    return drawn_heads(jax.random.fold_in(key, 5), SLIDE_WIDTH).astype(jnp.bfloat16)


def draw_new_positions(key, part):
    return jax.random.permutation(jax.random.fold_in(key, 7), SEQUENCE)[:NEW_TILES].astype(jnp.int32)


def level_of(key, shape, shards, low, high):
    def one(axis_at, blocks):
        heights = jax.random.uniform(jax.random.fold_in(jax.random.fold_in(key, 6), axis_at), (blocks,), jnp.float32, low / len(shards), high / len(shards))
        return jnp.repeat(jnp.exp(heights), shape[axis_at] // blocks).reshape((-1,) + (1,) * (len(shape) - axis_at - 1))

    level = one(*shards[0])
    for cut in shards[1:]:
        level = level * one(*cut)
    return level


def scatter_about(stream_key, shape, scale, limit, split=(), held_as=jnp.bfloat16):
    result = scale * jax.random.normal(stream_key, shape, jnp.float32)
    if split:
        result = result * level_of(stream_key, shape, split, -0.22, 0.18)
    return jnp.clip(result, -limit, limit).astype(held_as)


def setup_inputs(seed: int = 0) -> dict:
    splits = jax.random.split(jax.random.key(seed), 15)
    return {
        "tile_patches": scatter_about(splits[0], (NEW_TILES * PATCHES, PATCH_VEC), 1.0, 6.0, ((0, 128),)),
        "w_patch": scatter_about(splits[1], (PATCH_VEC, TILE_WIDTH), PATCH_VEC ** -0.5, 0.25),
        "w_tqkv": draw_w_tqkv(jax.random.fold_in(splits[14], 71), 0),
        "w_to": scatter_about(splits[3], (TILE_WIDTH, TILE_WIDTH), TILE_WIDTH ** -0.5, 0.15625, ((0, 8),)),
        "w_gu": scatter_about(splits[4], (2, TILE_WIDTH, TILE_HIDDEN), TILE_WIDTH ** -0.5, 0.15625, ((2, 8),)),
        "w_down": scatter_about(splits[5], (TILE_HIDDEN, TILE_WIDTH), TILE_HIDDEN ** -0.5, 0.09375, ((0, 8),)),
        "tile_gain": jnp.clip(1.0 + 0.18 * jax.random.normal(splits[6], (3, TILE_WIDTH), jnp.float32), 0.1, 1.9),
        "w_in": scatter_about(splits[7], (TILE_WIDTH, SLIDE_WIDTH), TILE_WIDTH ** -0.5, 0.15625),
        "slide_tokens": scatter_about(splits[8], (SEQUENCE, SLIDE_WIDTH), 1.0, 6.0, ((0, 128),)),
        "slide_gain": jnp.clip(1.0 + 0.18 * jax.random.normal(splits[9], (SLIDE_WIDTH,), jnp.float32), 0.1, 1.9),
        "w_sqkv": draw_w_sqkv(jax.random.fold_in(splits[14], 71), 0),
        "w_so": scatter_about(splits[11], (SLIDE_WIDTH, SLIDE_WIDTH), (SLIDE_WIDTH // 64) ** -0.5, 1.75),
        "pattern_of_group": jax.random.permutation(splits[12], 4).astype(jnp.int32),
        "new_positions": draw_new_positions(jax.random.fold_in(splits[14], 71), 0),
    }


def layer_norm(inputs, gain):
    inputs = inputs.astype(jnp.float32)
    center = inputs - lax.optimization_barrier(jnp.mean(inputs, axis=-1, keepdims=True))
    spread = lax.optimization_barrier(jnp.mean(center * center, axis=-1, keepdims=True))
    return center * lax.rsqrt(spread + 1e-06) * gain.astype(jnp.float32)

def rounded(inputs):
    return lax.optimization_barrier(inputs.astype(jnp.bfloat16)).astype(jnp.float32)

def block_sum(left, right, blocks):
    row_count = left.shape[0]
    inner = left.shape[1] // blocks
    lower_block_list = left.reshape(row_count, blocks, inner).astype(jnp.float32)
    upper_block_list = right.reshape(blocks, inner, right.shape[1]).astype(jnp.float32)
    running_sums = jnp.einsum('fpa,pam->pfm', lower_block_list, upper_block_list)
    return lax.optimization_barrier(jnp.sum(rounded(running_sums), axis=0))

def attend_tiles(query, keys, values, scale):
    scores = jnp.einsum('bqhd,bkhd->bhqk', query.astype(jnp.float32), keys.astype(jnp.float32)) * scale
    probs = jax.nn.softmax(scores, axis=-1).astype(jnp.bfloat16)
    return jnp.einsum('bhqk,bkhd->bqhd', probs.astype(jnp.float32), values.astype(jnp.float32)).astype(jnp.bfloat16)

def attend_segment(query, keys, values, scale):
    scores = jnp.einsum('qhd,khd->hqk', query.astype(jnp.float32), keys.astype(jnp.float32)) * scale
    probs = jax.nn.softmax(scores, axis=-1).astype(jnp.bfloat16)
    return jnp.einsum('hqk,khd->qhd', probs.astype(jnp.float32), values.astype(jnp.float32)).astype(jnp.bfloat16)

def reference(tile_patches, w_patch, w_tqkv, w_to, w_gu, w_down, tile_gain, w_in, slide_tokens, slide_gain, w_sqkv, w_so, pattern_of_group, new_positions):
    tokens_group = TILES * PATCHES

    def encode_group(patches):
        x_zero = jnp.dot(patches, w_patch, preferred_element_type=jnp.float32).astype(jnp.bfloat16)
        h_one = layer_norm(x_zero, tile_gain[0]).astype(jnp.bfloat16)
        projected = [jnp.dot(h_one, w_tqkv[index], preferred_element_type=jnp.float32).astype(jnp.bfloat16).reshape(TILES, PATCHES, TILE_HEADS, TILE_HEAD) for index in range(3)]
        attended = attend_tiles(projected[0], projected[1], projected[2], TILE_HEAD ** (-0.5)).reshape(tokens_group, TILE_WIDTH)
        x_one = (x_zero.astype(jnp.float32) + block_sum(attended, w_to, N_DEV)).astype(jnp.bfloat16)
        h_two = layer_norm(x_one, tile_gain[1]).astype(jnp.bfloat16)
        gate = jnp.dot(h_two, w_gu[0], preferred_element_type=jnp.float32)
        upward = jnp.dot(h_two, w_gu[1], preferred_element_type=jnp.float32)
        hidden = (jax.nn.silu(gate) * upward).astype(jnp.bfloat16)
        x_two = (x_one.astype(jnp.float32) + block_sum(hidden, w_down, N_DEV)).astype(jnp.bfloat16)
        pooled = lax.optimization_barrier(jnp.mean(x_two.astype(jnp.float32).reshape(TILES, PATCHES, TILE_WIDTH), axis=1))
        normed = layer_norm(pooled, tile_gain[2]).astype(jnp.bfloat16)
        return jnp.dot(normed, w_in, preferred_element_type=jnp.float32).astype(jnp.bfloat16)
    tile_embed = lax.map(encode_group, tile_patches.reshape(N_GRP, tokens_group, PATCH_VEC)).reshape(NEW_TILES, SLIDE_WIDTH)
    seq = slide_tokens.at[new_positions].set(tile_embed)
    h_slide = layer_norm(seq, slide_gain).astype(jnp.bfloat16)
    projected = [jnp.dot(h_slide, w_sqkv[index], preferred_element_type=jnp.float32).astype(jnp.bfloat16) for index in range(3)]
    dilation_rates = (1, N_DEV, N_DEV * N_GRP // 4, N_DEV * N_GRP)
    width_group = SLIDE_WIDTH // 4
    heads_group = SLIDE_HEADS // 4
    attended = jnp.zeros((SEQUENCE, SLIDE_WIDTH), jnp.bfloat16)
    for pattern in range(4):
        ratio = dilation_rates[pattern]
        segments = SEQUENCE // (ratio * ROWS_DEV)
        group = jnp.sum(jnp.where(pattern_of_group == pattern, lax.iota(jnp.int32, 4), 0)).astype(jnp.int32)
        column = (group * width_group).astype(jnp.int32)

        def pick(matrix):
            part = lax.dynamic_slice_in_dim(matrix, column, width_group, 1)
            part = part.reshape(segments, ROWS_DEV, ratio, heads_group, SLIDE_HEAD)
            return jnp.stack([part[:, :, member % ratio, member] for member in range(heads_group)], axis=2)
        picked_entries = [pick(matrix) for matrix in projected]
        outputs = lax.map(lambda triple: attend_segment(triple[0], triple[1], triple[2], SLIDE_HEAD ** (-0.5)), (picked_entries[0], picked_entries[1], picked_entries[2]))
        placed = jnp.zeros((segments, ROWS_DEV, ratio, heads_group, SLIDE_HEAD), jnp.bfloat16)
        for member in range(heads_group):
            placed = placed.at[:, :, member % ratio, member].set(outputs[:, :, member])
        attended = lax.dynamic_update_slice(attended, placed.reshape(SEQUENCE, width_group), (jnp.int32(0), column))
    slide_out = (seq.astype(jnp.float32) + jnp.dot(attended, w_so, preferred_element_type=jnp.float32)).astype(jnp.bfloat16)
    return (tile_embed, slide_out)
```

```python
import functools

import jax
import jax.numpy as jnp
from jax import lax
from jax.experimental import pallas as pl
from jax.experimental.pallas import tpu as pltpu
from jax.sharding import PartitionSpec as P

MESH = pl.DeviceIdType.MESH
BF16 = jnp.bfloat16
F32 = jnp.float32

TW = 1536
TH = 64
TP = 256
HB = 192
FB = 512
SW = 768
GW = 192
SH = 48
ROWS = 2048
DIL = (1, 8, 32, 128)
LOG2E = 1.4426950408889634


def dot(a, b):
    return jnp.dot(a, b, preferred_element_type=F32)


def dot_nt(a, b):
    return lax.dot_general(a, b, (((1,), (1,)), ((), ())), preferred_element_type=F32)


def norm(v, gain):
    center = v - jnp.mean(v, axis=-1, keepdims=True)
    spread = jnp.mean(center * center, axis=-1, keepdims=True)
    return center * lax.rsqrt(spread + 1e-06) * gain


def head_of(shape):
    return (lax.broadcasted_iota(jnp.int32, shape, 1) % GW) // SH


def encoder_kernel(
    patches,
    w_patch,
    w_tqkv,
    w_to,
    w_gu,
    w_down,
    w_in,
    tokens,
    w_slide,
    tgain,
    sgain,
    qkv0_out,
    q1_out,
    q2_out,
    q3_out,
    kv1,
    kv2,
    kv3,
    em,
    new_out,
    patches_s,
    w_patch_s,
    w_tqkv_s,
    wto_s,
    w_gu_s,
    w_down_s,
    w_in_s,
    tok_s,
    w_slide_s,
    hs,
    qkv0_s,
    kvc1,
    kvc2,
    kvc3,
    x0_s,
    att_s,
    pp_s,
    load_sem,
    out_sem,
    own_sem,
    send_sem,
    recv_sem,
    att_send,
    att_recv,
):
    grp = lax.axis_index("grp")
    dev = lax.axis_index("dev")
    core = grp % 2
    plane = grp // 4
    chip = (grp // 2) * 8 + dev
    local16 = (grp // 2) % 2 * 8 + dev
    sibling = (grp // 2) * 2 + (1 - core)

    def peer8(i):
        return (grp, (dev + i) % 8)

    def peer16(i):
        to = (local16 + i) % 16
        return (plane * 4 + (to // 8) * 2 + core, to % 8)

    def peer64(i):
        to = (chip + i) % 64
        return ((to // 8) * 2 + core, to % 8)

    def cross(i):
        return (i * 2 + (1 - core), dev)

    def peer_grp(i):
        return ((grp + i) % 16, dev)

    def load(src, dst, at):
        copy = pltpu.make_async_copy(src, dst, load_sem.at[at])
        copy.start()
        return copy

    ld_tok = load(tokens, tok_s, 0)
    ld_slide = load(w_slide, w_slide_s, 1)
    ld_patch = load(w_patch, w_patch_s, 2)
    ld_tqkv = load(w_tqkv, w_tqkv_s, 3)
    ld_gu = load(w_gu, w_gu_s, 4)
    ld_down = load(w_down, w_down_s, 5)
    ld_in = load(w_in, w_in_s, 6)

    my_patch = pl.ds(pl.multiple_of(dev * 96, 32), 96)
    half_row = pl.multiple_of(core * 96, 32)
    my_half = pl.ds(pl.multiple_of(dev * HB + core * 96, 32), 96)
    my_shard = pl.ds(pl.multiple_of(dev * HB, 64), HB)

    barrier = pltpu.get_barrier_semaphore()

    @pl.loop(1, 64)
    def _(i):
        pl.semaphore_signal(barrier, inc=1, device_id=peer64(i), device_id_type=MESH)

    @pl.loop(0, 8)
    def _(i):
        pl.semaphore_signal(barrier, inc=1, device_id=cross(i), device_id_type=MESH)

    pl.semaphore_wait(barrier, 71)

    own_patch = pltpu.make_async_copy(patches, patches_s.at[my_patch], own_sem.at[0])
    own_patch.start()
    own_wto = pltpu.make_async_copy(w_to, wto_s.at[my_shard], own_sem.at[1])
    own_wto.start()

    def push(src, dst, at, to):
        pltpu.make_async_remote_copy(
            src_ref=src,
            dst_ref=dst,
            send_sem=send_sem.at[at],
            recv_sem=recv_sem.at[at],
            device_id=to,
            device_id_type=MESH,
        ).start()

    def landed(ref, sem):
        pltpu.make_async_copy(ref, ref, sem).wait()

    @pl.loop(1, 8)
    def _(i):
        push(patches, patches_s.at[my_patch], 0, peer8(i))

    @pl.loop(1, 8)
    def _(i):
        push(w_to.at[pl.ds(half_row, 96)], wto_s.at[my_half], 1, peer8(i))

    ld_tok.wait()
    ld_slide.wait()

    @pl.loop(0, 8)
    def _(c):
        at = pl.ds(pl.multiple_of(c * 256, 256), 256)
        h = norm(tok_s[at, :].astype(F32), sgain[...])
        for b in range(6):
            hs[b, at, :] = h[:, b * 128 : (b + 1) * 128]
        y = dot(h.astype(BF16), w_slide_s[0])
        ones = lax.broadcasted_iota(jnp.int32, y.shape, 1) == 2 * 256 + GW
        qkv0_s[at, :] = jnp.where(ones, 1.0, y).astype(BF16)

    out0 = pltpu.make_async_copy(qkv0_s, qkv0_out, out_sem.at[0])
    out0.start()

    own_patch.wait()
    landed(patches_s.at[pl.ds(0, 672)], recv_sem.at[0])
    ld_patch.wait()
    ld_tqkv.wait()

    lanes = lax.broadcasted_iota(jnp.int32, (TP, HB), 1) // TH

    @pl.loop(0, 3)
    def _(t):
        at = pl.ds(pl.multiple_of(t * TP, TP), TP)
        x0 = dot(patches_s[at, :], w_patch_s[...]).astype(BF16)
        x0_s[at, :] = x0
        h1 = norm(x0.astype(F32), tgain[0:1, :]).astype(BF16)
        q = dot(h1, w_tqkv_s[0]).astype(BF16)
        k = dot(h1, w_tqkv_s[1]).astype(BF16)
        vt = dot(h1, w_tqkv_s[2]).T.astype(BF16)
        for h in range(3):
            s = dot_nt(jnp.where(lanes == h, q, jnp.zeros_like(q)), k) * (TH**-0.5)
            e = jnp.exp(s - jnp.max(s, axis=-1, keepdims=True))
            probs = (e / jnp.sum(e, axis=-1, keepdims=True)).astype(BF16)
            o = dot_nt(vt[h * TH : (h + 1) * TH, :], probs)
            rows = pl.ds(pl.multiple_of(dev * HB + h * TH, 64), TH)
            att_s[t, rows, :] = o.astype(BF16)

        @pl.loop(1, 8)
        def _(i):
            pltpu.make_async_remote_copy(
                src_ref=att_s.at[t, my_shard],
                dst_ref=att_s.at[t, my_shard],
                send_sem=att_send.at[t],
                recv_sem=att_recv.at[t],
                device_id=peer8(i),
                device_id_type=MESH,
            ).start()

    for p, kvc, q_out in ((1, kvc1, q1_out), (2, kvc2, q2_out), (3, kvc3, q3_out)):
        r = DIL[p]
        n = ROWS // r
        picked = jnp.concatenate(
            [
                jnp.concatenate([hs[b, pl.ds(j, n, stride=r), :] for b in range(6)], axis=1)
                for j in range(4)
            ],
            axis=0,
        ).astype(BF16)
        y = dot(picked, w_slide_s[p])
        head = head_of((n, SW))
        mine = jnp.zeros((n, SW), F32)
        for j in range(4):
            mine = jnp.where(head == j, y[j * n : (j + 1) * n, :], mine)
        kvc[...] = mine[:, :384].astype(BF16)
        q_out[...] = mine[:, 384:].astype(BF16)

    at1 = pl.ds(pl.multiple_of(dev * 256, 256), 256)
    at2 = pl.ds(pl.multiple_of((core * 16 + local16) * 64, 64), 64)
    at3 = pl.ds(pl.multiple_of((core * 64 + chip) * 16, 16), 16)
    own1 = pltpu.make_async_copy(kvc1, kv1.at[at1], own_sem.at[2])
    own2 = pltpu.make_async_copy(kvc2, kv2.at[at2], own_sem.at[3])
    own3 = pltpu.make_async_copy(kvc3, kv3.at[at3], own_sem.at[4])
    own1.start()
    own2.start()
    own3.start()

    @pl.loop(1, 64)
    def _(i):
        push(kvc3, kv3.at[at3], 2, peer64(i))

    @pl.loop(1, 16)
    def _(i):
        push(kvc2, kv2.at[at2], 3, peer16(i))

    @pl.loop(1, 8)
    def _(i):
        push(kvc1, kv1.at[at1], 4, peer8(i))

    own_wto.wait()
    landed(wto_s.at[pl.ds(0, 672)], recv_sem.at[1])

    @pl.loop(1, 8)
    def _(i):
        half = pl.ds(pl.multiple_of(((dev + i) % 8) * HB + core * 96, 32), 96)
        push(wto_s.at[half], wto_s.at[half], 5, (sibling, dev))

    landed(wto_s.at[pl.ds(0, 672)], recv_sem.at[5])
    ld_gu.wait()

    eight = lax.broadcasted_iota(jnp.int32, (8, 1), 0)

    def feed(t, sums):
        x_sum, h_sum = sums
        at = pl.ds(pl.multiple_of(t * TP, TP), TP)
        landed(att_s.at[t, pl.ds(0, 7 * HB)], att_recv.at[t])
        att = att_s[t].T
        x1 = (x0_s[at, :].astype(F32) + dot(att, wto_s[...])).astype(BF16).astype(F32)
        h2 = norm(x1, tgain[1:2, :]).astype(BF16)
        gate = dot(h2, w_gu_s[0])
        up = dot(h2, w_gu_s[1])
        hidden = (jax.nn.silu(gate) * up).astype(BF16).astype(F32)
        x_sum = x_sum + jnp.where(eight == t, jnp.sum(x1, axis=0, keepdims=True), 0.0)
        h_sum = h_sum + jnp.where(eight == t, jnp.sum(hidden, axis=0, keepdims=True), 0.0)
        return x_sum, h_sum

    x_sum, h_sum = lax.fori_loop(
        0, 3, feed, (jnp.zeros((8, TW), F32), jnp.zeros((8, FB), F32))
    )
    ld_down.wait()
    h_mean = h_sum * (1.0 / TP)
    coarse = h_mean.astype(BF16)
    fine = (h_mean - coarse.astype(F32)).astype(BF16)
    both = jnp.concatenate([coarse.astype(F32), fine.astype(F32)], axis=0).astype(BF16)
    part = dot(both, w_down_s[...])
    pp_s[dev] = part[0:8] + part[8:16]

    @pl.loop(1, 8)
    def _(i):
        push(pp_s.at[dev], pp_s.at[dev], 6, peer8(i))

    ld_in.wait()
    landed(pp_s.at[pl.ds(0, 7)], recv_sem.at[6])
    pooled = x_sum * (1.0 / TP) + jnp.sum(pp_s[...], axis=0)
    normed = norm(pooled, tgain[2:3, :]).astype(BF16)
    em[grp] = dot(normed, w_in_s[...]).astype(BF16).astype(F32)

    @pl.loop(1, 16)
    def _(i):
        push(em.at[grp], em.at[grp], 7, peer_grp(i))

    own3.wait()
    half3 = pl.ds(pl.multiple_of(core * 1024, 1024), 1024)
    landed(kv3.at[pl.ds(0, 63 * 16)], recv_sem.at[2])
    push(kv3.at[half3], kv3.at[half3], 8, (sibling, dev))
    own2.wait()
    landed(kv2.at[pl.ds(0, 15 * 64)], recv_sem.at[3])
    push(kv2.at[half3], kv2.at[half3], 9, (sibling, dev))

    landed(em.at[pl.ds(0, 15)], recv_sem.at[7])
    fresh = norm(em[...].reshape(128, SW), sgain[...]).astype(BF16)
    for p in range(4):
        new_out[:, p * SW : (p + 1) * SW] = dot(fresh, w_slide_s[p])

    own1.wait()
    landed(kv1.at[pl.ds(0, 7 * 256)], recv_sem.at[4])
    landed(kv3.at[half3], recv_sem.at[8])
    landed(kv2.at[half3], recv_sem.at[9])
    out0.wait()

    landed(patches_s.at[pl.ds(0, 672)], send_sem.at[0])
    landed(wto_s.at[pl.ds(0, 672)], send_sem.at[1])
    landed(kv3.at[pl.ds(0, 63 * 16)], send_sem.at[2])
    landed(kv2.at[pl.ds(0, 15 * 64)], send_sem.at[3])
    landed(kv1.at[pl.ds(0, 7 * 256)], send_sem.at[4])
    landed(wto_s.at[pl.ds(0, 672)], send_sem.at[5])
    landed(pp_s.at[pl.ds(0, 7)], send_sem.at[6])
    landed(em.at[pl.ds(0, 15)], send_sem.at[7])
    landed(kv3.at[half3], send_sem.at[8])
    landed(kv2.at[half3], send_sem.at[9])

    @pl.loop(0, 3)
    def _(t):
        landed(att_s.at[t, pl.ds(0, 7 * HB)], att_send.at[t])


def run_encoder(
    patches, w_patch, w_tqkv, w_to, w_gu, w_down, w_in, tokens, w_slide, tgain, sgain
):
    hbm = pl.BlockSpec(memory_space=pl.ANY)
    vmem = pl.BlockSpec(memory_space=pltpu.VMEM)
    shape = jax.ShapeDtypeStruct
    return pl.pallas_call(
        encoder_kernel,
        out_shape=(
            shape((ROWS, SW), BF16),
            shape((256, 384), BF16),
            shape((64, 384), BF16),
            shape((16, 384), BF16),
            shape((2048, 384), BF16),
            shape((2048, 384), BF16),
            shape((2048, 384), BF16),
            shape((16, 8, SW), F32),
            shape((128, 4 * SW), F32),
        ),
        in_specs=[hbm] * 9 + [vmem] * 2,
        out_specs=(hbm, vmem, vmem, vmem, hbm, hbm, hbm, vmem, vmem),
        scratch_shapes=[
            pltpu.VMEM((768, 588), BF16),
            pltpu.VMEM((588, TW), BF16),
            pltpu.VMEM((3, TW, HB), BF16),
            pltpu.VMEM((TW, TW), BF16),
            pltpu.VMEM((2, TW, FB), BF16),
            pltpu.VMEM((FB, TW), BF16),
            pltpu.VMEM((TW, SW), BF16),
            pltpu.VMEM((ROWS, SW), BF16),
            pltpu.VMEM((4, SW, SW), BF16),
            pltpu.VMEM((6, ROWS, 128), F32),
            pltpu.VMEM((ROWS, SW), BF16),
            pltpu.VMEM((256, 384), BF16),
            pltpu.VMEM((64, 384), BF16),
            pltpu.VMEM((16, 384), BF16),
            pltpu.VMEM((768, TW), BF16),
            pltpu.VMEM((3, TW, TP), BF16),
            pltpu.VMEM((8, 8, TW), F32),
            pltpu.SemaphoreType.DMA((7,)),
            pltpu.SemaphoreType.DMA((1,)),
            pltpu.SemaphoreType.DMA((5,)),
            pltpu.SemaphoreType.DMA((10,)),
            pltpu.SemaphoreType.DMA((10,)),
            pltpu.SemaphoreType.DMA((3,)),
            pltpu.SemaphoreType.DMA((3,)),
        ],
        compiler_params=pltpu.CompilerParams(
            collective_id=0, has_side_effects=True, vmem_limit_bytes=60 * 1024 * 1024
        ),
        name="encode",
    )(patches, w_patch, w_tqkv, w_to, w_gu, w_down, w_in, tokens, w_slide, tgain, sgain)


def attend(q, keys, values):
    s = dot_nt(q, keys)
    m = jnp.max(s, axis=-1, keepdims=True)
    e = jnp.exp2((s - m) * (LOG2E * SH**-0.5)).astype(BF16)
    return e, dot(e, values)


def slide_kernel(
    info,
    qkv0,
    q1,
    q2,
    q3,
    kv1,
    kv2,
    kv3,
    tokens,
    new,
    em,
    w_so,
    out,
    qkv0_s,
    q1_s,
    q2_s,
    q3_s,
    kv1_s,
    kv2_s,
    kv3_s,
    tok_s,
    far_s,
    sem,
):
    step = pl.program_id(0)

    @pl.when(step == 0)
    def _():
        place = info[48]
        copies = [
            pltpu.make_async_copy(src, dst, sem.at[at])
            for at, (src, dst) in enumerate(
                (
                    (qkv0, qkv0_s),
                    (q1, q1_s),
                    (q2, q2_s),
                    (q3, q3_s),
                    (kv1, kv1_s),
                    (kv2, kv2_s),
                    (kv3, kv3_s),
                    (tokens, tok_s),
                )
            )
        ]
        for copy in copies:
            copy.start()
        far_s[...] = jnp.zeros_like(far_s)
        for copy in copies:
            copy.wait()

        def put(ref, row, vector, columns=None):
            base = pl.multiple_of((row // 16) * 16, 16)
            width = ref.shape[1]
            block = ref[pl.ds(base, 16), :].astype(F32)
            hit = lax.broadcasted_iota(jnp.int32, (16, width), 0) == row - base
            if columns is not None:
                hit = jnp.logical_and(hit, columns)
            ref[pl.ds(base, 16), :] = jnp.where(hit, vector, block).astype(BF16)

        head16 = head_of((16, 384))

        @pl.loop(0, 48)
        def _(n):
            pos = info[n]
            row = (n // 3) * 8 + n % 3
            local = pos // ROWS == place
            here = pos % ROWS

            @pl.when(local)
            def _():
                vector = new[pl.ds(row, 1), 0:SW]
                ones = lax.broadcasted_iota(jnp.int32, (1, SW), 1) == 2 * 256 + GW
                put(qkv0_s, here, jnp.where(ones, 1.0, vector))
                put(tok_s, here, em[pl.ds(row, 1), :])

            for p, q_s, kv_s in ((1, q1_s, kv1_s), (2, q2_s, kv2_s), (3, q3_s, kv3_s)):
                r = DIL[p]
                count = ROWS // r
                owner = pos // ROWS
                seen = pos % r < 4
                within = owner // r == place // r
                if p == 1:
                    slot = owner % 8
                else:
                    grp = owner // 8
                    at_chip = (grp // 2) * 8 + owner % 8
                    slot = (grp % 2) * 16 + at_chip % 16 if p == 2 else (grp % 2) * 64 + at_chip
                columns = head16 == pos % r

                @pl.when(jnp.logical_and(seen, within))
                def _():
                    put(
                        kv_s,
                        slot * count + here // r,
                        new[pl.ds(row, 1), p * SW : p * SW + 384],
                        columns,
                    )

                    @pl.when(local)
                    def _():
                        put(
                            q_s,
                            here // r,
                            new[pl.ds(row, 1), p * SW + 384 : (p + 1) * SW],
                            columns,
                        )

        for p, q_s, kv_s in ((1, q1_s, kv1_s), (2, q2_s, kv2_s), (3, q3_s, kv3_s)):
            r = DIL[p]
            count = ROWS // r
            q = q_s[...]
            kv = kv_s[...]
            head = head_of((count, 384))
            for j in range(4):
                e, o = attend(jnp.where(head == j, q, jnp.zeros_like(q)), kv, kv)
                total = jnp.sum(e.astype(F32), axis=-1, keepdims=True)
                lane = lax.broadcasted_iota(jnp.int32, (count, 256), 1)
                mine = jnp.logical_and(lane >= j * SH, lane < (j + 1) * SH)
                o = jnp.where(mine, o[:, 0:256] / total, 0.0)
                for b in range(2):
                    far_s[2 * (p - 1) + b, pl.ds(j, count, stride=r), :] = o[
                        :, b * 128 : (b + 1) * 128
                    ]

    at = pl.ds(pl.multiple_of(step * 256, 256), 256)
    q = qkv0_s[at, 0:256]
    k = qkv0_s[:, 256:512]
    v = qkv0_s[:, 512:768]
    lane = lax.broadcasted_iota(jnp.int32, (256, 256), 1)
    near = jnp.zeros((256, 256), F32)
    for j in range(4):
        mine = jnp.logical_and(lane >= j * SH, lane < (j + 1) * SH)
        _, o = attend(jnp.where(mine, q, jnp.zeros_like(q)), k, v)
        near = jnp.where(mine, o / o[:, GW : GW + 1], near)
    total = tok_s[at, :].astype(F32) + dot(near.astype(BF16), w_so[0:256, :])
    for p in range(3):
        far = jnp.concatenate([far_s[2 * p, at, :], far_s[2 * p + 1, at, :]], axis=1)
        total = total + dot(far.astype(BF16), w_so[(p + 1) * 256 : (p + 2) * 256, :])
    out[...] = total.astype(BF16)


def run_slide(info, qkv0, q1, q2, q3, kv1, kv2, kv3, tokens, new, em, w_so):
    hbm = pl.BlockSpec(memory_space=pl.ANY)

    def whole(a):
        return pl.BlockSpec(a.shape, lambda i, info: (0,) * a.ndim)

    return pl.pallas_call(
        slide_kernel,
        out_shape=jax.ShapeDtypeStruct((ROWS, SW), BF16),
        grid_spec=pltpu.PrefetchScalarGridSpec(
            num_scalar_prefetch=1,
            grid=(8,),
            in_specs=[hbm] * 8 + [whole(new), whole(em), whole(w_so)],
            out_specs=pl.BlockSpec((256, SW), lambda i, info: (i, 0)),
            scratch_shapes=[
                pltpu.VMEM((ROWS, SW), BF16),
                pltpu.VMEM((256, 384), BF16),
                pltpu.VMEM((64, 384), BF16),
                pltpu.VMEM((16, 384), BF16),
                pltpu.VMEM((2048, 384), BF16),
                pltpu.VMEM((2048, 384), BF16),
                pltpu.VMEM((2048, 384), BF16),
                pltpu.VMEM((ROWS, SW), BF16),
                pltpu.VMEM((6, ROWS, 128), F32),
                pltpu.SemaphoreType.DMA((8,)),
            ],
        ),
        compiler_params=pltpu.CompilerParams(vmem_limit_bytes=56 * 1024 * 1024),
        name="slide",
    )(info, qkv0, q1, q2, q3, kv1, kv2, kv3, tokens, new, em, w_so)


def shards(
    tile_patches,
    w_patch,
    w_tqkv,
    w_to,
    w_gu,
    w_down,
    tile_gain,
    w_in,
    slide_tokens,
    slide_gain,
    w_sqkv,
    w_so,
    pattern_of_group,
    new_positions,
):
    grp = lax.axis_index("grp")
    place = grp * 8 + lax.axis_index("dev")
    uses = [pattern_of_group == p for p in range(4)]

    def columns(index, p):
        part = w_sqkv[index, :, 3 * GW :]
        for g in range(3):
            part = jnp.where(uses[p][g], w_sqkv[index, :, g * GW : (g + 1) * GW], part)
        return part

    def rows(p):
        part = w_so[3 * GW :]
        for g in range(3):
            part = jnp.where(uses[p][g], w_so[g * GW : (g + 1) * GW], part)
        return part

    gap = jnp.zeros((SW, 64), BF16)
    wide = jnp.zeros((SW, GW), BF16)
    w_slide = [
        jnp.concatenate(
            [columns(0, 0), gap, columns(1, 0), gap, columns(2, 0), gap], axis=1
        )
    ] + [
        jnp.concatenate([columns(2, p), columns(1, p), wide, columns(0, p)], axis=1)
        for p in (1, 2, 3)
    ]
    w_slide = jnp.stack(w_slide)
    (
        qkv0,
        q1,
        q2,
        q3,
        kv1,
        kv2,
        kv3,
        em,
        new,
    ) = run_encoder(
        tile_patches,
        w_patch,
        w_tqkv,
        w_to,
        w_gu,
        w_down,
        w_in,
        slide_tokens,
        w_slide,
        tile_gain,
        slide_gain.reshape(1, SW),
    )
    pad = jnp.zeros((64, SW), BF16)
    w_out = jnp.concatenate(
        [piece for p in range(4) for piece in (rows(p), pad)], axis=0
    )
    info = jnp.concatenate([new_positions, place.astype(jnp.int32).reshape(1)])
    slide_out = run_slide(
        info, qkv0, q1, q2, q3, kv1, kv2, kv3, slide_tokens, new, em.reshape(128, SW), w_out
    )
    tile_embed = lax.dynamic_slice_in_dim(em, grp, 1, 0)[0, 0:3].astype(BF16)
    return (tile_embed, slide_out)


def solution(mesh):
    placed = (
        P(("grp", "dev"), None),
        P(),
        P(None, None, "dev"),
        P("dev", None),
        P(None, None, "dev"),
        P("dev", None),
        P(),
        P(),
        P(("grp", "dev"), None),
        P(),
        P(),
        P(),
        P(),
        P(),
    )
    return jax.shard_map(
        shards,
        mesh=mesh,
        in_specs=placed,
        out_specs=(P("grp", None), P(("grp", "dev"), None)),
        check_vma=False,
    )
```

```python
import functools

import jax
import jax.numpy as jnp
from jax import lax
from jax.experimental import pallas as pl
from jax.experimental.pallas import tpu as pltpu
from jax.sharding import PartitionSpec as P

MESH = pl.DeviceIdType.MESH
BF16 = jnp.bfloat16
F32 = jnp.float32

TW = 1536
TH = 64
TP = 256
HB = 192
FB = 512
SW = 768
GW = 192
SH = 48
ROWS = 2048
DIL = (1, 8, 32, 128)
LOG2E = 1.4426950408889634
HIDE = -1e30
SCALE = LOG2E * SH**-0.5


def dot(a, b):
    return jnp.dot(a, b, preferred_element_type=F32)


def dot_nt(a, b):
    return lax.dot_general(a, b, (((1,), (1,)), ((), ())), preferred_element_type=F32)


def norm(v, gain):
    center = v - jnp.mean(v, axis=-1, keepdims=True)
    spread = jnp.mean(center * center, axis=-1, keepdims=True)
    return center * lax.rsqrt(spread + 1e-06) * gain


def head_of(shape):
    return (lax.broadcasted_iota(jnp.int32, shape, 1) % GW) // SH


def attend(q, keys, values):
    s = dot_nt(q, keys)
    m = jnp.max(s, axis=-1, keepdims=True)
    e = jnp.exp2((s - m) * SCALE).astype(BF16)
    return m, e, dot(e, values)


def encoder_kernel(
    patches,
    w_patch,
    w_tqkv,
    w_to,
    w_gu,
    w_down,
    w_in,
    tokens,
    w_sqkv,
    tgain,
    sgain,
    places,
    pattern,
    qkv0_out,
    near,
    stats,
    q1_out,
    q2_out,
    q3_out,
    kv1,
    kv2,
    kv3,
    em,
    new_out,
    patches_s,
    w_patch_s,
    w_tqkv_s,
    wto_s,
    w_gu_s,
    w_down_s,
    w_in_s,
    tok_s,
    w_raw,
    w_slide_s,
    hs,
    qkv0_s,
    kvc1,
    kvc2,
    kvc3,
    x0_s,
    att_s,
    pp_s,
    load_sem,
    out_sem,
    own_sem,
    send_sem,
    recv_sem,
    att_send,
    att_recv,
):
    grp = lax.axis_index("grp")
    dev = lax.axis_index("dev")
    core = grp % 2
    plane = grp // 4
    chip = (grp // 2) * 8 + dev
    local16 = (grp // 2) % 2 * 8 + dev
    sibling = (grp // 2) * 2 + (1 - core)

    def peer8(i):
        return (grp, (dev + i) % 8)

    def peer16(i):
        to = (local16 + i) % 16
        return (plane * 4 + (to // 8) * 2 + core, to % 8)

    def peer64(i):
        to = (chip + i) % 64
        return ((to // 8) * 2 + core, to % 8)

    def cross(i):
        return (i * 2 + (1 - core), dev)

    def peer_grp(i):
        return ((grp + i) % 16, dev)

    def load(src, dst, at):
        copy = pltpu.make_async_copy(src, dst, load_sem.at[at])
        copy.start()
        return copy

    ld_tok = load(tokens, tok_s, 0)
    ld_raw = load(w_sqkv, w_raw, 1)
    ld_patch = load(w_patch, w_patch_s, 2)
    ld_tqkv = load(w_tqkv, w_tqkv_s, 3)
    ld_gu = load(w_gu, w_gu_s, 4)
    ld_down = load(w_down, w_down_s, 5)
    ld_in = load(w_in, w_in_s, 6)

    my_patch = pl.ds(pl.multiple_of(dev * 96, 32), 96)
    half_row = pl.multiple_of(core * 96, 32)
    my_half = pl.ds(pl.multiple_of(dev * HB + core * 96, 32), 96)
    my_shard = pl.ds(pl.multiple_of(dev * HB, 64), HB)

    barrier = pltpu.get_barrier_semaphore()

    @pl.loop(1, 64)
    def _(i):
        pl.semaphore_signal(barrier, inc=1, device_id=peer64(i), device_id_type=MESH)

    @pl.loop(0, 8)
    def _(i):
        pl.semaphore_signal(barrier, inc=1, device_id=cross(i), device_id_type=MESH)

    pl.semaphore_wait(barrier, 71)

    own_patch = pltpu.make_async_copy(patches, patches_s.at[my_patch], own_sem.at[0])
    own_patch.start()
    own_wto = pltpu.make_async_copy(w_to, wto_s.at[my_shard], own_sem.at[1])
    own_wto.start()

    def push(src, dst, at, to):
        pltpu.make_async_remote_copy(
            src_ref=src,
            dst_ref=dst,
            send_sem=send_sem.at[at],
            recv_sem=recv_sem.at[at],
            device_id=to,
            device_id_type=MESH,
        ).start()

    def landed(ref, sem):
        pltpu.make_async_copy(ref, ref, sem).wait()

    @pl.loop(1, 8)
    def _(i):
        push(patches, patches_s.at[my_patch], 0, peer8(i))

    @pl.loop(1, 8)
    def _(i):
        push(w_to.at[pl.ds(half_row, 96)], wto_s.at[my_half], 1, peer8(i))

    ld_raw.wait()
    group = [
        sum(jnp.where(pattern[g] == p, g, 0) for g in range(4)) for p in range(4)
    ]

    @pl.loop(0, 3)
    def _(c):
        at = pl.ds(pl.multiple_of(c * 256, 256), 256)

        def part(index, p):
            pair = jnp.where(group[p] >= 2, w_raw[index, at, 384:], w_raw[index, at, :384])
            return jnp.where(group[p] % 2 == 1, pair[:, GW:], pair[:, :GW])

        for index in range(3):
            w_slide_s[0, at, index * 256 : (index + 1) * 256] = jnp.concatenate(
                [part(index, 0), jnp.zeros((256, 64), BF16)], axis=1
            )
        for p in range(1, 4):
            w_slide_s[p, at, :384] = jnp.concatenate([part(2, p), part(1, p)], axis=1)
            w_slide_s[p, at, 384:] = jnp.concatenate(
                [jnp.zeros((256, GW), BF16), part(0, p)], axis=1
            )

    ld_tok.wait()
    first = (grp * 8 + dev) * ROWS

    @pl.loop(0, 8)
    def _(c):
        at = pl.ds(pl.multiple_of(c * 256, 256), 256)
        h = norm(tok_s[at, :].astype(F32), sgain[...])
        for b in range(6):
            hs[b, at, :] = h[:, b * 128 : (b + 1) * 128]
        y = dot(h.astype(BF16), w_slide_s[0])
        row = lax.broadcasted_iota(jnp.int32, (256, 128), 0) + (first + c * 256)
        stale = jnp.max(jnp.where(row == places[...], 1.0, 0.0), axis=1, keepdims=True)
        column = lax.broadcasted_iota(jnp.int32, y.shape, 1)
        ones = jnp.logical_or(column == GW, column == 2 * 256 + GW)
        y = jnp.where(ones, 1.0, jnp.where(column == 256 + GW, stale * HIDE, y))
        qkv0_s[at, :] = y.astype(BF16)

    out0 = pltpu.make_async_copy(qkv0_s, qkv0_out, out_sem.at[0])
    out0.start()

    own_patch.wait()
    landed(patches_s.at[pl.ds(0, 672)], recv_sem.at[0])
    ld_patch.wait()
    ld_tqkv.wait()

    lanes = lax.broadcasted_iota(jnp.int32, (TP, HB), 1) // TH

    @pl.loop(0, 3)
    def _(t):
        at = pl.ds(pl.multiple_of(t * TP, TP), TP)
        x0 = dot(patches_s[at, :], w_patch_s[...]).astype(BF16)
        x0_s[at, :] = x0
        h1 = norm(x0.astype(F32), tgain[0:1, :]).astype(BF16)
        q = dot_nt(h1, w_tqkv_s[0]).astype(BF16)
        k = dot_nt(h1, w_tqkv_s[1]).astype(BF16)
        vt = dot_nt(w_tqkv_s[2], h1).astype(BF16)
        for h in range(3):
            s = dot_nt(jnp.where(lanes == h, q, jnp.zeros_like(q)), k) * (TH**-0.5)
            e = jnp.exp(s - jnp.max(s, axis=-1, keepdims=True))
            probs = (e / jnp.sum(e, axis=-1, keepdims=True)).astype(BF16)
            o = dot_nt(vt[h * TH : (h + 1) * TH, :], probs)
            rows = pl.ds(pl.multiple_of(dev * HB + h * TH, 64), TH)
            att_s[t, rows, :] = o.astype(BF16)

        @pl.loop(1, 8)
        def _(i):
            pltpu.make_async_remote_copy(
                src_ref=att_s.at[t, my_shard],
                dst_ref=att_s.at[t, my_shard],
                send_sem=att_send.at[t],
                recv_sem=att_recv.at[t],
                device_id=peer8(i),
                device_id_type=MESH,
            ).start()

    for p, kvc, q_out in ((1, kvc1, q1_out), (2, kvc2, q2_out), (3, kvc3, q3_out)):
        r = DIL[p]
        n = ROWS // r
        picked = jnp.concatenate(
            [
                jnp.concatenate([hs[b, pl.ds(j, n, stride=r), :] for b in range(6)], axis=1)
                for j in range(4)
            ],
            axis=0,
        ).astype(BF16)
        y = dot(picked, w_slide_s[p])
        head = head_of((n, SW))
        mine = jnp.zeros((n, SW), F32)
        for j in range(4):
            mine = jnp.where(head == j, y[j * n : (j + 1) * n, :], mine)
        kvc[...] = mine[:, :384].astype(BF16)
        q_out[...] = mine[:, 384:].astype(BF16)

    at1 = pl.ds(pl.multiple_of(dev * 256, 256), 256)
    at2 = pl.ds(pl.multiple_of((core * 16 + local16) * 64, 64), 64)
    at3 = pl.ds(pl.multiple_of((core * 64 + chip) * 16, 16), 16)
    own1 = pltpu.make_async_copy(kvc1, kv1.at[at1], own_sem.at[2])
    own2 = pltpu.make_async_copy(kvc2, kv2.at[at2], own_sem.at[3])
    own3 = pltpu.make_async_copy(kvc3, kv3.at[at3], own_sem.at[4])
    own1.start()
    own2.start()
    own3.start()

    @pl.loop(1, 64)
    def _(i):
        push(kvc3, kv3.at[at3], 2, peer64(i))

    @pl.loop(1, 16)
    def _(i):
        push(kvc2, kv2.at[at2], 3, peer16(i))

    @pl.loop(1, 8)
    def _(i):
        push(kvc1, kv1.at[at1], 4, peer8(i))

    def near_rows(first_block, last_block):
        @pl.loop(first_block, last_block)
        def _(b):
            at = pl.ds(pl.multiple_of(b * 256, 256), 256)
            q = qkv0_s[at, 0:256]
            lane = lax.broadcasted_iota(jnp.int32, (256, 256), 1)
            spot = lax.broadcasted_iota(jnp.int32, (256, 128), 1)
            found = jnp.zeros((256, 256), F32)
            kept = jnp.zeros((256, 128), F32)
            for j in range(4):
                mine = jnp.logical_and(lane >= j * SH, lane < (j + 1) * SH)
                used = jnp.logical_or(mine, lane == GW)
                m, _, o = attend(
                    jnp.where(used, q, jnp.zeros_like(q)),
                    qkv0_s[:, 256:512],
                    qkv0_s[:, 512:768],
                )
                count = o[:, GW : GW + 1]
                found = jnp.where(mine, o / count, found)
                kept = jnp.where(spot == j, m, jnp.where(spot == 4 + j, count, kept))
            near[at, :] = found.astype(BF16)
            stats[at, :] = kept

    near_rows(0, 2)

    own_wto.wait()
    landed(wto_s.at[pl.ds(0, 672)], recv_sem.at[1])

    @pl.loop(1, 8)
    def _(i):
        half = pl.ds(pl.multiple_of(((dev + i) % 8) * HB + core * 96, 32), 96)
        push(wto_s.at[half], wto_s.at[half], 5, (sibling, dev))

    near_rows(2, 4)
    landed(wto_s.at[pl.ds(0, 672)], recv_sem.at[5])
    ld_gu.wait()

    eight = lax.broadcasted_iota(jnp.int32, (8, 1), 0)

    def feed(t, sums):
        x_sum, h_sum = sums
        at = pl.ds(pl.multiple_of(t * TP, TP), TP)
        landed(att_s.at[t, pl.ds(0, 7 * HB)], att_recv.at[t])
        att = att_s[t].T
        x1 = (x0_s[at, :].astype(F32) + dot(att, wto_s[...])).astype(BF16).astype(F32)
        h2 = norm(x1, tgain[1:2, :]).astype(BF16)
        gate = dot(h2, w_gu_s[0])
        up = dot(h2, w_gu_s[1])
        hidden = (jax.nn.silu(gate) * up).astype(BF16).astype(F32)
        x_sum = x_sum + jnp.where(eight == t, jnp.sum(x1, axis=0, keepdims=True), 0.0)
        h_sum = h_sum + jnp.where(eight == t, jnp.sum(hidden, axis=0, keepdims=True), 0.0)
        return x_sum, h_sum

    x_sum, h_sum = lax.fori_loop(
        0, 3, feed, (jnp.zeros((8, TW), F32), jnp.zeros((8, FB), F32))
    )
    ld_down.wait()
    h_mean = h_sum * (1.0 / TP)
    coarse = h_mean.astype(BF16)
    fine = (h_mean - coarse.astype(F32)).astype(BF16)
    both = jnp.concatenate([coarse.astype(F32), fine.astype(F32)], axis=0).astype(BF16)
    part = dot(both, w_down_s[...])
    pp_s[dev] = part[0:8] + part[8:16]

    @pl.loop(1, 8)
    def _(i):
        push(pp_s.at[dev], pp_s.at[dev], 6, peer8(i))

    near_rows(4, 5)
    ld_in.wait()
    landed(pp_s.at[pl.ds(0, 7)], recv_sem.at[6])
    pooled = x_sum * (1.0 / TP) + jnp.sum(pp_s[...], axis=0)
    normed = norm(pooled, tgain[2:3, :]).astype(BF16)
    em[grp] = dot(normed, w_in_s[...]).astype(BF16).astype(F32)

    @pl.loop(1, 16)
    def _(i):
        push(em.at[grp], em.at[grp], 7, peer_grp(i))

    near_rows(5, 6)

    own3.wait()
    half3 = pl.ds(pl.multiple_of(core * 1024, 1024), 1024)
    landed(kv3.at[pl.ds(0, 63 * 16)], recv_sem.at[2])
    push(kv3.at[half3], kv3.at[half3], 8, (sibling, dev))
    own2.wait()
    landed(kv2.at[pl.ds(0, 15 * 64)], recv_sem.at[3])
    push(kv2.at[half3], kv2.at[half3], 9, (sibling, dev))

    near_rows(6, 8)
    landed(em.at[pl.ds(0, 15)], recv_sem.at[7])
    fresh = norm(em[...].reshape(128, SW), sgain[...]).astype(BF16)
    for p in range(4):
        new_out[:, p * SW : (p + 1) * SW] = dot(fresh, w_slide_s[p])

    own1.wait()
    landed(kv1.at[pl.ds(0, 7 * 256)], recv_sem.at[4])
    landed(kv3.at[half3], recv_sem.at[8])
    landed(kv2.at[half3], recv_sem.at[9])
    out0.wait()

    landed(patches_s.at[pl.ds(0, 672)], send_sem.at[0])
    landed(wto_s.at[pl.ds(0, 672)], send_sem.at[1])
    landed(kv3.at[pl.ds(0, 63 * 16)], send_sem.at[2])
    landed(kv2.at[pl.ds(0, 15 * 64)], send_sem.at[3])
    landed(kv1.at[pl.ds(0, 7 * 256)], send_sem.at[4])
    landed(wto_s.at[pl.ds(0, 672)], send_sem.at[5])
    landed(pp_s.at[pl.ds(0, 7)], send_sem.at[6])
    landed(em.at[pl.ds(0, 15)], send_sem.at[7])
    landed(kv3.at[half3], send_sem.at[8])
    landed(kv2.at[half3], send_sem.at[9])

    @pl.loop(0, 3)
    def _(t):
        landed(att_s.at[t, pl.ds(0, 7 * HB)], att_send.at[t])


def run_encoder(*args):
    hbm = pl.BlockSpec(memory_space=pl.ANY)
    vmem = pl.BlockSpec(memory_space=pltpu.VMEM)
    shape = jax.ShapeDtypeStruct
    return pl.pallas_call(
        encoder_kernel,
        out_shape=(
            shape((ROWS, SW), BF16),
            shape((ROWS, 256), BF16),
            shape((ROWS, 128), F32),
            shape((256, 384), BF16),
            shape((64, 384), BF16),
            shape((16, 384), BF16),
            shape((2048, 384), BF16),
            shape((2048, 384), BF16),
            shape((2048, 384), BF16),
            shape((16, 8, SW), F32),
            shape((128, 4 * SW), F32),
        ),
        in_specs=[hbm] * 9 + [vmem] * 3 + [pl.BlockSpec(memory_space=pltpu.SMEM)],
        out_specs=(hbm, vmem, vmem, vmem, vmem, vmem, hbm, hbm, hbm, vmem, vmem),
        scratch_shapes=[
            pltpu.VMEM((768, 588), BF16),
            pltpu.VMEM((588, TW), BF16),
            pltpu.VMEM((3, HB, TW), BF16),
            pltpu.VMEM((TW, TW), BF16),
            pltpu.VMEM((2, TW, FB), BF16),
            pltpu.VMEM((FB, TW), BF16),
            pltpu.VMEM((TW, SW), BF16),
            pltpu.VMEM((ROWS, SW), BF16),
            pltpu.VMEM((3, SW, SW), BF16),
            pltpu.VMEM((4, SW, SW), BF16),
            pltpu.VMEM((6, ROWS, 128), F32),
            pltpu.VMEM((ROWS, SW), BF16),
            pltpu.VMEM((256, 384), BF16),
            pltpu.VMEM((64, 384), BF16),
            pltpu.VMEM((16, 384), BF16),
            pltpu.VMEM((768, TW), BF16),
            pltpu.VMEM((3, TW, TP), BF16),
            pltpu.VMEM((8, 8, TW), F32),
            pltpu.SemaphoreType.DMA((7,)),
            pltpu.SemaphoreType.DMA((1,)),
            pltpu.SemaphoreType.DMA((5,)),
            pltpu.SemaphoreType.DMA((10,)),
            pltpu.SemaphoreType.DMA((10,)),
            pltpu.SemaphoreType.DMA((3,)),
            pltpu.SemaphoreType.DMA((3,)),
        ],
        compiler_params=pltpu.CompilerParams(
            collective_id=0, has_side_effects=True, vmem_limit_bytes=60 * 1024 * 1024
        ),
        name="encode",
    )(*args)


def slide_kernel(
    info,
    qkv0,
    near,
    stats,
    q1,
    q2,
    q3,
    kv1,
    kv2,
    kv3,
    tokens,
    new,
    em,
    places,
    w_so,
    out,
    embed_out,
    qkv0_s,
    near_s,
    stats_s,
    q1_s,
    q2_s,
    q3_s,
    kv1_s,
    kv2_s,
    kv3_s,
    tok_s,
    far_s,
    fresh_s,
    sem,
):
    step = pl.program_id(0)

    @pl.when(step == 0)
    def _():
        place = info[48]
        copies = [
            pltpu.make_async_copy(src, dst, sem.at[at])
            for at, (src, dst) in enumerate(
                (
                    (q1, q1_s),
                    (q2, q2_s),
                    (q3, q3_s),
                    (kv1, kv1_s),
                    (kv2, kv2_s),
                    (kv3, kv3_s),
                    (tokens, tok_s),
                    (near, near_s),
                    (qkv0, qkv0_s),
                    (stats, stats_s),
                )
            )
        ]
        for copy in copies:
            copy.start()
        embed_out[...] = em[pl.ds(pl.multiple_of((place // 8) * 8, 8), 8), :][0:3].astype(BF16)
        far_s[...] = jnp.zeros_like(far_s)
        for copy in copies:
            copy.wait()

        def put(ref, row, vector, columns=None):
            base = pl.multiple_of((row // 16) * 16, 16)
            width = ref.shape[1]
            block = ref[pl.ds(base, 16), :].astype(F32)
            hit = lax.broadcasted_iota(jnp.int32, (16, width), 0) == row - base
            if columns is not None:
                hit = jnp.logical_and(hit, columns)
            ref[pl.ds(base, 16), :] = jnp.where(hit, vector, block).astype(BF16)

        head16 = head_of((16, 384))

        def insert(n, found):
            pos = info[n]
            row = (n // 3) * 8 + n % 3
            local = pos // ROWS == place
            here = pos % ROWS

            @pl.when(local)
            def _():
                put(tok_s, here, em[pl.ds(row, 1), :])

            for p, q_s, kv_s in ((1, q1_s, kv1_s), (2, q2_s, kv2_s), (3, q3_s, kv3_s)):
                r = DIL[p]
                count = ROWS // r
                owner = pos // ROWS
                seen = pos % r < 4
                within = owner // r == place // r
                if p == 1:
                    slot = owner % 8
                else:
                    grp = owner // 8
                    at_chip = (grp // 2) * 8 + owner % 8
                    slot = (grp % 2) * 16 + at_chip % 16 if p == 2 else (grp % 2) * 64 + at_chip
                columns = head16 == pos % r

                @pl.when(jnp.logical_and(seen, within))
                def _():
                    put(
                        kv_s,
                        slot * count + here // r,
                        new[pl.ds(row, 1), p * SW : p * SW + 384],
                        columns,
                    )

                    @pl.when(local)
                    def _():
                        put(
                            q_s,
                            here // r,
                            new[pl.ds(row, 1), p * SW + 384 : (p + 1) * SW],
                            columns,
                        )

            return found + jnp.where(local, 1, 0)

        found = lax.fori_loop(0, 48, insert, jnp.int32(0))

        @pl.when(found > 0)
        def _():
            hide = jnp.where(places[...] // ROWS == place, 0.0, HIDE)
            lane = lax.broadcasted_iota(jnp.int32, (128, 256), 1)
            fresh_q = jnp.where(lane == GW, 1.0, new[:, 0:256]).astype(BF16)
            fresh_k = new[:, 256:512].astype(BF16)
            fresh_v = jnp.where(lane == GW, 1.0, new[:, 512:768]).astype(BF16)

            @pl.loop(0, 8)
            def _(b):
                at = pl.ds(pl.multiple_of(b * 256, 256), 256)
                lane = lax.broadcasted_iota(jnp.int32, (256, 256), 1)
                q = qkv0_s[at, 0:256]
                held = near_s[at, :].astype(F32)
                for j in range(4):
                    mine = jnp.logical_and(lane >= j * SH, lane < (j + 1) * SH)
                    s = dot_nt(jnp.where(mine, q, jnp.zeros_like(q)), fresh_k) + hide
                    m_old = stats_s[at, j : j + 1]
                    m = jnp.maximum(m_old, jnp.max(s, axis=-1, keepdims=True))
                    weight = stats_s[at, 4 + j : 5 + j] * jnp.exp2((m_old - m) * SCALE)
                    e = jnp.exp2((s - m) * SCALE).astype(BF16)
                    o = dot(e, fresh_v)
                    joined = (held * weight + o) / (weight + o[:, GW : GW + 1])
                    held = jnp.where(mine, joined, held)
                near_s[at, :] = held.astype(BF16)

            for j in range(4):
                mine = jnp.logical_and(lane >= j * SH, lane < (j + 1) * SH)
                used = jnp.logical_or(mine, lane == GW)
                q = jnp.where(used, fresh_q, jnp.zeros_like(fresh_q))
                s_old = dot_nt(q, qkv0_s[:, 256:512])
                s_new = dot_nt(q, fresh_k) + hide
                m = jnp.maximum(
                    jnp.max(s_old, axis=-1, keepdims=True), jnp.max(s_new, axis=-1, keepdims=True)
                )
                e_old = jnp.exp2((s_old - m) * SCALE).astype(BF16)
                e_new = jnp.exp2((s_new - m) * SCALE).astype(BF16)
                o = dot(e_old, qkv0_s[:, 512:768]) + dot(e_new, fresh_v)
                o = o / o[:, GW : GW + 1]
                fresh_s[...] = o if j == 0 else jnp.where(mine, o, fresh_s[...])

            @pl.loop(0, 48)
            def _(n):
                pos = info[n]

                @pl.when(pos // ROWS == place)
                def _():
                    put(near_s, pos % ROWS, fresh_s[pl.ds((n // 3) * 8 + n % 3, 1), :])

        for p, q_s, kv_s in ((1, q1_s, kv1_s), (2, q2_s, kv2_s), (3, q3_s, kv3_s)):
            r = DIL[p]
            count = ROWS // r
            q = q_s[...]
            kv = kv_s[...]
            head = head_of((count, 384))
            for j in range(4):
                _, e, o = attend(jnp.where(head == j, q, jnp.zeros_like(q)), kv, kv)
                total = jnp.sum(e.astype(F32), axis=-1, keepdims=True)
                lane = lax.broadcasted_iota(jnp.int32, (count, 256), 1)
                mine = jnp.logical_and(lane >= j * SH, lane < (j + 1) * SH)
                o = jnp.where(mine, o[:, 0:256] / total, 0.0)
                for b in range(2):
                    far_s[2 * (p - 1) + b, pl.ds(j, count, stride=r), :] = o[
                        :, b * 128 : (b + 1) * 128
                    ]

    at = pl.ds(pl.multiple_of(step * 256, 256), 256)

    def weights(p):
        return w_so[pl.ds(pl.multiple_of(info[49 + p] * GW, 64), GW), :]

    total = tok_s[at, :].astype(F32) + dot(near_s[at, 0:GW], weights(0))
    for p in range(3):
        far = jnp.concatenate([far_s[2 * p, at, :], far_s[2 * p + 1, at, :]], axis=1)
        total = total + dot(far[:, 0:GW].astype(BF16), weights(p + 1))
    out[...] = total.astype(BF16)


def run_slide(info, *args):
    hbm = pl.BlockSpec(memory_space=pl.ANY)
    vmem = pl.BlockSpec(memory_space=pltpu.VMEM)
    return pl.pallas_call(
        slide_kernel,
        out_shape=(
            jax.ShapeDtypeStruct((ROWS, SW), BF16),
            jax.ShapeDtypeStruct((3, SW), BF16),
        ),
        grid_spec=pltpu.PrefetchScalarGridSpec(
            num_scalar_prefetch=1,
            grid=(8,),
            in_specs=[hbm] * 10 + [vmem] * 4,
            out_specs=(
                pl.BlockSpec((256, SW), lambda i, info: (i, 0)),
                pl.BlockSpec((3, SW), lambda i, info: (0, 0)),
            ),
            scratch_shapes=[
                pltpu.VMEM((ROWS, SW), BF16),
                pltpu.VMEM((ROWS, 256), BF16),
                pltpu.VMEM((ROWS, 128), F32),
                pltpu.VMEM((256, 384), BF16),
                pltpu.VMEM((64, 384), BF16),
                pltpu.VMEM((16, 384), BF16),
                pltpu.VMEM((2048, 384), BF16),
                pltpu.VMEM((2048, 384), BF16),
                pltpu.VMEM((2048, 384), BF16),
                pltpu.VMEM((ROWS, SW), BF16),
                pltpu.VMEM((6, ROWS, 128), F32),
                pltpu.VMEM((128, 256), F32),
                pltpu.SemaphoreType.DMA((10,)),
            ],
        ),
        compiler_params=pltpu.CompilerParams(vmem_limit_bytes=56 * 1024 * 1024),
        name="slide",
    )(info, *args)


def shards(
    tile_patches,
    w_patch,
    w_tqkv,
    w_to,
    w_gu,
    w_down,
    tile_gain,
    w_in,
    slide_tokens,
    slide_gain,
    w_sqkv,
    w_so,
    pattern_of_group,
    new_positions,
):
    grp = lax.axis_index("grp")
    place = grp * 8 + lax.axis_index("dev")
    places = jnp.pad(new_positions.reshape(16, 3), ((0, 0), (0, 5)), constant_values=-1)
    places = places.reshape(1, 128)
    qkv0, near, stats, q1, q2, q3, kv1, kv2, kv3, em, new = run_encoder(
        tile_patches,
        w_patch,
        jnp.transpose(w_tqkv, (0, 2, 1)),
        w_to,
        w_gu,
        w_down,
        w_in,
        slide_tokens,
        w_sqkv,
        tile_gain,
        slide_gain.reshape(1, SW),
        places,
        pattern_of_group,
    )
    group = [
        jnp.sum(jnp.where(pattern_of_group == p, lax.iota(jnp.int32, 4), 0)) for p in range(4)
    ]
    info = jnp.concatenate(
        [new_positions, jnp.stack([place.astype(jnp.int32)] + group).astype(jnp.int32)]
    )
    slide_out, tile_embed = run_slide(
        info,
        qkv0,
        near,
        stats,
        q1,
        q2,
        q3,
        kv1,
        kv2,
        kv3,
        slide_tokens,
        new,
        em.reshape(128, SW),
        places,
        w_so,
    )
    return (tile_embed, slide_out)


def solution(mesh):
    placed = (
        P(("grp", "dev"), None),
        P(),
        P(None, None, "dev"),
        P("dev", None),
        P(None, None, "dev"),
        P("dev", None),
        P(),
        P(),
        P(("grp", "dev"), None),
        P(),
        P(),
        P(),
        P(),
        P(),
    )
    return jax.shard_map(
        shards,
        mesh=mesh,
        in_specs=placed,
        out_specs=(P("grp", None), P(("grp", "dev"), None)),
        check_vma=False,
    )
```

```python
import functools

import jax
import jax.numpy as jnp
from jax import lax
from jax.experimental import pallas as pl
from jax.experimental.pallas import tpu as pltpu
from jax.sharding import PartitionSpec as P

MESH = pl.DeviceIdType.MESH
BF16 = jnp.bfloat16
F32 = jnp.float32

TW = 1536
TH = 64
TP = 256
HB = 192
FB = 512
SW = 768
GW = 192
SH = 48
ROWS = 2048
DIL = (1, 8, 32, 128)
LOG2E = 1.4426950408889634
HIDE = -1e30
SCALE = LOG2E * SH**-0.5


def dot(a, b):
    return jnp.dot(a, b, preferred_element_type=F32)


def dot_nt(a, b):
    return lax.dot_general(a, b, (((1,), (1,)), ((), ())), preferred_element_type=F32)


def norm(v, gain):
    center = v - jnp.mean(v, axis=-1, keepdims=True)
    spread = jnp.mean(center * center, axis=-1, keepdims=True)
    return center * lax.rsqrt(spread + 1e-06) * gain


def head_of(shape):
    return (lax.broadcasted_iota(jnp.int32, shape, 1) % GW) // SH


def attend(q, keys, values):
    s = dot_nt(q, keys)
    m = jnp.max(s, axis=-1, keepdims=True)
    e = jnp.exp2((s - m) * SCALE).astype(BF16)
    return m, e, dot(e, values)


def with_ones(vt):
    tail = lax.broadcasted_iota(jnp.int32, (16, vt.shape[1]), 0) == 0
    tail = jnp.where(tail, 1.0, 0.0)
    pieces = []
    for j in range(4):
        pieces += [vt[j * SH : (j + 1) * SH, :], tail]
    return jnp.concatenate(pieces, axis=0).astype(BF16)


def only_head(j, rows, bias):
    lane = lax.broadcasted_iota(jnp.int32, (rows, 256), 1)
    mine = jnp.logical_and(lane >= j * SH, lane < (j + 1) * SH)
    return jnp.logical_or(mine, lane == GW) if bias else mine


def encoder_kernel(
    patches,
    w_patch,
    w_tqkv,
    w_to,
    w_gu,
    w_down,
    w_in,
    tokens,
    w_sqkv,
    tgain,
    sgain,
    positions,
    pattern,
    qk0_out,
    vt0_out,
    near,
    stats,
    q1_out,
    q2_out,
    q3_out,
    kv1,
    kv2,
    kv3,
    em,
    new_out,
    patches_s,
    w_patch_s,
    w_tqkv_s,
    wto_s,
    w_gu_s,
    w_down_s,
    w_in_s,
    tok_s,
    w_raw,
    w_slide_s,
    hs,
    qk0_s,
    vt0_s,
    kvc1,
    kvc2,
    kvc3,
    x0_s,
    att_s,
    pp_s,
    load_sem,
    out_sem,
    own_sem,
    send_sem,
    recv_sem,
    att_send,
    att_recv,
):
    grp = lax.axis_index("grp")
    dev = lax.axis_index("dev")
    core = grp % 2
    plane = grp // 4
    chip = (grp // 2) * 8 + dev
    local16 = (grp // 2) % 2 * 8 + dev
    sibling = (grp // 2) * 2 + (1 - core)

    z = dev % 4
    side = (grp // 2) % 2 * 2 + dev // 4

    def peer8(i):
        return (grp, (dev + i) % 8)

    def peer_z(i):
        return (grp, dev // 4 * 4 + (z + i) % 4)

    def peer_y(i):
        to = (side + i) % 4
        return (plane * 4 + to // 2 * 2 + core, to % 2 * 4 + z)

    def peer_x(i):
        return ((plane + i) % 4 * 4 + grp % 4, dev)

    def peer_grp(i):
        return ((grp + i) % 16, dev)

    def load(src, dst, at):
        copy = pltpu.make_async_copy(src, dst, load_sem.at[at])
        copy.start()
        return copy

    ld_tok = load(tokens, tok_s, 0)
    ld_raw = load(w_sqkv, w_raw, 1)
    ld_patch = load(w_patch, w_patch_s, 2)
    ld_tqkv = load(w_tqkv, w_tqkv_s, 3)
    ld_gu = load(w_gu, w_gu_s, 4)
    ld_down = load(w_down, w_down_s, 5)
    ld_in = load(w_in, w_in_s, 6)

    my_patch = pl.ds(pl.multiple_of(dev * 96, 32), 96)
    half_row = pl.multiple_of(core * 96, 32)
    my_half = pl.ds(pl.multiple_of(dev * HB + core * 96, 32), 96)
    quarter = pl.ds(pl.multiple_of(plane * 384, 128), 384)
    my_shard = pl.ds(pl.multiple_of(dev * HB, 64), HB)

    barrier = pltpu.get_barrier_semaphore()

    @pl.loop(1, 8)
    def _(i):
        pl.semaphore_signal(barrier, inc=1, device_id=peer8(i), device_id_type=MESH)

    @pl.loop(1, 16)
    def _(i):
        pl.semaphore_signal(barrier, inc=1, device_id=peer_grp(i), device_id_type=MESH)

    across = (plane * 4 + (1 - side // 2) * 2 + core, (dev + 4) % 8)
    pl.semaphore_signal(barrier, inc=1, device_id=across, device_id_type=MESH)
    pl.semaphore_wait(barrier, 23)

    own_patch = pltpu.make_async_copy(patches, patches_s.at[my_patch], own_sem.at[0])
    own_patch.start()
    own_wto = pltpu.make_async_copy(w_to, wto_s.at[my_shard], own_sem.at[1])
    own_wto.start()

    def push(src, dst, at, to):
        pltpu.make_async_remote_copy(
            src_ref=src,
            dst_ref=dst,
            send_sem=send_sem.at[at],
            recv_sem=recv_sem.at[at],
            device_id=to,
            device_id_type=MESH,
        ).start()

    def landed(ref, sem):
        pltpu.make_async_copy(ref, ref, sem).wait()

    @pl.loop(1, 8)
    def _(i):
        push(patches, patches_s.at[my_patch], 0, peer8(i))

    @pl.loop(1, 8)
    def _(i):
        push(w_to.at[pl.ds(half_row, 96), quarter], wto_s.at[my_half, quarter], 1, peer8(i))

    ld_raw.wait()
    group = [
        sum(jnp.where(pattern[g] == p, g, 0) for g in range(4)) for p in range(4)
    ]

    @pl.loop(0, 3)
    def _(c):
        at = pl.ds(pl.multiple_of(c * 256, 256), 256)

        def part(index, p):
            pair = jnp.where(group[p] >= 2, w_raw[index, at, 384:], w_raw[index, at, :384])
            return jnp.where(group[p] % 2 == 1, pair[:, GW:], pair[:, :GW])

        for index in range(3):
            w_slide_s[0, at, index * 256 : (index + 1) * 256] = jnp.concatenate(
                [part(index, 0), jnp.zeros((256, 64), BF16)], axis=1
            )
        for p in range(1, 4):
            w_slide_s[p, at, :384] = jnp.concatenate([part(2, p), part(1, p)], axis=1)
            w_slide_s[p, at, 384:] = jnp.concatenate(
                [jnp.zeros((256, GW), BF16), part(0, p)], axis=1
            )

    lane128 = lax.broadcasted_iota(jnp.int32, (1, 128), 1)
    places = lax.fori_loop(
        0,
        48,
        lambda n, held: jnp.where(lane128 == n, positions[n], held),
        jnp.full((1, 128), -1, jnp.int32),
    )
    ld_tok.wait()
    first = (grp * 8 + dev) * ROWS

    @pl.loop(0, 8)
    def _(c):
        at = pl.ds(pl.multiple_of(c * 256, 256), 256)
        h = norm(tok_s[at, :].astype(F32), sgain[...].reshape(1, SW))
        for b in range(6):
            hs[b, at, :] = h[:, b * 128 : (b + 1) * 128]
        y = dot(h.astype(BF16), w_slide_s[0])
        row = lax.broadcasted_iota(jnp.int32, (256, 128), 0) + (first + c * 256)
        stale = jnp.max(jnp.where(row == places, 1.0, 0.0), axis=1, keepdims=True)
        column = lax.broadcasted_iota(jnp.int32, (256, 512), 1)
        qk = jnp.where(column == 256 + GW, stale * HIDE, y[:, :512])
        qk0_s[at, :] = jnp.where(column == GW, 1.0, qk).astype(BF16)
        vt0_s[:, at] = with_ones(y[:, 512 : 512 + GW].T)

    out0 = pltpu.make_async_copy(qk0_s, qk0_out, out_sem.at[0])
    out0.start()
    out1 = pltpu.make_async_copy(vt0_s, vt0_out, out_sem.at[1])
    out1.start()

    own_patch.wait()
    landed(patches_s.at[pl.ds(0, 672)], recv_sem.at[0])
    ld_patch.wait()
    ld_tqkv.wait()

    lanes = lax.broadcasted_iota(jnp.int32, (TP, HB), 1) // TH

    @pl.loop(0, 3)
    def _(t):
        at = pl.ds(pl.multiple_of(t * TP, TP), TP)
        x0 = dot(patches_s[at, :], w_patch_s[...]).astype(BF16)
        x0_s[at, :] = x0
        h1 = norm(x0.astype(F32), tgain[0:1, :]).astype(BF16)
        q = dot_nt(h1, w_tqkv_s[0]).astype(BF16)
        k = dot_nt(h1, w_tqkv_s[1]).astype(BF16)
        vt = dot_nt(w_tqkv_s[2], h1).astype(BF16)
        for h in range(3):
            s = dot_nt(jnp.where(lanes == h, q, jnp.zeros_like(q)), k) * (TH**-0.5)
            e = jnp.exp(s - jnp.max(s, axis=-1, keepdims=True))
            probs = (e / jnp.sum(e, axis=-1, keepdims=True)).astype(BF16)
            o = dot_nt(vt[h * TH : (h + 1) * TH, :], probs)
            rows = pl.ds(pl.multiple_of(dev * HB + h * TH, 64), TH)
            att_s[t, rows, :] = o.astype(BF16)

        @pl.loop(1, 8)
        def _(i):
            pltpu.make_async_remote_copy(
                src_ref=att_s.at[t, my_shard],
                dst_ref=att_s.at[t, my_shard],
                send_sem=att_send.at[t],
                recv_sem=att_recv.at[t],
                device_id=peer8(i),
                device_id_type=MESH,
            ).start()

    own_wto.wait()
    landed(wto_s.at[pl.ds(0, 672), quarter], recv_sem.at[1])

    @pl.loop(1, 8)
    def _(i):
        half = pl.ds(pl.multiple_of(((dev + i) % 8) * HB + core * 96, 32), 96)

        @pl.loop(1, 4)
        def _(step):
            push(wto_s.at[half, quarter], wto_s.at[half, quarter], 10, peer_x(step))

    for p, kvc, q_out in ((1, kvc1, q1_out), (2, kvc2, q2_out), (3, kvc3, q3_out)):
        r = DIL[p]
        n = ROWS // r
        picked = jnp.concatenate(
            [
                jnp.concatenate([hs[b, pl.ds(j, n, stride=r), :] for b in range(6)], axis=1)
                for j in range(4)
            ],
            axis=0,
        ).astype(BF16)
        y = dot(picked, w_slide_s[p])
        head = head_of((n, SW))
        mine = jnp.zeros((n, SW), F32)
        for j in range(4):
            mine = jnp.where(head == j, y[j * n : (j + 1) * n, :], mine)
        kvc[...] = mine[:, :384].astype(BF16)
        q_out[...] = mine[:, 384:].astype(BF16)

    at1 = pl.ds(pl.multiple_of(dev * 256, 256), 256)
    at1_y = pl.ds(pl.multiple_of((dev + 4) % 8 * 256, 256), 256)
    at2 = pl.ds(pl.multiple_of((core * 16 + local16) * 64, 64), 64)
    at2_z = pl.ds(pl.multiple_of((core * 16 + local16 // 4 * 4) * 64, 256), 256)
    at3 = pl.ds(pl.multiple_of((core * 64 + chip) * 16, 16), 16)
    at3_z = pl.ds(pl.multiple_of((core * 64 + chip // 4 * 4) * 16, 64), 64)
    at3_y = pl.ds(pl.multiple_of((core * 64 + chip // 16 * 16) * 16, 256), 256)
    own1 = pltpu.make_async_copy(kvc1, kv1.at[at1], own_sem.at[2])
    own2 = pltpu.make_async_copy(kvc2, kv2.at[at2], own_sem.at[3])
    own3 = pltpu.make_async_copy(kvc3, kv3.at[at3], own_sem.at[4])
    own1.start()
    own2.start()
    own3.start()

    push(kvc1, kv1.at[at1], 13, (grp, (dev + 4) % 8))

    @pl.loop(1, 4)
    def _(i):
        push(kvc3, kv3.at[at3], 2, peer_z(i))
        push(kvc2, kv2.at[at2], 11, peer_z(i))
        push(kvc1, kv1.at[at1], 14, peer_z(i))

    def near_rows(first_block, last_block):
        @pl.loop(first_block, last_block)
        def _(b):
            at = pl.ds(pl.multiple_of(b * 256, 256), 256)
            q = qk0_s[at, 0:256]
            for j in range(4):
                s = dot_nt(
                    qk0_s[:, 256:512],
                    jnp.where(only_head(j, 256, True), q, jnp.zeros_like(q)),
                )
                m = jnp.max(s, axis=0, keepdims=True)
                e = jnp.exp2((s - m) * SCALE).astype(BF16)
                o = dot(vt0_s[j * 64 : (j + 1) * 64, :], e)
                count = o[SH : SH + 1, :]
                near[j * SH : (j + 1) * SH, at] = (o[:SH, :] / count).astype(BF16)
                stats[j : j + 1, at] = m
                stats[4 + j : 5 + j, at] = count

    near_rows(0, 1)

    own3.wait()
    landed(kv3.at[pl.ds(0, 3 * 16)], recv_sem.at[2])
    own2.wait()
    landed(kv2.at[pl.ds(0, 3 * 64)], recv_sem.at[11])
    landed(kv1.at[at1_y], recv_sem.at[13])

    @pl.loop(1, 4)
    def _(i):
        push(kv3.at[at3_z], kv3.at[at3_z], 3, peer_y(i))
        push(kv2.at[at2_z], kv2.at[at2_z], 12, peer_y(i))
        push(kv1.at[at1_y], kv1.at[at1_y], 14, peer_z(i))

    near_rows(1, 3)

    landed(kv3.at[pl.ds(0, 3 * 64)], recv_sem.at[3])

    @pl.loop(1, 4)
    def _(i):
        push(kv3.at[at3_y], kv3.at[at3_y], 4, peer_x(i))

    landed(wto_s.at[pl.ds(0, 672), pl.ds(0, 1152)], recv_sem.at[10])

    @pl.loop(1, 8)
    def _(i):
        half = pl.ds(pl.multiple_of(((dev + i) % 8) * HB + core * 96, 32), 96)
        push(wto_s.at[half], wto_s.at[half], 5, (sibling, dev))

    near_rows(3, 5)
    landed(wto_s.at[pl.ds(0, 672)], recv_sem.at[5])
    ld_gu.wait()

    eight = lax.broadcasted_iota(jnp.int32, (8, 1), 0)

    def feed(t, sums):
        x_sum, h_sum = sums
        at = pl.ds(pl.multiple_of(t * TP, TP), TP)
        landed(att_s.at[t, pl.ds(0, 7 * HB)], att_recv.at[t])
        att = att_s[t].T
        x1 = (x0_s[at, :].astype(F32) + dot(att, wto_s[...])).astype(BF16).astype(F32)
        h2 = norm(x1, tgain[1:2, :]).astype(BF16)
        gate = dot(h2, w_gu_s[0])
        up = dot(h2, w_gu_s[1])
        hidden = (jax.nn.silu(gate) * up).astype(BF16).astype(F32)
        x_sum = x_sum + jnp.where(eight == t, jnp.sum(x1, axis=0, keepdims=True), 0.0)
        h_sum = h_sum + jnp.where(eight == t, jnp.sum(hidden, axis=0, keepdims=True), 0.0)
        return x_sum, h_sum

    x_sum, h_sum = lax.fori_loop(
        0, 3, feed, (jnp.zeros((8, TW), F32), jnp.zeros((8, FB), F32))
    )
    ld_down.wait()
    h_mean = h_sum * (1.0 / TP)
    coarse = h_mean.astype(BF16)
    fine = (h_mean - coarse.astype(F32)).astype(BF16)
    both = jnp.concatenate([coarse.astype(F32), fine.astype(F32)], axis=0).astype(BF16)
    part = dot(both, w_down_s[...])
    pp_s[dev] = part[0:8] + part[8:16]

    @pl.loop(1, 8)
    def _(i):
        push(pp_s.at[dev], pp_s.at[dev], 6, peer8(i))

    near_rows(5, 6)
    ld_in.wait()
    landed(pp_s.at[pl.ds(0, 7)], recv_sem.at[6])
    pooled = x_sum * (1.0 / TP) + jnp.sum(pp_s[...], axis=0)
    normed = norm(pooled, tgain[2:3, :]).astype(BF16)
    em[grp] = dot(normed, w_in_s[...]).astype(BF16).astype(F32)

    @pl.loop(1, 16)
    def _(i):
        push(em.at[grp], em.at[grp], 7, peer_grp(i))

    half3 = pl.ds(pl.multiple_of(core * 1024, 1024), 1024)
    landed(kv2.at[pl.ds(0, 3 * 256)], recv_sem.at[12])
    push(kv2.at[half3], kv2.at[half3], 9, (sibling, dev))
    landed(kv3.at[pl.ds(0, 3 * 256)], recv_sem.at[4])
    push(kv3.at[half3], kv3.at[half3], 8, (sibling, dev))
    near_rows(6, 8)
    landed(em.at[pl.ds(0, 15)], recv_sem.at[7])
    fresh = norm(em[...].reshape(128, SW), sgain[...].reshape(1, SW)).astype(BF16)
    for p in range(4):
        new_out[:, p * SW : (p + 1) * SW] = dot(fresh, w_slide_s[p])

    own1.wait()
    landed(kv1.at[pl.ds(0, 6 * 256)], recv_sem.at[14])
    landed(kv3.at[half3], recv_sem.at[8])
    landed(kv2.at[half3], recv_sem.at[9])
    out0.wait()
    out1.wait()

    landed(patches_s.at[pl.ds(0, 672)], send_sem.at[0])
    landed(wto_s.at[pl.ds(0, 672), quarter], send_sem.at[1])
    landed(wto_s.at[pl.ds(0, 672), pl.ds(0, 1152)], send_sem.at[10])
    landed(kv3.at[pl.ds(0, 3 * 16)], send_sem.at[2])
    landed(kv3.at[pl.ds(0, 3 * 64)], send_sem.at[3])
    landed(kv3.at[pl.ds(0, 3 * 256)], send_sem.at[4])
    landed(kv2.at[pl.ds(0, 3 * 64)], send_sem.at[11])
    landed(kv2.at[pl.ds(0, 3 * 256)], send_sem.at[12])
    landed(kv1.at[at1_y], send_sem.at[13])
    landed(kv1.at[pl.ds(0, 6 * 256)], send_sem.at[14])
    landed(wto_s.at[pl.ds(0, 672)], send_sem.at[5])
    landed(pp_s.at[pl.ds(0, 7)], send_sem.at[6])
    landed(em.at[pl.ds(0, 15)], send_sem.at[7])
    landed(kv3.at[half3], send_sem.at[8])
    landed(kv2.at[half3], send_sem.at[9])

    @pl.loop(0, 3)
    def _(t):
        landed(att_s.at[t, pl.ds(0, 7 * HB)], att_send.at[t])


def run_encoder(*args):
    hbm = pl.BlockSpec(memory_space=pl.ANY)
    vmem = pl.BlockSpec(memory_space=pltpu.VMEM)
    shape = jax.ShapeDtypeStruct
    return pl.pallas_call(
        encoder_kernel,
        out_shape=(
            shape((ROWS, 512), BF16),
            shape((256, ROWS), BF16),
            shape((GW, ROWS), BF16),
            shape((8, ROWS), F32),
            shape((256, 384), BF16),
            shape((64, 384), BF16),
            shape((16, 384), BF16),
            shape((2048, 384), BF16),
            shape((2048, 384), BF16),
            shape((2048, 384), BF16),
            shape((16, 8, SW), F32),
            shape((128, 4 * SW), F32),
        ),
        in_specs=[hbm] * 9 + [vmem] * 2 + [pl.BlockSpec(memory_space=pltpu.SMEM)] * 2,
        out_specs=(hbm, hbm, vmem, vmem, vmem, vmem, vmem, hbm, hbm, hbm, vmem, vmem),
        scratch_shapes=[
            pltpu.VMEM((768, 588), BF16),
            pltpu.VMEM((588, TW), BF16),
            pltpu.VMEM((3, HB, TW), BF16),
            pltpu.VMEM((TW, TW), BF16),
            pltpu.VMEM((2, TW, FB), BF16),
            pltpu.VMEM((FB, TW), BF16),
            pltpu.VMEM((TW, SW), BF16),
            pltpu.VMEM((ROWS, SW), BF16),
            pltpu.VMEM((3, SW, SW), BF16),
            pltpu.VMEM((4, SW, SW), BF16),
            pltpu.VMEM((6, ROWS, 128), F32),
            pltpu.VMEM((ROWS, 512), BF16),
            pltpu.VMEM((256, ROWS), BF16),
            pltpu.VMEM((256, 384), BF16),
            pltpu.VMEM((64, 384), BF16),
            pltpu.VMEM((16, 384), BF16),
            pltpu.VMEM((768, TW), BF16),
            pltpu.VMEM((3, TW, TP), BF16),
            pltpu.VMEM((8, 8, TW), F32),
            pltpu.SemaphoreType.DMA((7,)),
            pltpu.SemaphoreType.DMA((2,)),
            pltpu.SemaphoreType.DMA((5,)),
            pltpu.SemaphoreType.DMA((15,)),
            pltpu.SemaphoreType.DMA((15,)),
            pltpu.SemaphoreType.DMA((3,)),
            pltpu.SemaphoreType.DMA((3,)),
        ],
        compiler_params=pltpu.CompilerParams(
            collective_id=0, has_side_effects=True, vmem_limit_bytes=60 * 1024 * 1024
        ),
        name="encode",
    )(*args)


def slide_kernel(
    positions,
    pattern,
    qk0,
    vt0,
    near,
    stats,
    q1,
    q2,
    q3,
    kv1,
    kv2,
    kv3,
    tokens,
    new,
    em,
    w_so,
    out,
    embed_out,
    qk0_s,
    vt0_s,
    near_s,
    stats_s,
    q1_s,
    q2_s,
    q3_s,
    kv1_s,
    kv2_s,
    kv3_s,
    tok_s,
    far_s,
    sem,
):
    step = pl.program_id(0)
    place = lax.axis_index("grp") * 8 + lax.axis_index("dev")

    @pl.when(step == 0)
    def _():
        copies = [
            pltpu.make_async_copy(src, dst, sem.at[at])
            for at, (src, dst) in enumerate(
                (
                    (q1, q1_s),
                    (q2, q2_s),
                    (q3, q3_s),
                    (kv1, kv1_s),
                    (kv2, kv2_s),
                    (kv3, kv3_s),
                    (tokens, tok_s),
                    (near, near_s),
                    (qk0, qk0_s),
                    (vt0, vt0_s),
                    (stats, stats_s),
                )
            )
        ]
        for copy in copies:
            copy.start()
        embed_out[...] = em[pl.ds(pl.multiple_of((place // 8) * 8, 8), 8), :][0:3].astype(BF16)
        far_s[...] = jnp.zeros_like(far_s)
        for copy in copies:
            copy.wait()

        def put(ref, row, vector, columns=None):
            base = pl.multiple_of((row // 16) * 16, 16)
            width = ref.shape[1]
            block = ref[pl.ds(base, 16), :].astype(F32)
            hit = lax.broadcasted_iota(jnp.int32, (16, width), 0) == row - base
            if columns is not None:
                hit = jnp.logical_and(hit, columns)
            ref[pl.ds(base, 16), :] = jnp.where(hit, vector, block).astype(BF16)

        head16 = head_of((16, 384))

        def insert(n, found):
            pos = positions[n]
            row = (n // 3) * 8 + n % 3
            local = pos // ROWS == place
            here = pos % ROWS

            @pl.when(local)
            def _():
                put(tok_s, here, em[pl.ds(row, 1), :])

            for p, q_s, kv_s in ((1, q1_s, kv1_s), (2, q2_s, kv2_s), (3, q3_s, kv3_s)):
                r = DIL[p]
                count = ROWS // r
                owner = pos // ROWS
                seen = pos % r < 4
                within = owner // r == place // r
                if p == 1:
                    slot = owner % 8
                else:
                    grp = owner // 8
                    at_chip = (grp // 2) * 8 + owner % 8
                    slot = (grp % 2) * 16 + at_chip % 16 if p == 2 else (grp % 2) * 64 + at_chip
                columns = head16 == pos % r

                @pl.when(jnp.logical_and(seen, within))
                def _():
                    put(
                        kv_s,
                        slot * count + here // r,
                        new[pl.ds(row, 1), p * SW : p * SW + 384],
                        columns,
                    )

                    @pl.when(local)
                    def _():
                        put(
                            q_s,
                            here // r,
                            new[pl.ds(row, 1), p * SW + 384 : (p + 1) * SW],
                            columns,
                        )

            return found + jnp.where(local, 1, 0)

        found = lax.fori_loop(0, 48, insert, jnp.int32(0))

        @pl.when(found > 0)
        def _():
            slots = lax.broadcasted_iota(jnp.int32, (128, 1), 0)
            places = lax.fori_loop(
                0,
                48,
                lambda n, held: jnp.where(slots == (n // 3) * 8 + n % 3, positions[n], held),
                jnp.full((128, 1), -1, jnp.int32),
            )
            hide = jnp.where(places // ROWS == place, 0.0, HIDE)
            lane = lax.broadcasted_iota(jnp.int32, (128, 256), 1)
            fresh_q = jnp.where(lane == GW, 1.0, new[:, 0:256]).astype(BF16)
            fresh_k = new[:, 256:512].astype(BF16)
            fresh_vt = with_ones(new[:, 512 : 512 + GW].T)

            made = []
            for j in range(4):
                q = jnp.where(only_head(j, 128, True), fresh_q, jnp.zeros_like(fresh_q))
                s_old = dot_nt(qk0_s[:, 256:512], q)
                s_new = dot_nt(fresh_k, q) + hide
                m = jnp.maximum(
                    jnp.max(s_old, axis=0, keepdims=True), jnp.max(s_new, axis=0, keepdims=True)
                )
                e_old = jnp.exp2((s_old - m) * SCALE).astype(BF16)
                e_new = jnp.exp2((s_new - m) * SCALE).astype(BF16)
                head_rows = slice(j * 64, (j + 1) * 64)
                o = dot(vt0_s[head_rows, :], e_old) + dot(fresh_vt[head_rows, :], e_new)
                made.append(o[:SH, :] / o[SH : SH + 1, :])
            made = jnp.concatenate(made, axis=0).astype(BF16)

            @pl.loop(0, 4)
            def _(b):
                at = pl.ds(pl.multiple_of(b * 512, 512), 512)
                q = qk0_s[at, 0:256]
                joined = []
                for j in range(4):
                    k = jnp.where(only_head(j, 128, False), fresh_k, jnp.zeros_like(fresh_k))
                    s = dot_nt(k, q) + hide
                    m_old = stats_s[j : j + 1, at]
                    m = jnp.maximum(m_old, jnp.max(s, axis=0, keepdims=True))
                    weight = stats_s[4 + j : 5 + j, at] * jnp.exp2((m_old - m) * SCALE)
                    e = jnp.exp2((s - m) * SCALE).astype(BF16)
                    o = dot(fresh_vt[j * 64 : (j + 1) * 64, :], e)
                    held = near_s[j * SH : (j + 1) * SH, at].astype(F32)
                    joined.append((held * weight + o[:SH, :]) / (weight + o[SH : SH + 1, :]))
                row = lax.broadcasted_iota(jnp.int32, (128, 512), 1) + (place * ROWS + b * 512)
                hit = jnp.where(row == places, 1.0, 0.0)
                anew = dot(made, hit.astype(BF16))
                taken = jnp.max(hit, axis=0, keepdims=True) > 0.0
                near_s[:, at] = jnp.where(taken, anew, jnp.concatenate(joined, axis=0)).astype(
                    BF16
                )

        def far_heads(p, q_s, kv_s, heads):
            r = DIL[p]
            count = ROWS // r
            q = q_s[...]
            kv = kv_s[...]
            head = head_of((count, 384))
            stack = [jnp.where(head == j, q, jnp.zeros_like(q)) for j in heads]
            _, e, o = attend(jnp.concatenate(stack, axis=0), kv, kv)
            o = o[:, 0:256] / jnp.sum(e.astype(F32), axis=-1, keepdims=True)
            for at, j in enumerate(heads):
                mine = jnp.where(
                    only_head(j, count, False), o[at * count : (at + 1) * count, :], 0.0
                )
                for b in range(2):
                    far_s[2 * (p - 1) + b, pl.ds(j, count, stride=r), :] = mine[
                        :, b * 128 : (b + 1) * 128
                    ]

        for j in range(4):
            far_heads(1, q1_s, kv1_s, (j,))
        far_heads(2, q2_s, kv2_s, (0, 1, 2, 3))
        far_heads(3, q3_s, kv3_s, (0, 1, 2, 3))

    at = pl.ds(pl.multiple_of(step * 256, 256), 256)

    def weights(p):
        group = sum(jnp.where(pattern[g] == p, g, 0) for g in range(4))
        return w_so[pl.ds(pl.multiple_of(group * GW, 64), GW), :]

    total = tok_s[at, :].astype(F32) + dot(near_s[:, at].T, weights(0))
    for p in range(3):
        far = jnp.concatenate([far_s[2 * p, at, :], far_s[2 * p + 1, at, :]], axis=1)
        total = total + dot(far[:, 0:GW].astype(BF16), weights(p + 1))
    out[...] = total.astype(BF16)


def run_slide(*args):
    hbm = pl.BlockSpec(memory_space=pl.ANY)
    vmem = pl.BlockSpec(memory_space=pltpu.VMEM)
    return pl.pallas_call(
        slide_kernel,
        out_shape=(
            jax.ShapeDtypeStruct((ROWS, SW), BF16),
            jax.ShapeDtypeStruct((3, SW), BF16),
        ),
        grid_spec=pltpu.PrefetchScalarGridSpec(
            num_scalar_prefetch=2,
            grid=(8,),
            in_specs=[hbm] * 11 + [vmem] * 3,
            out_specs=(
                pl.BlockSpec((256, SW), lambda i, *_: (i, 0)),
                pl.BlockSpec((3, SW), lambda i, *_: (0, 0)),
            ),
            scratch_shapes=[
                pltpu.VMEM((ROWS, 512), BF16),
                pltpu.VMEM((256, ROWS), BF16),
                pltpu.VMEM((GW, ROWS), BF16),
                pltpu.VMEM((8, ROWS), F32),
                pltpu.VMEM((256, 384), BF16),
                pltpu.VMEM((64, 384), BF16),
                pltpu.VMEM((16, 384), BF16),
                pltpu.VMEM((2048, 384), BF16),
                pltpu.VMEM((2048, 384), BF16),
                pltpu.VMEM((2048, 384), BF16),
                pltpu.VMEM((ROWS, SW), BF16),
                pltpu.VMEM((6, ROWS, 128), F32),
                pltpu.SemaphoreType.DMA((11,)),
            ],
        ),
        compiler_params=pltpu.CompilerParams(vmem_limit_bytes=56 * 1024 * 1024),
        name="slide",
    )(*args)


def shards(
    tile_patches,
    w_patch,
    w_tqkv,
    w_to,
    w_gu,
    w_down,
    tile_gain,
    w_in,
    slide_tokens,
    slide_gain,
    w_sqkv,
    w_so,
    pattern_of_group,
    new_positions,
):
    qk0, vt0, near, stats, q1, q2, q3, kv1, kv2, kv3, em, new = run_encoder(
        tile_patches,
        w_patch,
        jnp.transpose(w_tqkv, (0, 2, 1)),
        w_to,
        w_gu,
        w_down,
        w_in,
        slide_tokens,
        w_sqkv,
        tile_gain,
        slide_gain,
        new_positions,
        pattern_of_group,
    )
    slide_out, tile_embed = run_slide(
        new_positions,
        pattern_of_group,
        qk0,
        vt0,
        near,
        stats,
        q1,
        q2,
        q3,
        kv1,
        kv2,
        kv3,
        slide_tokens,
        new,
        em.reshape(128, SW),
        w_so,
    )
    return (tile_embed, slide_out)


def solution(mesh):
    placed = (
        P(("grp", "dev"), None),
        P(),
        P(None, None, "dev"),
        P("dev", None),
        P(None, None, "dev"),
        P("dev", None),
        P(),
        P(),
        P(("grp", "dev"), None),
        P(),
        P(),
        P(),
        P(),
        P(),
    )
    return jax.shard_map(
        shards,
        mesh=mesh,
        in_specs=placed,
        out_specs=(P("grp", None), P(("grp", "dev"), None)),
        check_vma=False,
    )
```

```python
import functools

import jax
import jax.numpy as jnp
from jax import lax
from jax.experimental import pallas as pl
from jax.experimental.pallas import tpu as pltpu
from jax.sharding import PartitionSpec as P

MESH = pl.DeviceIdType.MESH
BF16 = jnp.bfloat16
F32 = jnp.float32

TW = 1536
TH = 64
TP = 256
HB = 192
FB = 512
SW = 768
GW = 192
SH = 48
ROWS = 2048
DIL = (1, 8, 32, 128)
LOG2E = 1.4426950408889634
HIDE = -1e30
KEYS_AT, HALF_AT, FEED_AT, EMBED_AT = 6, 10, 12, 14
SCALE = LOG2E * SH**-0.5


def dot(a, b):
    return jnp.dot(a, b, preferred_element_type=F32)


def dot_nt(a, b):
    return lax.dot_general(a, b, (((1,), (1,)), ((), ())), preferred_element_type=F32)


def norm(v, gain):
    center = v - jnp.mean(v, axis=-1, keepdims=True)
    spread = jnp.mean(center * center, axis=-1, keepdims=True)
    return center * lax.rsqrt(spread + 1e-06) * gain


def head_of(shape):
    return (lax.broadcasted_iota(jnp.int32, shape, 1) % GW) // SH


def attend(q, keys, values):
    s = dot_nt(q, keys)
    m = jnp.max(s, axis=-1, keepdims=True)
    e = jnp.exp2((s - m) * SCALE).astype(BF16)
    return m, e, dot(e, values)


def with_ones(vt):
    tail = lax.broadcasted_iota(jnp.int32, (16, vt.shape[1]), 0) == 0
    tail = jnp.where(tail, 1.0, 0.0)
    pieces = []
    for j in range(4):
        pieces += [vt[j * SH : (j + 1) * SH, :], tail]
    return jnp.concatenate(pieces, axis=0).astype(BF16)


def only_head(j, rows, bias=False, shift=False):
    lane = lax.broadcasted_iota(jnp.int32, (rows, 256), 1)
    mine = jnp.logical_and(lane >= j * SH, lane < (j + 1) * SH)
    if bias:
        mine = jnp.logical_or(mine, lane == GW)
    if shift:
        mine = jnp.logical_or(mine, lane == GW + 1 + j)
    return mine


def encoder_kernel(
    patches,
    w_patch,
    w_tqkv,
    w_to,
    w_gu,
    w_down,
    w_in,
    tokens,
    w_sqkv,
    tgain,
    sgain,
    positions,
    pattern,
    qk0_out,
    vt0_out,
    near,
    stats,
    q1_out,
    q2_out,
    q3_out,
    kv1,
    kv2,
    kv3,
    em,
    new_out,
    patches_s,
    w_patch_s,
    w_tqkv_s,
    wto_s,
    w_gu_s,
    w_down_s,
    w_in_s,
    tok_s,
    w_raw,
    w_slide_s,
    hs,
    qk0_s,
    vt0_s,
    kvc1,
    kvc2,
    kvc3,
    x0_s,
    att_s,
    pp_s,
    largest,
    x_sum_s,
    load_sem,
    out_sem,
    own_sem,
    send_sem,
    recv_sem,
    att_send,
    att_recv,
):
    grp = lax.axis_index("grp")
    dev = lax.axis_index("dev")
    core = grp % 2
    plane = grp // 4
    chip = (grp // 2) * 8 + dev
    local16 = (grp // 2) % 2 * 8 + dev
    sibling = (grp // 2) * 2 + (1 - core)

    z = dev % 4
    side = (grp // 2) % 2 * 2 + dev // 4

    def peer8(i):
        return (grp, (dev + i) % 8)

    def peer_z(i):
        return (grp, dev // 4 * 4 + (z + i) % 4)

    def peer_y(i):
        to = (side + i) % 4
        return (plane * 4 + to // 2 * 2 + core, to % 2 * 4 + z)

    def peer_x(i):
        return ((plane + i) % 4 * 4 + grp % 4, dev)

    def peer_grp(i):
        return ((grp + i) % 16, dev)

    def load(src, dst, at):
        copy = pltpu.make_async_copy(src, dst, load_sem.at[at])
        copy.start()
        return copy

    ld_tok = load(tokens, tok_s, 0)
    ld_raw = load(w_sqkv, w_raw, 1)
    ld_patch = load(w_patch, w_patch_s, 2)
    ld_tqkv = load(w_tqkv, w_tqkv_s, 3)
    ld_gu = load(w_gu, w_gu_s, 4)
    ld_down = load(w_down, w_down_s, 5)
    ld_in = load(w_in, w_in_s, 6)

    my_patch = pl.ds(pl.multiple_of(dev * 96, 32), 96)
    half_row = pl.multiple_of(core * 96, 32)
    my_half = pl.ds(pl.multiple_of(dev * HB + core * 96, 32), 96)
    quarter = pl.ds(pl.multiple_of(plane * 384, 128), 384)
    my_shard = pl.ds(pl.multiple_of(dev * HB, 64), HB)

    barrier = pltpu.get_barrier_semaphore()

    @pl.loop(1, 8)
    def _(i):
        pl.semaphore_signal(barrier, inc=1, device_id=peer8(i), device_id_type=MESH)

    @pl.loop(1, 16)
    def _(i):
        pl.semaphore_signal(barrier, inc=1, device_id=peer_grp(i), device_id_type=MESH)

    across = (plane * 4 + (1 - side // 2) * 2 + core, (dev + 4) % 8)
    pl.semaphore_signal(barrier, inc=1, device_id=across, device_id_type=MESH)
    pl.semaphore_wait(barrier, 23)

    own_patch = pltpu.make_async_copy(patches, patches_s.at[my_patch], own_sem.at[0])
    own_patch.start()
    own_wto = pltpu.make_async_copy(w_to, wto_s.at[my_shard], own_sem.at[1])
    own_wto.start()

    def push(src, dst, at, to):
        pltpu.make_async_remote_copy(
            src_ref=src,
            dst_ref=dst,
            send_sem=send_sem.at[at],
            recv_sem=recv_sem.at[at],
            device_id=to,
            device_id_type=MESH,
        ).start()

    def landed(ref, sem):
        pltpu.make_async_copy(ref, ref, sem).wait()

    @pl.loop(1, 8)
    def _(i):
        push(patches, patches_s.at[my_patch], 0, peer8(i))

    @pl.loop(1, 8)
    def _(i):
        push(w_to.at[pl.ds(half_row, 96), quarter], wto_s.at[my_half, quarter], 1, peer8(i))

    ld_raw.wait()
    group = [
        sum(jnp.where(pattern[g] == p, g, 0) for g in range(4)) for p in range(4)
    ]

    @pl.loop(0, 3)
    def _(c):
        at = pl.ds(pl.multiple_of(c * 256, 256), 256)

        def part(index, p):
            pair = jnp.where(group[p] >= 2, w_raw[index, at, 384:], w_raw[index, at, :384])
            return jnp.where(group[p] % 2 == 1, pair[:, GW:], pair[:, :GW])

        for index in range(3):
            w_slide_s[0, at, index * 256 : (index + 1) * 256] = jnp.concatenate(
                [part(index, 0), jnp.zeros((256, 64), BF16)], axis=1
            )
        for p in range(1, 4):
            w_slide_s[p, at, :384] = jnp.concatenate([part(2, p), part(1, p)], axis=1)
            w_slide_s[p, at, 384:] = jnp.concatenate(
                [jnp.zeros((256, GW), BF16), part(0, p)], axis=1
            )

    lane128 = lax.broadcasted_iota(jnp.int32, (1, 128), 1)
    places = lax.fori_loop(
        0,
        48,
        lambda n, held: jnp.where(lane128 == n, positions[n], held),
        jnp.full((1, 128), -1, jnp.int32),
    )
    ld_tok.wait()
    first = (grp * 8 + dev) * ROWS
    source = lax.broadcasted_iota(jnp.int32, (256, 256), 0)
    target = lax.broadcasted_iota(jnp.int32, (256, 256), 1)
    to_lane = jnp.logical_and(source < GW, target == GW + 1 + source // SH)
    to_lane = jnp.where(to_lane, 1.0, 0.0).astype(BF16)
    largest[...] = jnp.zeros_like(largest)

    @pl.loop(0, 8)
    def _(c):
        at = pl.ds(pl.multiple_of(c * 256, 256), 256)
        h = norm(tok_s[at, :].astype(F32), sgain[...].reshape(1, SW))
        for b in range(6):
            hs[b, at, :] = h[:, b * 128 : (b + 1) * 128]
        y = dot(h.astype(BF16), w_slide_s[0])
        row = lax.broadcasted_iota(jnp.int32, (256, 128), 0) + (first + c * 256)
        stale = jnp.max(jnp.where(row == places, 1.0, 0.0), axis=1, keepdims=True)
        column = lax.broadcasted_iota(jnp.int32, (256, 256), 1)
        q = y[:, 0:256].astype(BF16)
        k = y[:, 256:512].astype(BF16)
        q_size = jnp.sqrt(dot((q.astype(F32) * q.astype(F32)).astype(BF16), to_lane)) * 1.02
        k_size = dot((k.astype(F32) * k.astype(F32)).astype(BF16), to_lane)
        largest[...] = jnp.maximum(largest[...], jnp.max(k_size, axis=0, keepdims=True))
        q = jnp.where(column == GW, 1.0, q.astype(F32) - q_size)
        qk0_s[at, 0:256] = q.astype(BF16)
        qk0_s[at, 256:512] = jnp.where(column == GW, stale * HIDE, k.astype(F32)).astype(BF16)
        vt0_s[:, at] = with_ones(y[:, 512 : 512 + GW].T)

    bound = (jnp.sqrt(largest[...]) * 1.02).astype(BF16)

    @pl.loop(0, 8)
    def _(c):
        at = pl.ds(pl.multiple_of(c * 256, 256), 256)
        k = qk0_s[at, 256:512]
        qk0_s[at, 256:512] = jnp.where(target > GW, bound.astype(F32), k.astype(F32)).astype(BF16)

    out0 = pltpu.make_async_copy(qk0_s, qk0_out, out_sem.at[0])
    out0.start()
    out1 = pltpu.make_async_copy(vt0_s, vt0_out, out_sem.at[1])
    out1.start()

    own_patch.wait()
    landed(patches_s.at[pl.ds(0, 672)], recv_sem.at[0])
    ld_patch.wait()
    ld_tqkv.wait()

    lanes = lax.broadcasted_iota(jnp.int32, (TP, HB), 1) // TH

    @pl.loop(0, 3)
    def _(t):
        at = pl.ds(pl.multiple_of(t * TP, TP), TP)
        @pl.when(t == 1)
        def _():
            own_wto.wait()
            landed(wto_s.at[pl.ds(0, 672), quarter], recv_sem.at[1])

            @pl.loop(1, 8)
            def _(i):
                half = pl.ds(pl.multiple_of(((dev + i) % 8) * HB + core * 96, 32), 96)

                @pl.loop(1, 4)
                def _(step):
                    push(wto_s.at[half, quarter], wto_s.at[half, quarter], 10, peer_x(step))

        x0 = dot(patches_s[at, :], w_patch_s[...]).astype(BF16)
        x0_s[at, :] = x0
        h1 = norm(x0.astype(F32), tgain[0:1, :]).astype(BF16)
        q = dot_nt(h1, w_tqkv_s[0]).astype(BF16)
        k = dot_nt(h1, w_tqkv_s[1]).astype(BF16)
        vt = dot_nt(w_tqkv_s[2], h1).astype(BF16)
        for h in range(3):
            s = dot_nt(jnp.where(lanes == h, q, jnp.zeros_like(q)), k) * (TH**-0.5)
            e = jnp.exp(s - jnp.max(s, axis=-1, keepdims=True))
            probs = (e / jnp.sum(e, axis=-1, keepdims=True)).astype(BF16)
            o = dot_nt(vt[h * TH : (h + 1) * TH, :], probs)
            rows = pl.ds(pl.multiple_of(dev * HB + h * TH, 64), TH)
            att_s[t, rows, :] = o.astype(BF16)

        @pl.loop(1, 8)
        def _(i):
            pltpu.make_async_remote_copy(
                src_ref=att_s.at[t, my_shard],
                dst_ref=att_s.at[t, my_shard],
                send_sem=att_send.at[t],
                recv_sem=att_recv.at[t],
                device_id=peer8(i),
                device_id_type=MESH,
            ).start()

    for p, kvc, q_out in ((1, kvc1, q1_out), (2, kvc2, q2_out), (3, kvc3, q3_out)):
        r = DIL[p]
        n = ROWS // r
        picked = jnp.concatenate(
            [
                jnp.concatenate([hs[b, pl.ds(j, n, stride=r), :] for b in range(6)], axis=1)
                for j in range(4)
            ],
            axis=0,
        ).astype(BF16)
        y = dot(picked, w_slide_s[p])
        head = head_of((n, SW))
        mine = jnp.zeros((n, SW), F32)
        for j in range(4):
            mine = jnp.where(head == j, y[j * n : (j + 1) * n, :], mine)
        kvc[...] = mine[:, :384].astype(BF16)
        q_out[...] = mine[:, 384:].astype(BF16)

    at1 = pl.ds(pl.multiple_of(dev * 256, 256), 256)
    at1_y = pl.ds(pl.multiple_of((dev + 4) % 8 * 256, 256), 256)
    at2 = pl.ds(pl.multiple_of((core * 16 + local16) * 64, 64), 64)
    at2_z = pl.ds(pl.multiple_of((core * 16 + local16 // 4 * 4) * 64, 256), 256)
    at3 = pl.ds(pl.multiple_of((core * 64 + chip) * 16, 16), 16)
    at3_z = pl.ds(pl.multiple_of((core * 64 + chip // 4 * 4) * 16, 64), 64)
    at3_y = pl.ds(pl.multiple_of((core * 64 + chip // 16 * 16) * 16, 256), 256)
    own1 = pltpu.make_async_copy(kvc1, kv1.at[at1], own_sem.at[2])
    own2 = pltpu.make_async_copy(kvc2, kv2.at[at2], own_sem.at[3])
    own3 = pltpu.make_async_copy(kvc3, kv3.at[at3], own_sem.at[4])
    own1.start()
    own2.start()
    own3.start()

    eight = lax.broadcasted_iota(jnp.int32, (8, 1), 0)
    half3 = pl.ds(pl.multiple_of(core * 1024, 1024), 1024)

    def feed(t, sums):
        x_sum, h_sum = sums
        at = pl.ds(pl.multiple_of(t * TP, TP), TP)
        landed(att_s.at[t, pl.ds(0, 7 * HB)], att_recv.at[t])
        att = att_s[t].T
        x1 = (x0_s[at, :].astype(F32) + dot(att, wto_s[...])).astype(BF16).astype(F32)
        h2 = norm(x1, tgain[1:2, :]).astype(BF16)
        gate = dot(h2, w_gu_s[0])
        up = dot(h2, w_gu_s[1])
        hidden = (jax.nn.silu(gate) * up).astype(BF16).astype(F32)
        x_sum = x_sum + jnp.where(eight == t, jnp.sum(x1, axis=0, keepdims=True), 0.0)
        h_sum = h_sum + jnp.where(eight == t, jnp.sum(hidden, axis=0, keepdims=True), 0.0)
        return x_sum, h_sum

    @pl.loop(0, 16)
    def _(u):
        j = u % 4
        at = pl.ds(pl.multiple_of(u // 4 * 512, 512), 512)
        q = qk0_s[at, 0:256]
        q = jnp.where(only_head(j, 512, True, True), q, jnp.zeros_like(q))
        e = jnp.exp2(dot_nt(qk0_s[:, 256:512], q) * SCALE).astype(BF16)
        o = dot(vt0_s[pl.ds(pl.multiple_of(j * 64, 64), 64), :], e)
        count = o[SH : SH + 1, :]
        near[pl.ds(pl.multiple_of(j * SH, 16), SH), at] = (o[:SH, :] / count).astype(BF16)
        lane = lax.broadcasted_iota(jnp.int32, (8, 256), 1)
        limit = jnp.where(lane == GW + 1 + j, -bound.astype(F32), 0.0).astype(BF16)
        stats[j, :, at] = dot_nt(limit, q)
        stats[4 + j, :, at] = jnp.broadcast_to(count, (8, 512))

        @pl.when(u == KEYS_AT)
        def _():
            push(kvc1, kv1.at[at1], 13, (grp, (dev + 4) % 8))

            @pl.loop(1, 4)
            def _(i):
                push(kvc3, kv3.at[at3], 2, peer_z(i))
                push(kvc2, kv2.at[at2], 11, peer_z(i))
                push(kvc1, kv1.at[at1], 14, peer_z(i))

        @pl.when(u == HALF_AT)
        def _():
            landed(wto_s.at[pl.ds(0, 672), pl.ds(0, 1152)], recv_sem.at[10])

            @pl.loop(1, 8)
            def _(i):
                half = pl.ds(pl.multiple_of(((dev + i) % 8) * HB + core * 96, 32), 96)
                push(wto_s.at[half], wto_s.at[half], 5, (sibling, dev))

        @pl.when(u == FEED_AT)
        def _():
            own3.wait()
            landed(kv3.at[pl.ds(0, 3 * 16)], recv_sem.at[2])
            own2.wait()
            landed(kv2.at[pl.ds(0, 3 * 64)], recv_sem.at[11])
            landed(kv1.at[at1_y], recv_sem.at[13])

            @pl.loop(1, 4)
            def _(i):
                push(kv3.at[at3_z], kv3.at[at3_z], 3, peer_y(i))
                push(kv2.at[at2_z], kv2.at[at2_z], 12, peer_y(i))
                push(kv1.at[at1_y], kv1.at[at1_y], 14, peer_z(i))

            landed(wto_s.at[pl.ds(0, 672)], recv_sem.at[5])
            ld_gu.wait()
            x_sum, h_sum = lax.fori_loop(
                0, 3, feed, (jnp.zeros((8, TW), F32), jnp.zeros((8, FB), F32))
            )
            x_sum_s[...] = x_sum
            ld_down.wait()
            h_mean = h_sum * (1.0 / TP)
            coarse = h_mean.astype(BF16)
            fine = (h_mean - coarse.astype(F32)).astype(BF16)
            both = jnp.concatenate([coarse.astype(F32), fine.astype(F32)], axis=0).astype(BF16)
            part = dot(both, w_down_s[...])
            pp_s[dev] = part[0:8] + part[8:16]

            @pl.loop(1, 8)
            def _(i):
                push(pp_s.at[dev], pp_s.at[dev], 6, peer8(i))

            landed(kv3.at[pl.ds(0, 3 * 64)], recv_sem.at[3])

            @pl.loop(1, 4)
            def _(i):
                push(kv3.at[at3_y], kv3.at[at3_y], 4, peer_x(i))

        @pl.when(u == EMBED_AT)
        def _():
            ld_in.wait()
            landed(pp_s.at[pl.ds(0, 7)], recv_sem.at[6])
            pooled = x_sum_s[...] * (1.0 / TP) + jnp.sum(pp_s[...], axis=0)
            normed = norm(pooled, tgain[2:3, :]).astype(BF16)
            em[grp] = dot(normed, w_in_s[...]).astype(BF16).astype(F32)

            @pl.loop(1, 16)
            def _(i):
                push(em.at[grp], em.at[grp], 7, peer_grp(i))

            landed(kv2.at[pl.ds(0, 3 * 256)], recv_sem.at[12])
            push(kv2.at[half3], kv2.at[half3], 9, (sibling, dev))

    landed(kv3.at[pl.ds(0, 3 * 256)], recv_sem.at[4])
    push(kv3.at[half3], kv3.at[half3], 8, (sibling, dev))
    landed(em.at[pl.ds(0, 15)], recv_sem.at[7])
    tile = lax.broadcasted_iota(jnp.int32, (48, 128), 0)
    slot = lax.broadcasted_iota(jnp.int32, (48, 128), 1)
    gather = jnp.where(slot == tile // 3 * 8 + tile % 3, 1.0, 0.0).astype(BF16)
    fresh = dot(gather, em[...].reshape(128, SW).astype(BF16))
    fresh = norm(fresh, sgain[...].reshape(1, SW)).astype(BF16)
    for p in range(4):
        new_out[:, p * SW : (p + 1) * SW] = dot(fresh, w_slide_s[p])

    own1.wait()
    landed(kv1.at[pl.ds(0, 6 * 256)], recv_sem.at[14])
    landed(kv3.at[half3], recv_sem.at[8])
    landed(kv2.at[half3], recv_sem.at[9])
    out0.wait()
    out1.wait()

    landed(patches_s.at[pl.ds(0, 672)], send_sem.at[0])
    landed(wto_s.at[pl.ds(0, 672), quarter], send_sem.at[1])
    landed(wto_s.at[pl.ds(0, 672), pl.ds(0, 1152)], send_sem.at[10])
    landed(kv3.at[pl.ds(0, 3 * 16)], send_sem.at[2])
    landed(kv3.at[pl.ds(0, 3 * 64)], send_sem.at[3])
    landed(kv3.at[pl.ds(0, 3 * 256)], send_sem.at[4])
    landed(kv2.at[pl.ds(0, 3 * 64)], send_sem.at[11])
    landed(kv2.at[pl.ds(0, 3 * 256)], send_sem.at[12])
    landed(kv1.at[at1_y], send_sem.at[13])
    landed(kv1.at[pl.ds(0, 6 * 256)], send_sem.at[14])
    landed(wto_s.at[pl.ds(0, 672)], send_sem.at[5])
    landed(pp_s.at[pl.ds(0, 7)], send_sem.at[6])
    landed(em.at[pl.ds(0, 15)], send_sem.at[7])
    landed(kv3.at[half3], send_sem.at[8])
    landed(kv2.at[half3], send_sem.at[9])

    @pl.loop(0, 3)
    def _(t):
        landed(att_s.at[t, pl.ds(0, 7 * HB)], att_send.at[t])


def run_encoder(*args):
    hbm = pl.BlockSpec(memory_space=pl.ANY)
    vmem = pl.BlockSpec(memory_space=pltpu.VMEM)
    shape = jax.ShapeDtypeStruct
    return pl.pallas_call(
        encoder_kernel,
        out_shape=(
            shape((ROWS, 512), BF16),
            shape((256, ROWS), BF16),
            shape((GW, ROWS), BF16),
            shape((8, 8, ROWS), F32),
            shape((256, 384), BF16),
            shape((64, 384), BF16),
            shape((16, 384), BF16),
            shape((2048, 384), BF16),
            shape((2048, 384), BF16),
            shape((2048, 384), BF16),
            shape((16, 8, SW), F32),
            shape((48, 4 * SW), F32),
        ),
        in_specs=[hbm] * 9 + [vmem] * 2 + [pl.BlockSpec(memory_space=pltpu.SMEM)] * 2,
        out_specs=(hbm, hbm, vmem, vmem, vmem, vmem, vmem, hbm, hbm, hbm, vmem, vmem),
        scratch_shapes=[
            pltpu.VMEM((768, 588), BF16),
            pltpu.VMEM((588, TW), BF16),
            pltpu.VMEM((3, HB, TW), BF16),
            pltpu.VMEM((TW, TW), BF16),
            pltpu.VMEM((2, TW, FB), BF16),
            pltpu.VMEM((FB, TW), BF16),
            pltpu.VMEM((TW, SW), BF16),
            pltpu.VMEM((ROWS, SW), BF16),
            pltpu.VMEM((3, SW, SW), BF16),
            pltpu.VMEM((4, SW, SW), BF16),
            pltpu.VMEM((6, ROWS, 128), F32),
            pltpu.VMEM((ROWS, 512), BF16),
            pltpu.VMEM((256, ROWS), BF16),
            pltpu.VMEM((256, 384), BF16),
            pltpu.VMEM((64, 384), BF16),
            pltpu.VMEM((16, 384), BF16),
            pltpu.VMEM((768, TW), BF16),
            pltpu.VMEM((3, TW, TP), BF16),
            pltpu.VMEM((8, 8, TW), F32),
            pltpu.VMEM((1, 256), F32),
            pltpu.VMEM((8, TW), F32),
            pltpu.SemaphoreType.DMA((7,)),
            pltpu.SemaphoreType.DMA((2,)),
            pltpu.SemaphoreType.DMA((5,)),
            pltpu.SemaphoreType.DMA((15,)),
            pltpu.SemaphoreType.DMA((15,)),
            pltpu.SemaphoreType.DMA((3,)),
            pltpu.SemaphoreType.DMA((3,)),
        ],
        compiler_params=pltpu.CompilerParams(
            collective_id=0, has_side_effects=True, vmem_limit_bytes=60 * 1024 * 1024
        ),
        name="encode",
    )(*args)


def slide_kernel(
    positions,
    pattern,
    qk0,
    vt0,
    near,
    stats,
    q1,
    q2,
    q3,
    kv1,
    kv2,
    kv3,
    tokens,
    new,
    em,
    w_so,
    out,
    embed_out,
    qk0_s,
    vt0_s,
    near_s,
    stats_s,
    q1_s,
    q2_s,
    q3_s,
    kv1_s,
    kv2_s,
    kv3_s,
    tok_s,
    far_s,
    wso_s,
    sem,
):
    step = pl.program_id(0)
    place = lax.axis_index("grp") * 8 + lax.axis_index("dev")

    def weights(p):
        group = sum(jnp.where(pattern[g] == p, g, 0) for g in range(4))
        return w_so[pl.ds(pl.multiple_of(group * GW, 64), GW), :]

    @pl.when(step == 0)
    def _():
        copies = [
            pltpu.make_async_copy(src, dst, sem.at[at])
            for at, (src, dst) in enumerate(
                (
                    (q1, q1_s),
                    (q2, q2_s),
                    (q3, q3_s),
                    (kv1, kv1_s),
                    (kv2, kv2_s),
                    (kv3, kv3_s),
                    (tokens, tok_s),
                    (near, near_s),
                    (qk0, qk0_s),
                    (vt0, vt0_s),
                    (stats, stats_s),
                )
            )
        ]
        for copy in copies:
            copy.start()
        for p in range(4):
            wso_s[p * 256 : p * 256 + GW, :] = weights(p)
            wso_s[p * 256 + GW : (p + 1) * 256, :] = jnp.zeros((64, SW), BF16)
        embed_out[...] = em[pl.ds(pl.multiple_of((place // 8) * 8, 8), 8), :][0:3].astype(BF16)
        far_s[...] = jnp.zeros_like(far_s)
        for copy in copies:
            copy.wait()

        def put(ref, row, vector, columns=None):
            base = pl.multiple_of((row // 16) * 16, 16)
            width = ref.shape[1]
            block = ref[pl.ds(base, 16), :].astype(F32)
            hit = lax.broadcasted_iota(jnp.int32, (16, width), 0) == row - base
            if columns is not None:
                hit = jnp.logical_and(hit, columns)
            ref[pl.ds(base, 16), :] = jnp.where(hit, vector, block).astype(BF16)

        head16 = head_of((16, 384))

        def insert(n, found):
            pos = positions[n]
            owner = jnp.right_shift(pos, 11)
            here = jnp.bitwise_and(pos, ROWS - 1)
            local = owner == place

            @pl.when(local)
            def _():
                put(tok_s, here, em[pl.ds((n // 3) * 8 + n % 3, 1), :])

            for p, q_s, kv_s in ((1, q1_s, kv1_s), (2, q2_s, kv2_s), (3, q3_s, kv3_s)):
                bits = (0, 3, 5, 7)[p]
                member = jnp.bitwise_and(pos, DIL[p] - 1)
                within = jnp.right_shift(owner, bits) == jnp.right_shift(place, bits)
                at = jnp.right_shift(here, bits)

                @pl.when(jnp.logical_and(member < 4, within))
                def _():
                    if p == 1:
                        slot = jnp.bitwise_and(owner, 7)
                    else:
                        grp = jnp.right_shift(owner, 3)
                        of_core = jnp.right_shift(grp, 1) * 8 + jnp.bitwise_and(owner, 7)
                        many = (0, 8, 16, 64)[p]
                        slot = jnp.bitwise_and(grp, 1) * many + jnp.bitwise_and(of_core, many - 1)
                    columns = head16 == member
                    put(
                        kv_s,
                        slot * (ROWS // DIL[p]) + at,
                        new[pl.ds(n, 1), p * SW : p * SW + 384],
                        columns,
                    )

                    @pl.when(local)
                    def _():
                        put(q_s, at, new[pl.ds(n, 1), p * SW + 384 : (p + 1) * SW], columns)

            return found + jnp.where(local, 1, 0)

        found = lax.fori_loop(0, 48, insert, jnp.int32(0))

        @pl.when(jnp.min(stats_s[4:8]) < 2.0**-60)
        def _():
            @pl.loop(0, 16)
            def _(u):
                j = u % 4
                at = pl.ds(pl.multiple_of(u // 4 * 512, 512), 512)
                q = qk0_s[at, 0:256]
                s = dot_nt(
                    qk0_s[:, 256:512], jnp.where(only_head(j, 512, True), q, jnp.zeros_like(q))
                )
                m = jnp.max(s, axis=0, keepdims=True)
                e = jnp.exp2((s - m) * SCALE).astype(BF16)
                o = dot(vt0_s[pl.ds(pl.multiple_of(j * 64, 64), 64), :], e)
                count = o[SH : SH + 1, :]
                rows = pl.ds(pl.multiple_of(j * SH, 16), SH)
                near_s[rows, at] = (o[:SH, :] / count).astype(BF16)
                stats_s[j, :, at] = jnp.broadcast_to(m, (8, 512))
                stats_s[4 + j, :, at] = jnp.broadcast_to(count, (8, 512))

        @pl.when(found > 0)
        def _():
            slots = lax.broadcasted_iota(jnp.int32, (48, 1), 0)
            places = lax.fori_loop(
                0,
                48,
                lambda n, held: jnp.where(slots == n, positions[n], held),
                jnp.full((48, 1), -1, jnp.int32),
            )
            hide = jnp.where(places // ROWS == place, 0.0, HIDE)
            lane = lax.broadcasted_iota(jnp.int32, (48, 256), 1)
            fresh_q = jnp.where(lane == GW, 1.0, new[:, 0:256]).astype(BF16)
            fresh_k = new[:, 256:512].astype(BF16)
            fresh_vt = with_ones(new[:, 512 : 512 + GW].T)

            made = []
            for j in range(4):
                q = jnp.where(only_head(j, 48, True), fresh_q, jnp.zeros_like(fresh_q))
                s_old = dot_nt(qk0_s[:, 256:512], q)
                s_new = dot_nt(fresh_k, q) + hide
                m = jnp.maximum(
                    jnp.max(s_old, axis=0, keepdims=True), jnp.max(s_new, axis=0, keepdims=True)
                )
                e_old = jnp.exp2((s_old - m) * SCALE).astype(BF16)
                e_new = jnp.exp2((s_new - m) * SCALE).astype(BF16)
                head_rows = slice(j * 64, (j + 1) * 64)
                o = dot(vt0_s[head_rows, :], e_old) + dot(fresh_vt[head_rows, :], e_new)
                made.append(o[:SH, :] / o[SH : SH + 1, :])
            made = jnp.concatenate(made, axis=0).astype(BF16)

            @pl.loop(0, 4)
            def _(b):
                at = pl.ds(pl.multiple_of(b * 512, 512), 512)
                q = qk0_s[at, 0:256]
                joined = []
                for j in range(4):
                    k = jnp.where(only_head(j, 48, False), fresh_k, jnp.zeros_like(fresh_k))
                    s = dot_nt(k, q) + hide
                    m_old = stats_s[j, 0:1, at]
                    m = jnp.maximum(m_old, jnp.max(s, axis=0, keepdims=True))
                    weight = stats_s[4 + j, 0:1, at] * jnp.exp2((m_old - m) * SCALE)
                    e = jnp.exp2((s - m) * SCALE).astype(BF16)
                    o = dot(fresh_vt[j * 64 : (j + 1) * 64, :], e)
                    held = near_s[j * SH : (j + 1) * SH, at].astype(F32)
                    joined.append((held * weight + o[:SH, :]) / (weight + o[SH : SH + 1, :]))
                row = lax.broadcasted_iota(jnp.int32, (48, 512), 1) + (place * ROWS + b * 512)
                hit = jnp.where(row == places, 1.0, 0.0)
                anew = dot(made, hit.astype(BF16))
                taken = jnp.max(hit, axis=0, keepdims=True) > 0.0
                near_s[:, at] = jnp.where(taken, anew, jnp.concatenate(joined, axis=0)).astype(
                    BF16
                )

        def far_heads(p, q_s, kv_s, heads):
            r = DIL[p]
            count = ROWS // r
            q = q_s[...]
            kv = kv_s[...]
            head = head_of((count, 384))
            stack = [jnp.where(head == j, q, jnp.zeros_like(q)) for j in heads]
            _, e, o = attend(jnp.concatenate(stack, axis=0), kv, kv)
            o = o[:, 0:256] / jnp.sum(e.astype(F32), axis=-1, keepdims=True)
            for at, j in enumerate(heads):
                mine = jnp.where(
                    only_head(j, count, False), o[at * count : (at + 1) * count, :], 0.0
                )
                for b in range(2):
                    far_s[2 * (p - 1) + b, pl.ds(j, count, stride=r), :] = mine[
                        :, b * 128 : (b + 1) * 128
                    ]

        for j in range(4):
            far_heads(1, q1_s, kv1_s, (j,))
        far_heads(2, q2_s, kv2_s, (0, 1, 2, 3))
        far_heads(3, q3_s, kv3_s, (0, 1, 2, 3))

    at = pl.ds(pl.multiple_of(step * 512, 512), 512)

    near_t = jnp.concatenate([near_s[:, at], jnp.zeros((64, 512), BF16)], axis=0).T
    far = jnp.concatenate([far_s[b, at, :] for b in range(6)], axis=1).astype(BF16)
    total = tok_s[at, :].astype(F32) + dot(jnp.concatenate([near_t, far], axis=1), wso_s[...])
    out[...] = total.astype(BF16)


def run_slide(*args):
    hbm = pl.BlockSpec(memory_space=pl.ANY)
    vmem = pl.BlockSpec(memory_space=pltpu.VMEM)
    return pl.pallas_call(
        slide_kernel,
        out_shape=(
            jax.ShapeDtypeStruct((ROWS, SW), BF16),
            jax.ShapeDtypeStruct((3, SW), BF16),
        ),
        grid_spec=pltpu.PrefetchScalarGridSpec(
            num_scalar_prefetch=2,
            grid=(4,),
            in_specs=[hbm] * 11 + [vmem] * 3,
            out_specs=(
                pl.BlockSpec((512, SW), lambda i, *_: (i, 0)),
                pl.BlockSpec((3, SW), lambda i, *_: (0, 0)),
            ),
            scratch_shapes=[
                pltpu.VMEM((ROWS, 512), BF16),
                pltpu.VMEM((256, ROWS), BF16),
                pltpu.VMEM((GW, ROWS), BF16),
                pltpu.VMEM((8, 8, ROWS), F32),
                pltpu.VMEM((256, 384), BF16),
                pltpu.VMEM((64, 384), BF16),
                pltpu.VMEM((16, 384), BF16),
                pltpu.VMEM((2048, 384), BF16),
                pltpu.VMEM((2048, 384), BF16),
                pltpu.VMEM((2048, 384), BF16),
                pltpu.VMEM((ROWS, SW), BF16),
                pltpu.VMEM((6, ROWS, 128), F32),
                pltpu.VMEM((1024, SW), BF16),
                pltpu.SemaphoreType.DMA((11,)),
            ],
        ),
        compiler_params=pltpu.CompilerParams(vmem_limit_bytes=56 * 1024 * 1024),
        name="slide",
    )(*args)


def shards(
    tile_patches,
    w_patch,
    w_tqkv,
    w_to,
    w_gu,
    w_down,
    tile_gain,
    w_in,
    slide_tokens,
    slide_gain,
    w_sqkv,
    w_so,
    pattern_of_group,
    new_positions,
):
    qk0, vt0, near, stats, q1, q2, q3, kv1, kv2, kv3, em, new = run_encoder(
        tile_patches,
        w_patch,
        jnp.transpose(w_tqkv, (0, 2, 1)),
        w_to,
        w_gu,
        w_down,
        w_in,
        slide_tokens,
        w_sqkv,
        tile_gain,
        slide_gain,
        new_positions,
        pattern_of_group,
    )
    slide_out, tile_embed = run_slide(
        new_positions,
        pattern_of_group,
        qk0,
        vt0,
        near,
        stats,
        q1,
        q2,
        q3,
        kv1,
        kv2,
        kv3,
        slide_tokens,
        new,
        em.reshape(128, SW),
        w_so,
    )
    return (tile_embed, slide_out)


def solution(mesh):
    placed = (
        P(("grp", "dev"), None),
        P(),
        P(None, None, "dev"),
        P("dev", None),
        P(None, None, "dev"),
        P("dev", None),
        P(),
        P(),
        P(("grp", "dev"), None),
        P(),
        P(),
        P(),
        P(),
        P(),
    )
    return jax.shard_map(
        shards,
        mesh=mesh,
        in_specs=placed,
        out_specs=(P("grp", None), P(("grp", "dev"), None)),
        check_vma=False,
    )
```

```python
import functools

import jax
import jax.numpy as jnp
from jax import lax
from jax.experimental import pallas as pl
from jax.experimental.pallas import tpu as pltpu
from jax.sharding import PartitionSpec as P

MESH = pl.DeviceIdType.MESH
BF16 = jnp.bfloat16
F32 = jnp.float32

TW = 1536
TH = 64
TP = 256
HB = 192
FB = 512
SW = 768
GW = 192
SH = 48
ROWS = 2048
DIL = (1, 8, 32, 128)
LOG2E = 1.4426950408889634
HIDE = -1e30
KEYS_AT, HALF_AT, FEED_AT, EMBED_AT = 9, 8, 12, 14
SCALE = LOG2E * SH**-0.5


def dot(a, b):
    return jnp.dot(a, b, preferred_element_type=F32)


def dot_nt(a, b):
    return lax.dot_general(a, b, (((1,), (1,)), ((), ())), preferred_element_type=F32)


def norm(v, gain):
    center = v - jnp.mean(v, axis=-1, keepdims=True)
    spread = jnp.mean(center * center, axis=-1, keepdims=True)
    return center * lax.rsqrt(spread + 1e-06) * gain


def head_of(shape):
    return (lax.broadcasted_iota(jnp.int32, shape, 1) % GW) // SH


def attend(q, keys, values):
    s = dot_nt(q, keys)
    m = jnp.max(s, axis=-1, keepdims=True)
    e = jnp.exp2((s - m) * SCALE).astype(BF16)
    return m, e, dot(e, values)


def with_ones(vt):
    tail = lax.broadcasted_iota(jnp.int32, (16, vt.shape[1]), 0) == 0
    tail = jnp.where(tail, 1.0, 0.0)
    pieces = []
    for j in range(4):
        pieces += [vt[j * SH : (j + 1) * SH, :], tail]
    return jnp.concatenate(pieces, axis=0).astype(BF16)


def only_head(j, rows, bias=False, shift=False):
    lane = lax.broadcasted_iota(jnp.int32, (rows, 256), 1)
    mine = jnp.logical_and(lane >= j * SH, lane < (j + 1) * SH)
    if bias:
        mine = jnp.logical_or(mine, lane == GW)
    if shift:
        mine = jnp.logical_or(mine, lane == GW + 1 + j)
    return mine


def encoder_kernel(
    patches,
    w_patch,
    w_tqkv,
    w_to,
    w_gu,
    w_down,
    w_in,
    tokens,
    w_sqkv,
    tgain,
    sgain,
    positions,
    pattern,
    qk0_out,
    vt0_out,
    near,
    stats,
    q1_out,
    q2_out,
    q3_out,
    kv1,
    kv2,
    kv3,
    em,
    new_out,
    patches_s,
    w_patch_s,
    w_tqkv_s,
    wto_s,
    w_gu_s,
    w_down_s,
    w_in_s,
    tok_s,
    w_raw,
    w_slide_s,
    hs,
    qk0_s,
    vt0_s,
    kvc1,
    kvc2,
    kvc3,
    x0_s,
    att_s,
    pp_s,
    largest,
    x_sum_s,
    load_sem,
    out_sem,
    own_sem,
    send_sem,
    recv_sem,
    att_send,
    att_recv,
):
    grp = lax.axis_index("grp")
    dev = lax.axis_index("dev")
    core = grp % 2
    plane = grp // 4
    chip = (grp // 2) * 8 + dev
    local16 = (grp // 2) % 2 * 8 + dev
    sibling = (grp // 2) * 2 + (1 - core)

    z = dev % 4
    side = (grp // 2) % 2 * 2 + dev // 4

    def peer8(i):
        return (grp, (dev + i) % 8)

    def peer_z(i):
        return (grp, dev // 4 * 4 + (z + i) % 4)

    def peer_y(i):
        to = (side + i) % 4
        return (plane * 4 + to // 2 * 2 + core, to % 2 * 4 + z)

    def peer_x(i):
        return ((plane + i) % 4 * 4 + grp % 4, dev)

    def peer_grp(i):
        return ((grp + i) % 16, dev)

    def load(src, dst, at):
        copy = pltpu.make_async_copy(src, dst, load_sem.at[at])
        copy.start()
        return copy

    ld_tok = load(tokens, tok_s, 0)
    ld_raw = load(w_sqkv, w_raw, 1)
    ld_patch = load(w_patch, w_patch_s, 2)
    ld_tqkv = load(w_tqkv, w_tqkv_s, 3)
    ld_gu = load(w_gu, w_gu_s, 4)
    ld_down = load(w_down, w_down_s, 5)
    ld_in = load(w_in, w_in_s, 6)

    my_patch = pl.ds(pl.multiple_of(dev * 96, 32), 96)
    half_row = pl.multiple_of(core * 96, 32)
    my_half = pl.ds(pl.multiple_of(dev * HB + core * 96, 32), 96)
    quarter = pl.ds(pl.multiple_of(plane * 384, 128), 384)
    my_shard = pl.ds(pl.multiple_of(dev * HB, 64), HB)

    barrier = pltpu.get_barrier_semaphore()

    @pl.loop(1, 8)
    def _(i):
        pl.semaphore_signal(barrier, inc=1, device_id=peer8(i), device_id_type=MESH)

    @pl.loop(1, 16)
    def _(i):
        pl.semaphore_signal(barrier, inc=1, device_id=peer_grp(i), device_id_type=MESH)

    across = (plane * 4 + (1 - side // 2) * 2 + core, (dev + 4) % 8)
    pl.semaphore_signal(barrier, inc=1, device_id=across, device_id_type=MESH)
    pl.semaphore_wait(barrier, 23)

    own_patch = pltpu.make_async_copy(patches, patches_s.at[my_patch], own_sem.at[0])
    own_patch.start()
    own_wto = pltpu.make_async_copy(w_to, wto_s.at[my_shard], own_sem.at[1])
    own_wto.start()

    def push(src, dst, at, to):
        pltpu.make_async_remote_copy(
            src_ref=src,
            dst_ref=dst,
            send_sem=send_sem.at[at],
            recv_sem=recv_sem.at[at],
            device_id=to,
            device_id_type=MESH,
        ).start()

    def landed(ref, sem):
        pltpu.make_async_copy(ref, ref, sem).wait()

    @pl.loop(1, 8)
    def _(i):
        push(w_to.at[pl.ds(half_row, 96), quarter], wto_s.at[my_half, quarter], 1, peer8(i))

    @pl.loop(1, 8)
    def _(i):
        push(patches, patches_s.at[my_patch], 0, peer8(i))

    ld_raw.wait()
    group = [
        sum(jnp.where(pattern[g] == p, g, 0) for g in range(4)) for p in range(4)
    ]

    @pl.loop(0, 3)
    def _(c):
        at = pl.ds(pl.multiple_of(c * 256, 256), 256)

        def part(index, p):
            pair = jnp.where(group[p] >= 2, w_raw[index, at, 384:], w_raw[index, at, :384])
            return jnp.where(group[p] % 2 == 1, pair[:, GW:], pair[:, :GW])

        for index in range(3):
            w_slide_s[0, at, index * 256 : (index + 1) * 256] = jnp.concatenate(
                [part(index, 0), jnp.zeros((256, 64), BF16)], axis=1
            )
        for p in range(1, 4):
            w_slide_s[p, at, :384] = jnp.concatenate([part(2, p), part(1, p)], axis=1)
            w_slide_s[p, at, 384:] = jnp.concatenate(
                [jnp.zeros((256, GW), BF16), part(0, p)], axis=1
            )

    lane128 = lax.broadcasted_iota(jnp.int32, (1, 128), 1)
    places = lax.fori_loop(
        0,
        48,
        lambda n, held: jnp.where(lane128 == n, positions[n], held),
        jnp.full((1, 128), -1, jnp.int32),
    )
    ld_tok.wait()
    first = (grp * 8 + dev) * ROWS
    source = lax.broadcasted_iota(jnp.int32, (256, 256), 0)
    target = lax.broadcasted_iota(jnp.int32, (256, 256), 1)
    to_lane = jnp.logical_and(source < GW, target == GW + 1 + source // SH)
    to_lane = jnp.where(to_lane, 1.0, 0.0).astype(BF16)
    largest[...] = jnp.zeros_like(largest)

    @pl.loop(0, 8)
    def _(c):
        at = pl.ds(pl.multiple_of(c * 256, 256), 256)
        h = norm(tok_s[at, :].astype(F32), sgain[...].reshape(1, SW))
        for b in range(6):
            hs[b, at, :] = h[:, b * 128 : (b + 1) * 128]
        y = dot(h.astype(BF16), w_slide_s[0])
        row = lax.broadcasted_iota(jnp.int32, (256, 128), 0) + (first + c * 256)
        stale = jnp.max(jnp.where(row == places, 1.0, 0.0), axis=1, keepdims=True)
        column = lax.broadcasted_iota(jnp.int32, (256, 256), 1)
        q = y[:, 0:256].astype(BF16)
        k = y[:, 256:512].astype(BF16)
        q_size = jnp.sqrt(dot((q.astype(F32) * q.astype(F32)).astype(BF16), to_lane)) * 1.02
        k_size = dot((k.astype(F32) * k.astype(F32)).astype(BF16), to_lane)
        largest[...] = jnp.maximum(largest[...], jnp.max(k_size, axis=0, keepdims=True))
        q = jnp.where(column == GW, 1.0, q.astype(F32) - q_size)
        qk0_s[at, 0:256] = q.astype(BF16)
        qk0_s[at, 256:512] = jnp.where(column == GW, stale * HIDE, k.astype(F32)).astype(BF16)
        vt0_s[:, at] = with_ones(y[:, 512 : 512 + GW].T)

    own_wto.wait()
    landed(wto_s.at[pl.ds(0, 672), quarter], recv_sem.at[1])

    @pl.loop(1, 8)
    def _(i):
        half = pl.ds(pl.multiple_of(((dev + i) % 8) * HB + core * 96, 32), 96)

        @pl.loop(1, 4)
        def _(step):
            push(wto_s.at[half, quarter], wto_s.at[half, quarter], 10, peer_x(step))

    bound = (jnp.sqrt(largest[...]) * 1.02).astype(BF16)

    @pl.loop(0, 8)
    def _(c):
        at = pl.ds(pl.multiple_of(c * 256, 256), 256)
        k = qk0_s[at, 256:512]
        qk0_s[at, 256:512] = jnp.where(target > GW, bound.astype(F32), k.astype(F32)).astype(BF16)

    out0 = pltpu.make_async_copy(qk0_s, qk0_out, out_sem.at[0])
    out0.start()
    out1 = pltpu.make_async_copy(vt0_s, vt0_out, out_sem.at[1])
    out1.start()

    own_patch.wait()
    landed(patches_s.at[pl.ds(0, 672)], recv_sem.at[0])
    ld_patch.wait()
    ld_tqkv.wait()

    lanes = lax.broadcasted_iota(jnp.int32, (TP, HB), 1) // TH

    @pl.loop(0, 3)
    def _(t):
        at = pl.ds(pl.multiple_of(t * TP, TP), TP)
        x0 = dot(patches_s[at, :], w_patch_s[...]).astype(BF16)
        x0_s[at, :] = x0
        h1 = norm(x0.astype(F32), tgain[0:1, :]).astype(BF16)
        q = dot_nt(h1, w_tqkv_s[0]).astype(BF16)
        k = dot_nt(h1, w_tqkv_s[1]).astype(BF16)
        vt = dot_nt(w_tqkv_s[2], h1).astype(BF16)
        for h in range(3):
            s = dot_nt(jnp.where(lanes == h, q, jnp.zeros_like(q)), k) * (TH**-0.5)
            e = jnp.exp(s - jnp.max(s, axis=-1, keepdims=True))
            probs = (e / jnp.sum(e, axis=-1, keepdims=True)).astype(BF16)
            o = dot_nt(vt[h * TH : (h + 1) * TH, :], probs)
            rows = pl.ds(pl.multiple_of(dev * HB + h * TH, 64), TH)
            att_s[t, rows, :] = o.astype(BF16)

        @pl.loop(1, 8)
        def _(i):
            pltpu.make_async_remote_copy(
                src_ref=att_s.at[t, my_shard],
                dst_ref=att_s.at[t, my_shard],
                send_sem=att_send.at[t],
                recv_sem=att_recv.at[t],
                device_id=peer8(i),
                device_id_type=MESH,
            ).start()

    for p, kvc, q_out in ((1, kvc1, q1_out), (2, kvc2, q2_out), (3, kvc3, q3_out)):
        r = DIL[p]
        n = ROWS // r
        picked = jnp.concatenate(
            [
                jnp.concatenate([hs[b, pl.ds(j, n, stride=r), :] for b in range(6)], axis=1)
                for j in range(4)
            ],
            axis=0,
        ).astype(BF16)
        y = dot(picked, w_slide_s[p])
        head = head_of((n, SW))
        mine = jnp.zeros((n, SW), F32)
        for j in range(4):
            mine = jnp.where(head == j, y[j * n : (j + 1) * n, :], mine)
        kvc[...] = mine[:, :384].astype(BF16)
        q_out[...] = mine[:, 384:].astype(BF16)

    at1 = pl.ds(pl.multiple_of(dev * 256, 256), 256)
    at1_y = pl.ds(pl.multiple_of((dev + 4) % 8 * 256, 256), 256)
    at2 = pl.ds(pl.multiple_of((core * 16 + local16) * 64, 64), 64)
    at2_z = pl.ds(pl.multiple_of((core * 16 + local16 // 4 * 4) * 64, 256), 256)
    at3 = pl.ds(pl.multiple_of((core * 64 + chip) * 16, 16), 16)
    at3_z = pl.ds(pl.multiple_of((core * 64 + chip // 4 * 4) * 16, 64), 64)
    at3_y = pl.ds(pl.multiple_of((core * 64 + chip // 16 * 16) * 16, 256), 256)
    own1 = pltpu.make_async_copy(kvc1, kv1.at[at1], own_sem.at[2])
    own2 = pltpu.make_async_copy(kvc2, kv2.at[at2], own_sem.at[3])
    own3 = pltpu.make_async_copy(kvc3, kv3.at[at3], own_sem.at[4])
    own1.start()
    own2.start()
    own3.start()

    eight = lax.broadcasted_iota(jnp.int32, (8, 1), 0)
    half3 = pl.ds(pl.multiple_of(core * 1024, 1024), 1024)

    def feed(t, sums):
        x_sum, h_sum = sums
        at = pl.ds(pl.multiple_of(t * TP, TP), TP)
        landed(att_s.at[t, pl.ds(0, 7 * HB)], att_recv.at[t])
        att = att_s[t].T
        x1 = (x0_s[at, :].astype(F32) + dot(att, wto_s[...])).astype(BF16).astype(F32)
        h2 = norm(x1, tgain[1:2, :]).astype(BF16)
        gate = dot(h2, w_gu_s[0])
        up = dot(h2, w_gu_s[1])
        hidden = (jax.nn.silu(gate) * up).astype(BF16).astype(F32)
        x_sum = x_sum + jnp.where(eight == t, jnp.sum(x1, axis=0, keepdims=True), 0.0)
        h_sum = h_sum + jnp.where(eight == t, jnp.sum(hidden, axis=0, keepdims=True), 0.0)
        return x_sum, h_sum

    @pl.loop(0, 16)
    def _(u):
        j = u % 4
        at = pl.ds(pl.multiple_of(u // 4 * 512, 512), 512)
        q = qk0_s[at, 0:256]
        q = jnp.where(only_head(j, 512, True, True), q, jnp.zeros_like(q))
        e = jnp.exp2(dot_nt(qk0_s[:, 256:512], q) * SCALE).astype(BF16)
        o = dot(vt0_s[pl.ds(pl.multiple_of(j * 64, 64), 64), :], e)
        count = o[SH : SH + 1, :]
        near[pl.ds(pl.multiple_of(j * SH, 16), SH), at] = (o[:SH, :] / count).astype(BF16)
        lane = lax.broadcasted_iota(jnp.int32, (8, 256), 1)
        limit = jnp.where(lane == GW + 1 + j, -bound.astype(F32), 0.0).astype(BF16)
        stats[j, :, at] = dot_nt(limit, q)
        stats[4 + j, :, at] = jnp.broadcast_to(count, (8, 512))

        @pl.when(u == KEYS_AT)
        def _():
            push(kvc1, kv1.at[at1], 13, (grp, (dev + 4) % 8))

            @pl.loop(1, 4)
            def _(i):
                push(kvc3, kv3.at[at3], 2, peer_z(i))
                push(kvc2, kv2.at[at2], 11, peer_z(i))
                push(kvc1, kv1.at[at1], 14, peer_z(i))

        @pl.when(u == HALF_AT)
        def _():
            landed(wto_s.at[pl.ds(0, 672), pl.ds(0, 1152)], recv_sem.at[10])

            @pl.loop(1, 8)
            def _(i):
                half = pl.ds(pl.multiple_of(((dev + i) % 8) * HB + core * 96, 32), 96)
                push(wto_s.at[half], wto_s.at[half], 5, (sibling, dev))

        @pl.when(u == FEED_AT)
        def _():
            own3.wait()
            landed(kv3.at[pl.ds(0, 3 * 16)], recv_sem.at[2])
            own2.wait()
            landed(kv2.at[pl.ds(0, 3 * 64)], recv_sem.at[11])
            landed(kv1.at[at1_y], recv_sem.at[13])

            @pl.loop(1, 4)
            def _(i):
                push(kv3.at[at3_z], kv3.at[at3_z], 3, peer_y(i))
                push(kv2.at[at2_z], kv2.at[at2_z], 12, peer_y(i))
                push(kv1.at[at1_y], kv1.at[at1_y], 14, peer_z(i))

            landed(wto_s.at[pl.ds(0, 672)], recv_sem.at[5])
            ld_gu.wait()
            x_sum, h_sum = lax.fori_loop(
                0, 3, feed, (jnp.zeros((8, TW), F32), jnp.zeros((8, FB), F32))
            )
            x_sum_s[...] = x_sum
            ld_down.wait()
            h_mean = h_sum * (1.0 / TP)
            coarse = h_mean.astype(BF16)
            fine = (h_mean - coarse.astype(F32)).astype(BF16)
            both = jnp.concatenate([coarse.astype(F32), fine.astype(F32)], axis=0).astype(BF16)
            part = dot(both, w_down_s[...])
            pp_s[dev] = part[0:8] + part[8:16]

            @pl.loop(1, 8)
            def _(i):
                push(pp_s.at[dev], pp_s.at[dev], 6, peer8(i))

            landed(kv3.at[pl.ds(0, 3 * 64)], recv_sem.at[3])

            @pl.loop(1, 4)
            def _(i):
                push(kv3.at[at3_y], kv3.at[at3_y], 4, peer_x(i))

        @pl.when(u == EMBED_AT)
        def _():
            ld_in.wait()
            landed(pp_s.at[pl.ds(0, 7)], recv_sem.at[6])
            pooled = x_sum_s[...] * (1.0 / TP) + jnp.sum(pp_s[...], axis=0)
            normed = norm(pooled, tgain[2:3, :]).astype(BF16)
            em[grp] = dot(normed, w_in_s[...]).astype(BF16).astype(F32)

            @pl.loop(1, 16)
            def _(i):
                push(em.at[grp], em.at[grp], 7, peer_grp(i))

            landed(kv2.at[pl.ds(0, 3 * 256)], recv_sem.at[12])
            push(kv2.at[half3], kv2.at[half3], 9, (sibling, dev))

    landed(kv3.at[pl.ds(0, 3 * 256)], recv_sem.at[4])
    push(kv3.at[half3], kv3.at[half3], 8, (sibling, dev))
    landed(em.at[pl.ds(0, 15)], recv_sem.at[7])
    tile = lax.broadcasted_iota(jnp.int32, (48, 128), 0)
    slot = lax.broadcasted_iota(jnp.int32, (48, 128), 1)
    gather = jnp.where(slot == tile // 3 * 8 + tile % 3, 1.0, 0.0).astype(BF16)
    fresh = dot(gather, em[...].reshape(128, SW).astype(BF16))
    fresh = norm(fresh, sgain[...].reshape(1, SW)).astype(BF16)
    for p in range(4):
        new_out[:, p * SW : (p + 1) * SW] = dot(fresh, w_slide_s[p])

    own1.wait()
    landed(kv1.at[pl.ds(0, 6 * 256)], recv_sem.at[14])
    landed(kv3.at[half3], recv_sem.at[8])
    landed(kv2.at[half3], recv_sem.at[9])
    out0.wait()
    out1.wait()

    landed(patches_s.at[pl.ds(0, 672)], send_sem.at[0])
    landed(wto_s.at[pl.ds(0, 672), quarter], send_sem.at[1])
    landed(wto_s.at[pl.ds(0, 672), pl.ds(0, 1152)], send_sem.at[10])
    landed(kv3.at[pl.ds(0, 3 * 16)], send_sem.at[2])
    landed(kv3.at[pl.ds(0, 3 * 64)], send_sem.at[3])
    landed(kv3.at[pl.ds(0, 3 * 256)], send_sem.at[4])
    landed(kv2.at[pl.ds(0, 3 * 64)], send_sem.at[11])
    landed(kv2.at[pl.ds(0, 3 * 256)], send_sem.at[12])
    landed(kv1.at[at1_y], send_sem.at[13])
    landed(kv1.at[pl.ds(0, 6 * 256)], send_sem.at[14])
    landed(wto_s.at[pl.ds(0, 672)], send_sem.at[5])
    landed(pp_s.at[pl.ds(0, 7)], send_sem.at[6])
    landed(em.at[pl.ds(0, 15)], send_sem.at[7])
    landed(kv3.at[half3], send_sem.at[8])
    landed(kv2.at[half3], send_sem.at[9])

    @pl.loop(0, 3)
    def _(t):
        landed(att_s.at[t, pl.ds(0, 7 * HB)], att_send.at[t])


def run_encoder(*args):
    hbm = pl.BlockSpec(memory_space=pl.ANY)
    vmem = pl.BlockSpec(memory_space=pltpu.VMEM)
    shape = jax.ShapeDtypeStruct
    return pl.pallas_call(
        encoder_kernel,
        out_shape=(
            shape((ROWS, 512), BF16),
            shape((256, ROWS), BF16),
            shape((GW, ROWS), BF16),
            shape((8, 8, ROWS), F32),
            shape((256, 384), BF16),
            shape((64, 384), BF16),
            shape((16, 384), BF16),
            shape((2048, 384), BF16),
            shape((2048, 384), BF16),
            shape((2048, 384), BF16),
            shape((16, 8, SW), F32),
            shape((48, 4 * SW), F32),
        ),
        in_specs=[hbm] * 9 + [vmem] * 2 + [pl.BlockSpec(memory_space=pltpu.SMEM)] * 2,
        out_specs=(hbm, hbm, vmem, vmem, vmem, vmem, vmem, hbm, hbm, hbm, vmem, vmem),
        scratch_shapes=[
            pltpu.VMEM((768, 588), BF16),
            pltpu.VMEM((588, TW), BF16),
            pltpu.VMEM((3, HB, TW), BF16),
            pltpu.VMEM((TW, TW), BF16),
            pltpu.VMEM((2, TW, FB), BF16),
            pltpu.VMEM((FB, TW), BF16),
            pltpu.VMEM((TW, SW), BF16),
            pltpu.VMEM((ROWS, SW), BF16),
            pltpu.VMEM((3, SW, SW), BF16),
            pltpu.VMEM((4, SW, SW), BF16),
            pltpu.VMEM((6, ROWS, 128), F32),
            pltpu.VMEM((ROWS, 512), BF16),
            pltpu.VMEM((256, ROWS), BF16),
            pltpu.VMEM((256, 384), BF16),
            pltpu.VMEM((64, 384), BF16),
            pltpu.VMEM((16, 384), BF16),
            pltpu.VMEM((768, TW), BF16),
            pltpu.VMEM((3, TW, TP), BF16),
            pltpu.VMEM((8, 8, TW), F32),
            pltpu.VMEM((1, 256), F32),
            pltpu.VMEM((8, TW), F32),
            pltpu.SemaphoreType.DMA((7,)),
            pltpu.SemaphoreType.DMA((2,)),
            pltpu.SemaphoreType.DMA((5,)),
            pltpu.SemaphoreType.DMA((15,)),
            pltpu.SemaphoreType.DMA((15,)),
            pltpu.SemaphoreType.DMA((3,)),
            pltpu.SemaphoreType.DMA((3,)),
        ],
        compiler_params=pltpu.CompilerParams(
            collective_id=0, has_side_effects=True, vmem_limit_bytes=60 * 1024 * 1024
        ),
        name="encode",
    )(*args)


def slide_kernel(
    positions,
    pattern,
    qk0,
    vt0,
    near,
    stats,
    q1,
    q2,
    q3,
    kv1,
    kv2,
    kv3,
    tokens,
    new,
    em,
    w_so,
    out,
    embed_out,
    qk0_s,
    vt0_s,
    near_s,
    stats_s,
    q1_s,
    q2_s,
    q3_s,
    kv1_s,
    kv2_s,
    kv3_s,
    tok_s,
    far_s,
    wso_s,
    sem,
):
    step = pl.program_id(0)
    place = lax.axis_index("grp") * 8 + lax.axis_index("dev")

    def weights(p):
        group = sum(jnp.where(pattern[g] == p, g, 0) for g in range(4))
        return w_so[pl.ds(pl.multiple_of(group * GW, 64), GW), :]

    @pl.when(step == 0)
    def _():
        copies = [
            pltpu.make_async_copy(src, dst, sem.at[at])
            for at, (src, dst) in enumerate(
                (
                    (q1, q1_s),
                    (q2, q2_s),
                    (q3, q3_s),
                    (kv1, kv1_s),
                    (kv2, kv2_s),
                    (kv3, kv3_s),
                    (tokens, tok_s),
                    (near, near_s),
                    (qk0, qk0_s),
                    (vt0, vt0_s),
                    (stats, stats_s),
                )
            )
        ]
        for copy in copies:
            copy.start()
        for p in range(4):
            wso_s[p * 256 : p * 256 + GW, :] = weights(p)
            wso_s[p * 256 + GW : (p + 1) * 256, :] = jnp.zeros((64, SW), BF16)
        embed_out[...] = em[pl.ds(pl.multiple_of((place // 8) * 8, 8), 8), :][0:3].astype(BF16)
        far_s[...] = jnp.zeros_like(far_s)
        for copy in copies[:7]:
            copy.wait()

        def put(ref, row, vector, columns=None):
            base = pl.multiple_of((row // 16) * 16, 16)
            width = ref.shape[1]
            block = ref[pl.ds(base, 16), :].astype(F32)
            hit = lax.broadcasted_iota(jnp.int32, (16, width), 0) == row - base
            if columns is not None:
                hit = jnp.logical_and(hit, columns)
            ref[pl.ds(base, 16), :] = jnp.where(hit, vector, block).astype(BF16)

        head16 = head_of((16, 384))

        def insert(n, found):
            pos = positions[n]
            owner = jnp.right_shift(pos, 11)
            here = jnp.bitwise_and(pos, ROWS - 1)
            local = owner == place

            @pl.when(local)
            def _():
                put(tok_s, here, em[pl.ds((n // 3) * 8 + n % 3, 1), :])

            for p, q_s, kv_s in ((1, q1_s, kv1_s), (2, q2_s, kv2_s), (3, q3_s, kv3_s)):
                bits = (0, 3, 5, 7)[p]
                member = jnp.bitwise_and(pos, DIL[p] - 1)
                within = jnp.right_shift(owner, bits) == jnp.right_shift(place, bits)
                at = jnp.right_shift(here, bits)

                @pl.when(jnp.logical_and(member < 4, within))
                def _():
                    if p == 1:
                        slot = jnp.bitwise_and(owner, 7)
                    else:
                        grp = jnp.right_shift(owner, 3)
                        of_core = jnp.right_shift(grp, 1) * 8 + jnp.bitwise_and(owner, 7)
                        many = (0, 8, 16, 64)[p]
                        slot = jnp.bitwise_and(grp, 1) * many + jnp.bitwise_and(of_core, many - 1)
                    columns = head16 == member
                    put(
                        kv_s,
                        slot * (ROWS // DIL[p]) + at,
                        new[pl.ds(n, 1), p * SW : p * SW + 384],
                        columns,
                    )

                    @pl.when(local)
                    def _():
                        put(q_s, at, new[pl.ds(n, 1), p * SW + 384 : (p + 1) * SW], columns)

            return found + jnp.where(local, 1, 0)

        found = lax.fori_loop(0, 48, insert, jnp.int32(0))

        for copy in copies[7:]:
            copy.wait()

        @pl.when(jnp.min(stats_s[4:8]) < 2.0**-60)
        def _():
            @pl.loop(0, 16)
            def _(u):
                j = u % 4
                at = pl.ds(pl.multiple_of(u // 4 * 512, 512), 512)
                q = qk0_s[at, 0:256]
                s = dot_nt(
                    qk0_s[:, 256:512], jnp.where(only_head(j, 512, True), q, jnp.zeros_like(q))
                )
                m = jnp.max(s, axis=0, keepdims=True)
                e = jnp.exp2((s - m) * SCALE).astype(BF16)
                o = dot(vt0_s[pl.ds(pl.multiple_of(j * 64, 64), 64), :], e)
                count = o[SH : SH + 1, :]
                rows = pl.ds(pl.multiple_of(j * SH, 16), SH)
                near_s[rows, at] = (o[:SH, :] / count).astype(BF16)
                stats_s[j, :, at] = jnp.broadcast_to(m, (8, 512))
                stats_s[4 + j, :, at] = jnp.broadcast_to(count, (8, 512))

        @pl.when(found > 0)
        def _():
            slots = lax.broadcasted_iota(jnp.int32, (48, 1), 0)
            lanes = lax.broadcasted_iota(jnp.int32, (1, 48), 1)
            nowhere = (jnp.full((48, 1), -1, jnp.int32), jnp.full((1, 48), -1, jnp.int32))
            places, across = lax.fori_loop(
                0,
                48,
                lambda n, held: (
                    jnp.where(slots == n, positions[n], held[0]),
                    jnp.where(lanes == n, positions[n], held[1]),
                ),
                nowhere,
            )
            hide = jnp.where(jnp.right_shift(places, 11) == place, 0.0, HIDE)
            hide = jnp.concatenate([hide] * 4, axis=0)
            hide_across = jnp.where(jnp.right_shift(across, 11) == place, 0.0, HIDE)
            lane = lax.broadcasted_iota(jnp.int32, (48, 256), 1)
            fresh_q = jnp.where(lane == GW, 1.0, new[:, 0:256]).astype(BF16)
            fresh_k = new[:, 256:512].astype(BF16)
            fresh_vt = with_ones(new[:, 512 : 512 + GW].T)

            def stacked(rows, bias):
                return jnp.concatenate(
                    [
                        jnp.where(only_head(j, 48, bias), rows, jnp.zeros_like(rows))
                        for j in range(4)
                    ],
                    axis=0,
                )

            q = stacked(fresh_q, True)
            s_old = dot_nt(q, qk0_s[:, 256:512])
            s_new = dot_nt(q, fresh_k) + hide_across
            m = jnp.maximum(
                jnp.max(s_old, axis=1, keepdims=True), jnp.max(s_new, axis=1, keepdims=True)
            )
            e_old = jnp.exp2((s_old - m) * SCALE).astype(BF16)
            e_new = jnp.exp2((s_new - m) * SCALE).astype(BF16)
            made = []
            for j in range(4):
                head_rows = slice(j * 64, (j + 1) * 64)
                of_head = slice(j * 48, (j + 1) * 48)
                o = dot_nt(vt0_s[head_rows, :], e_old[of_head]) + dot_nt(
                    fresh_vt[head_rows, :], e_new[of_head]
                )
                made.append(o[:SH, :] / o[SH : SH + 1, :])
            made = jnp.concatenate(made, axis=0).astype(BF16)
            k = stacked(fresh_k, False)

            @pl.loop(0, 4)
            def _(b):
                at = pl.ds(pl.multiple_of(b * 512, 512), 512)
                all_s = dot_nt(k, qk0_s[at, 0:256]) + hide
                joined = []
                for j in range(4):
                    s = all_s[j * 48 : (j + 1) * 48, :]
                    m_old = stats_s[j, 0:1, at]
                    m = jnp.maximum(m_old, jnp.max(s, axis=0, keepdims=True))
                    weight = stats_s[4 + j, 0:1, at] * jnp.exp2((m_old - m) * SCALE)
                    e = jnp.exp2((s - m) * SCALE).astype(BF16)
                    o = dot(fresh_vt[j * 64 : (j + 1) * 64, :], e)
                    held = near_s[j * SH : (j + 1) * SH, at].astype(F32)
                    joined.append((held * weight + o[:SH, :]) / (weight + o[SH : SH + 1, :]))
                row = lax.broadcasted_iota(jnp.int32, (48, 512), 1) + (place * ROWS + b * 512)
                hit = jnp.where(row == places, 1.0, 0.0)
                anew = dot(made, hit.astype(BF16))
                taken = jnp.max(hit, axis=0, keepdims=True) > 0.0
                near_s[:, at] = jnp.where(taken, anew, jnp.concatenate(joined, axis=0)).astype(
                    BF16
                )

        def far_heads(p, q_s, kv_s, heads):
            r = DIL[p]
            count = ROWS // r
            q = q_s[...]
            kv = kv_s[...]
            head = head_of((count, 384))
            stack = [jnp.where(head == j, q, jnp.zeros_like(q)) for j in heads]
            _, e, o = attend(jnp.concatenate(stack, axis=0), kv, kv)
            o = o[:, 0:256] / jnp.sum(e.astype(F32), axis=-1, keepdims=True)
            for at, j in enumerate(heads):
                mine = jnp.where(
                    only_head(j, count, False), o[at * count : (at + 1) * count, :], 0.0
                )
                for b in range(2):
                    far_s[2 * (p - 1) + b, pl.ds(j, count, stride=r), :] = mine[
                        :, b * 128 : (b + 1) * 128
                    ]

        for j in range(4):
            far_heads(1, q1_s, kv1_s, (j,))
        far_heads(2, q2_s, kv2_s, (0, 1, 2, 3))
        far_heads(3, q3_s, kv3_s, (0, 1, 2, 3))

    at = pl.ds(pl.multiple_of(step * 512, 512), 512)

    near_t = jnp.concatenate([near_s[:, at], jnp.zeros((64, 512), BF16)], axis=0).T
    far = jnp.concatenate([far_s[b, at, :] for b in range(6)], axis=1).astype(BF16)
    total = tok_s[at, :].astype(F32) + dot(jnp.concatenate([near_t, far], axis=1), wso_s[...])
    out[...] = total.astype(BF16)


def run_slide(*args):
    hbm = pl.BlockSpec(memory_space=pl.ANY)
    vmem = pl.BlockSpec(memory_space=pltpu.VMEM)
    return pl.pallas_call(
        slide_kernel,
        out_shape=(
            jax.ShapeDtypeStruct((ROWS, SW), BF16),
            jax.ShapeDtypeStruct((3, SW), BF16),
        ),
        grid_spec=pltpu.PrefetchScalarGridSpec(
            num_scalar_prefetch=2,
            grid=(4,),
            in_specs=[hbm] * 11 + [vmem] * 3,
            out_specs=(
                pl.BlockSpec((512, SW), lambda i, *_: (i, 0)),
                pl.BlockSpec((3, SW), lambda i, *_: (0, 0)),
            ),
            scratch_shapes=[
                pltpu.VMEM((ROWS, 512), BF16),
                pltpu.VMEM((256, ROWS), BF16),
                pltpu.VMEM((GW, ROWS), BF16),
                pltpu.VMEM((8, 8, ROWS), F32),
                pltpu.VMEM((256, 384), BF16),
                pltpu.VMEM((64, 384), BF16),
                pltpu.VMEM((16, 384), BF16),
                pltpu.VMEM((2048, 384), BF16),
                pltpu.VMEM((2048, 384), BF16),
                pltpu.VMEM((2048, 384), BF16),
                pltpu.VMEM((ROWS, SW), BF16),
                pltpu.VMEM((6, ROWS, 128), F32),
                pltpu.VMEM((1024, SW), BF16),
                pltpu.SemaphoreType.DMA((11,)),
            ],
        ),
        compiler_params=pltpu.CompilerParams(vmem_limit_bytes=56 * 1024 * 1024),
        name="slide",
    )(*args)


def shards(
    tile_patches,
    w_patch,
    w_tqkv,
    w_to,
    w_gu,
    w_down,
    tile_gain,
    w_in,
    slide_tokens,
    slide_gain,
    w_sqkv,
    w_so,
    pattern_of_group,
    new_positions,
):
    qk0, vt0, near, stats, q1, q2, q3, kv1, kv2, kv3, em, new = run_encoder(
        tile_patches,
        w_patch,
        jnp.transpose(w_tqkv, (0, 2, 1)),
        w_to,
        w_gu,
        w_down,
        w_in,
        slide_tokens,
        w_sqkv,
        tile_gain,
        slide_gain,
        new_positions,
        pattern_of_group,
    )
    slide_out, tile_embed = run_slide(
        new_positions,
        pattern_of_group,
        qk0,
        vt0,
        near,
        stats,
        q1,
        q2,
        q3,
        kv1,
        kv2,
        kv3,
        slide_tokens,
        new,
        em.reshape(128, SW),
        w_so,
    )
    return (tile_embed, slide_out)


def solution(mesh):
    placed = (
        P(("grp", "dev"), None),
        P(),
        P(None, None, "dev"),
        P("dev", None),
        P(None, None, "dev"),
        P("dev", None),
        P(),
        P(),
        P(("grp", "dev"), None),
        P(),
        P(),
        P(),
        P(),
        P(),
    )
    return jax.shard_map(
        shards,
        mesh=mesh,
        in_specs=placed,
        out_specs=(P("grp", None), P(("grp", "dev"), None)),
        check_vma=False,
    )
```

```python
import functools

import jax
import jax.numpy as jnp
from jax import lax
from jax.experimental import pallas as pl
from jax.experimental.pallas import tpu as pltpu
from jax.sharding import PartitionSpec as P

MESH = pl.DeviceIdType.MESH
BF16 = jnp.bfloat16
F32 = jnp.float32

TW = 1536
TH = 64
TP = 256
HB = 192
FB = 512
SW = 768
GW = 192
SH = 48
ROWS = 2048
DIL = (1, 8, 32, 128)
LOG2E = 1.4426950408889634
HIDE = -1e30
KEYS_AT, HALF_AT, FEED_AT, EMBED_AT = 3, 11, 12, 14
SCALE = LOG2E * SH**-0.5


def dot(a, b):
    return jnp.dot(a, b, preferred_element_type=F32)


def dot_nt(a, b):
    return lax.dot_general(a, b, (((1,), (1,)), ((), ())), preferred_element_type=F32)


def norm(v, gain):
    center = v - jnp.mean(v, axis=-1, keepdims=True)
    spread = jnp.mean(center * center, axis=-1, keepdims=True)
    return center * lax.rsqrt(spread + 1e-06) * gain


def head_of(shape):
    return (lax.broadcasted_iota(jnp.int32, shape, 1) % GW) // SH


def attend(q, keys, values):
    s = dot_nt(q, keys)
    m = jnp.max(s, axis=-1, keepdims=True)
    e = jnp.exp2((s - m) * SCALE).astype(BF16)
    return m, e, dot(e, values)


def with_ones(vt):
    tail = lax.broadcasted_iota(jnp.int32, (16, vt.shape[1]), 0) == 0
    tail = jnp.where(tail, 1.0, 0.0)
    pieces = []
    for j in range(4):
        pieces += [vt[j * SH : (j + 1) * SH, :], tail]
    return jnp.concatenate(pieces, axis=0).astype(BF16)


def only_head(j, rows, bias=False, shift=False):
    lane = lax.broadcasted_iota(jnp.int32, (rows, 256), 1)
    mine = jnp.logical_and(lane >= j * SH, lane < (j + 1) * SH)
    if bias:
        mine = jnp.logical_or(mine, lane == GW)
    if shift:
        mine = jnp.logical_or(mine, lane == GW + 1 + j)
    return mine


def encoder_kernel(
    patches,
    w_patch,
    w_tqkv,
    w_to,
    w_gu,
    w_down,
    w_in,
    tokens,
    w_sqkv,
    tgain,
    sgain,
    positions,
    pattern,
    qk0_out,
    vt0_out,
    near,
    stats,
    q1_out,
    q2_out,
    q3_out,
    kv1,
    kv2,
    kv3,
    em,
    new_out,
    patches_s,
    w_patch_s,
    w_tqkv_s,
    wto_s,
    w_gu_s,
    w_down_s,
    w_in_s,
    tok_s,
    w_raw,
    w_slide_s,
    hs,
    qk0_s,
    vt0_s,
    kvc1,
    kvc2,
    kvc3,
    x0_s,
    att_s,
    pp_s,
    largest,
    x_sum_s,
    load_sem,
    out_sem,
    own_sem,
    send_sem,
    recv_sem,
    att_send,
    att_recv,
):
    grp = lax.axis_index("grp")
    dev = lax.axis_index("dev")
    core = grp % 2
    plane = grp // 4
    chip = (grp // 2) * 8 + dev
    local16 = (grp // 2) % 2 * 8 + dev
    sibling = (grp // 2) * 2 + (1 - core)

    z = dev % 4
    side = (grp // 2) % 2 * 2 + dev // 4

    def peer8(i):
        return (grp, (dev + i) % 8)

    def peer_z(i):
        return (grp, dev // 4 * 4 + (z + i) % 4)

    def peer_y(i):
        to = (side + i) % 4
        return (plane * 4 + to // 2 * 2 + core, to % 2 * 4 + z)

    def peer_x(i):
        return ((plane + i) % 4 * 4 + grp % 4, dev)

    def peer_grp(i):
        return ((grp + i) % 16, dev)

    def load(src, dst, at):
        copy = pltpu.make_async_copy(src, dst, load_sem.at[at])
        copy.start()
        return copy

    ld_tok = load(tokens, tok_s, 0)
    ld_raw = load(w_sqkv, w_raw, 1)
    ld_patch = load(w_patch, w_patch_s, 2)
    ld_tqkv = load(w_tqkv, w_tqkv_s, 3)
    ld_gu = load(w_gu, w_gu_s, 4)
    ld_down = load(w_down, w_down_s, 5)
    ld_in = load(w_in, w_in_s, 6)

    my_patch = pl.ds(pl.multiple_of(dev * 96, 32), 96)
    half_row = pl.multiple_of(core * 96, 32)
    my_half = pl.ds(pl.multiple_of(dev * HB + core * 96, 32), 96)
    quarter = pl.ds(pl.multiple_of(plane * 384, 128), 384)
    my_shard = pl.ds(pl.multiple_of(dev * HB, 64), HB)

    barrier = pltpu.get_barrier_semaphore()

    @pl.loop(1, 8)
    def _(i):
        pl.semaphore_signal(barrier, inc=1, device_id=peer8(i), device_id_type=MESH)

    @pl.loop(1, 16)
    def _(i):
        pl.semaphore_signal(barrier, inc=1, device_id=peer_grp(i), device_id_type=MESH)

    across = (plane * 4 + (1 - side // 2) * 2 + core, (dev + 4) % 8)
    pl.semaphore_signal(barrier, inc=1, device_id=across, device_id_type=MESH)
    pl.semaphore_wait(barrier, 23)

    own_patch = pltpu.make_async_copy(patches, patches_s.at[my_patch], own_sem.at[0])
    own_patch.start()
    own_wto = pltpu.make_async_copy(w_to, wto_s.at[my_shard], own_sem.at[1])
    own_wto.start()

    def push(src, dst, at, to):
        pltpu.make_async_remote_copy(
            src_ref=src,
            dst_ref=dst,
            send_sem=send_sem.at[at],
            recv_sem=recv_sem.at[at],
            device_id=to,
            device_id_type=MESH,
        ).start()

    def landed(ref, sem):
        pltpu.make_async_copy(ref, ref, sem).wait()

    @pl.loop(1, 8)
    def _(i):
        push(patches, patches_s.at[my_patch], 0, peer8(i))

    ld_raw.wait()
    group = [
        sum(jnp.where(pattern[g] == p, g, 0) for g in range(4)) for p in range(4)
    ]

    @pl.loop(0, 3)
    def _(c):
        at = pl.ds(pl.multiple_of(c * 256, 256), 256)

        def part(index, p):
            pair = jnp.where(group[p] >= 2, w_raw[index, at, 384:], w_raw[index, at, :384])
            return jnp.where(group[p] % 2 == 1, pair[:, GW:], pair[:, :GW])

        for index in range(3):
            w_slide_s[0, at, index * 256 : (index + 1) * 256] = jnp.concatenate(
                [part(index, 0), jnp.zeros((256, 64), BF16)], axis=1
            )
        for p in range(1, 4):
            w_slide_s[p, at, :384] = jnp.concatenate([part(2, p), part(1, p)], axis=1)
            w_slide_s[p, at, 384:] = jnp.concatenate(
                [jnp.zeros((256, GW), BF16), part(0, p)], axis=1
            )

    lane128 = lax.broadcasted_iota(jnp.int32, (1, 128), 1)
    places = lax.fori_loop(
        0,
        48,
        lambda n, held: jnp.where(lane128 == n, positions[n], held),
        jnp.full((1, 128), -1, jnp.int32),
    )
    ld_tok.wait()
    first = (grp * 8 + dev) * ROWS
    source = lax.broadcasted_iota(jnp.int32, (256, 256), 0)
    target = lax.broadcasted_iota(jnp.int32, (256, 256), 1)
    to_lane = jnp.logical_and(source < GW, target == GW + 1 + source // SH)
    to_lane = jnp.where(to_lane, 1.0, 0.0).astype(BF16)
    largest[...] = jnp.zeros_like(largest)

    @pl.loop(0, 8)
    def _(c):
        at = pl.ds(pl.multiple_of(c * 256, 256), 256)
        h = norm(tok_s[at, :].astype(F32), sgain[...].reshape(1, SW))
        for b in range(6):
            hs[b, at, :] = h[:, b * 128 : (b + 1) * 128]
        y = dot(h.astype(BF16), w_slide_s[0])
        row = lax.broadcasted_iota(jnp.int32, (256, 128), 0) + (first + c * 256)
        stale = jnp.max(jnp.where(row == places, 1.0, 0.0), axis=1, keepdims=True)
        column = lax.broadcasted_iota(jnp.int32, (256, 256), 1)
        q = y[:, 0:256].astype(BF16)
        k = y[:, 256:512].astype(BF16)
        q_size = jnp.sqrt(dot((q.astype(F32) * q.astype(F32)).astype(BF16), to_lane)) * 1.02
        k_size = dot((k.astype(F32) * k.astype(F32)).astype(BF16), to_lane)
        largest[...] = jnp.maximum(largest[...], jnp.max(k_size, axis=0, keepdims=True))
        q = jnp.where(column == GW, 1.0, q.astype(F32) - q_size)
        qk0_s[at, 0:256] = q.astype(BF16)
        qk0_s[at, 256:512] = jnp.where(column == GW, stale * HIDE, k.astype(F32)).astype(BF16)
        vt0_s[:, at] = with_ones(y[:, 512 : 512 + GW].T)

    bound = (jnp.sqrt(largest[...]) * 1.02).astype(BF16)

    @pl.loop(0, 8)
    def _(c):
        at = pl.ds(pl.multiple_of(c * 256, 256), 256)
        k = qk0_s[at, 256:512]
        qk0_s[at, 256:512] = jnp.where(target > GW, bound.astype(F32), k.astype(F32)).astype(BF16)

    out0 = pltpu.make_async_copy(qk0_s, qk0_out, out_sem.at[0])
    out0.start()
    out1 = pltpu.make_async_copy(vt0_s, vt0_out, out_sem.at[1])
    out1.start()

    own_patch.wait()
    landed(patches_s.at[pl.ds(0, 672)], recv_sem.at[0])
    @pl.loop(1, 8)
    def _(i):
        push(w_to.at[pl.ds(half_row, 96), quarter], wto_s.at[my_half, quarter], 1, peer8(i))

    ld_patch.wait()
    ld_tqkv.wait()

    lanes = lax.broadcasted_iota(jnp.int32, (TP, HB), 1) // TH

    @pl.loop(0, 3)
    def _(t):
        at = pl.ds(pl.multiple_of(t * TP, TP), TP)
        x0 = dot(patches_s[at, :], w_patch_s[...]).astype(BF16)
        x0_s[at, :] = x0
        h1 = norm(x0.astype(F32), tgain[0:1, :]).astype(BF16)
        q = dot_nt(h1, w_tqkv_s[0]).astype(BF16)
        k = dot_nt(h1, w_tqkv_s[1]).astype(BF16)
        vt = dot_nt(w_tqkv_s[2], h1).astype(BF16)
        for h in range(3):
            s = dot_nt(jnp.where(lanes == h, q, jnp.zeros_like(q)), k) * (TH**-0.5)
            e = jnp.exp(s - jnp.max(s, axis=-1, keepdims=True))
            probs = (e / jnp.sum(e, axis=-1, keepdims=True)).astype(BF16)
            o = dot_nt(vt[h * TH : (h + 1) * TH, :], probs)
            rows = pl.ds(pl.multiple_of(dev * HB + h * TH, 64), TH)
            att_s[t, rows, :] = o.astype(BF16)

        @pl.loop(1, 8)
        def _(i):
            pltpu.make_async_remote_copy(
                src_ref=att_s.at[t, my_shard],
                dst_ref=att_s.at[t, my_shard],
                send_sem=att_send.at[t],
                recv_sem=att_recv.at[t],
                device_id=peer8(i),
                device_id_type=MESH,
            ).start()

    own_wto.wait()
    landed(wto_s.at[pl.ds(0, 672), quarter], recv_sem.at[1])

    @pl.loop(1, 8)
    def _(i):
        half = pl.ds(pl.multiple_of(((dev + i) % 8) * HB + core * 96, 32), 96)

        @pl.loop(1, 4)
        def _(step):
            push(wto_s.at[half, quarter], wto_s.at[half, quarter], 10, peer_x(step))

    for p, kvc, q_out in ((1, kvc1, q1_out), (2, kvc2, q2_out), (3, kvc3, q3_out)):
        r = DIL[p]
        n = ROWS // r
        picked = jnp.concatenate(
            [
                jnp.concatenate([hs[b, pl.ds(j, n, stride=r), :] for b in range(6)], axis=1)
                for j in range(4)
            ],
            axis=0,
        ).astype(BF16)
        y = dot(picked, w_slide_s[p])
        head = head_of((n, SW))
        mine = jnp.zeros((n, SW), F32)
        for j in range(4):
            mine = jnp.where(head == j, y[j * n : (j + 1) * n, :], mine)
        kvc[...] = mine[:, :384].astype(BF16)
        q_out[...] = mine[:, 384:].astype(BF16)

    at1 = pl.ds(pl.multiple_of(dev * 256, 256), 256)
    at1_y = pl.ds(pl.multiple_of((dev + 4) % 8 * 256, 256), 256)
    at2 = pl.ds(pl.multiple_of((core * 16 + local16) * 64, 64), 64)
    at2_z = pl.ds(pl.multiple_of((core * 16 + local16 // 4 * 4) * 64, 256), 256)
    at3 = pl.ds(pl.multiple_of((core * 64 + chip) * 16, 16), 16)
    at3_z = pl.ds(pl.multiple_of((core * 64 + chip // 4 * 4) * 16, 64), 64)
    at3_y = pl.ds(pl.multiple_of((core * 64 + chip // 16 * 16) * 16, 256), 256)
    own1 = pltpu.make_async_copy(kvc1, kv1.at[at1], own_sem.at[2])
    own2 = pltpu.make_async_copy(kvc2, kv2.at[at2], own_sem.at[3])
    own3 = pltpu.make_async_copy(kvc3, kv3.at[at3], own_sem.at[4])
    own1.start()
    own2.start()
    own3.start()

    eight = lax.broadcasted_iota(jnp.int32, (8, 1), 0)
    half3 = pl.ds(pl.multiple_of(core * 1024, 1024), 1024)

    def feed(t, sums):
        x_sum, h_sum = sums
        at = pl.ds(pl.multiple_of(t * TP, TP), TP)
        landed(att_s.at[t, pl.ds(0, 7 * HB)], att_recv.at[t])
        att = att_s[t].T
        x1 = (x0_s[at, :].astype(F32) + dot(att, wto_s[...])).astype(BF16).astype(F32)
        h2 = norm(x1, tgain[1:2, :]).astype(BF16)
        gate = dot(h2, w_gu_s[0])
        up = dot(h2, w_gu_s[1])
        hidden = (jax.nn.silu(gate) * up).astype(BF16).astype(F32)
        x_sum = x_sum + jnp.where(eight == t, jnp.sum(x1, axis=0, keepdims=True), 0.0)
        h_sum = h_sum + jnp.where(eight == t, jnp.sum(hidden, axis=0, keepdims=True), 0.0)
        return x_sum, h_sum

    @pl.loop(0, 16)
    def _(u):
        j = u % 4
        at = pl.ds(pl.multiple_of(u // 4 * 512, 512), 512)
        q = qk0_s[at, 0:256]
        q = jnp.where(only_head(j, 512, True, True), q, jnp.zeros_like(q))
        e = jnp.exp2(dot_nt(qk0_s[:, 256:512], q) * SCALE).astype(BF16)
        o = dot(vt0_s[pl.ds(pl.multiple_of(j * 64, 64), 64), :], e)
        count = o[SH : SH + 1, :]
        near[pl.ds(pl.multiple_of(j * SH, 16), SH), at] = (o[:SH, :] / count).astype(BF16)
        lane = lax.broadcasted_iota(jnp.int32, (8, 256), 1)
        limit = jnp.where(lane == GW + 1 + j, -bound.astype(F32), 0.0).astype(BF16)
        stats[j, :, at] = dot_nt(limit, q)
        stats[4 + j, :, at] = jnp.broadcast_to(count, (8, 512))

        @pl.when(u == KEYS_AT)
        def _():
            push(kvc1, kv1.at[at1], 13, (grp, (dev + 4) % 8))

            @pl.loop(1, 4)
            def _(i):
                push(kvc3, kv3.at[at3], 2, peer_z(i))
                push(kvc2, kv2.at[at2], 11, peer_z(i))

        @pl.when(u == HALF_AT)
        def _():
            landed(wto_s.at[pl.ds(0, 672), pl.ds(0, 1152)], recv_sem.at[10])

            @pl.loop(1, 8)
            def _(i):
                half = pl.ds(pl.multiple_of(((dev + i) % 8) * HB + core * 96, 32), 96)
                push(wto_s.at[half], wto_s.at[half], 5, (sibling, dev))

        @pl.when(u == FEED_AT)
        def _():
            own3.wait()
            landed(kv3.at[pl.ds(0, 3 * 16)], recv_sem.at[2])
            own2.wait()
            landed(kv2.at[pl.ds(0, 3 * 64)], recv_sem.at[11])
            landed(kv1.at[at1_y], recv_sem.at[13])

            @pl.loop(1, 4)
            def _(i):
                push(kv3.at[at3_z], kv3.at[at3_z], 3, peer_y(i))
                push(kv2.at[at2_z], kv2.at[at2_z], 12, peer_y(i))
                push(kvc1, kv1.at[at1], 14, peer_z(i))
                push(kv1.at[at1_y], kv1.at[at1_y], 14, peer_z(i))

            landed(wto_s.at[pl.ds(0, 672)], recv_sem.at[5])
            ld_gu.wait()
            x_sum, h_sum = lax.fori_loop(
                0, 3, feed, (jnp.zeros((8, TW), F32), jnp.zeros((8, FB), F32))
            )
            x_sum_s[...] = x_sum
            ld_down.wait()
            h_mean = h_sum * (1.0 / TP)
            coarse = h_mean.astype(BF16)
            fine = (h_mean - coarse.astype(F32)).astype(BF16)
            both = jnp.concatenate([coarse.astype(F32), fine.astype(F32)], axis=0).astype(BF16)
            part = dot(both, w_down_s[...])
            pp_s[dev] = part[0:8] + part[8:16]

            @pl.loop(1, 8)
            def _(i):
                push(pp_s.at[dev], pp_s.at[dev], 6, peer8(i))

            landed(kv3.at[pl.ds(0, 3 * 64)], recv_sem.at[3])

            @pl.loop(1, 4)
            def _(i):
                push(kv3.at[at3_y], kv3.at[at3_y], 4, peer_x(i))

        @pl.when(u == EMBED_AT)
        def _():
            ld_in.wait()
            landed(pp_s.at[pl.ds(0, 7)], recv_sem.at[6])
            pooled = x_sum_s[...] * (1.0 / TP) + jnp.sum(pp_s[...], axis=0)
            normed = norm(pooled, tgain[2:3, :]).astype(BF16)
            em[grp] = dot(normed, w_in_s[...]).astype(BF16).astype(F32)

            @pl.loop(1, 16)
            def _(i):
                push(em.at[grp], em.at[grp], 7, peer_grp(i))

            landed(kv2.at[pl.ds(0, 3 * 256)], recv_sem.at[12])
            push(kv2.at[half3], kv2.at[half3], 9, (sibling, dev))

    landed(kv3.at[pl.ds(0, 3 * 256)], recv_sem.at[4])
    push(kv3.at[half3], kv3.at[half3], 8, (sibling, dev))
    landed(em.at[pl.ds(0, 15)], recv_sem.at[7])
    tile = lax.broadcasted_iota(jnp.int32, (48, 128), 0)
    slot = lax.broadcasted_iota(jnp.int32, (48, 128), 1)
    gather = jnp.where(slot == tile // 3 * 8 + tile % 3, 1.0, 0.0).astype(BF16)
    fresh = dot(gather, em[...].reshape(128, SW).astype(BF16))
    fresh = norm(fresh, sgain[...].reshape(1, SW)).astype(BF16)
    for p in range(4):
        new_out[:, p * SW : (p + 1) * SW] = dot(fresh, w_slide_s[p])

    own1.wait()
    landed(kv1.at[pl.ds(0, 6 * 256)], recv_sem.at[14])
    landed(kv3.at[half3], recv_sem.at[8])
    landed(kv2.at[half3], recv_sem.at[9])
    out0.wait()
    out1.wait()

    landed(patches_s.at[pl.ds(0, 672)], send_sem.at[0])
    landed(wto_s.at[pl.ds(0, 672), quarter], send_sem.at[1])
    landed(wto_s.at[pl.ds(0, 672), pl.ds(0, 1152)], send_sem.at[10])
    landed(kv3.at[pl.ds(0, 3 * 16)], send_sem.at[2])
    landed(kv3.at[pl.ds(0, 3 * 64)], send_sem.at[3])
    landed(kv3.at[pl.ds(0, 3 * 256)], send_sem.at[4])
    landed(kv2.at[pl.ds(0, 3 * 64)], send_sem.at[11])
    landed(kv2.at[pl.ds(0, 3 * 256)], send_sem.at[12])
    landed(kv1.at[at1_y], send_sem.at[13])
    landed(kv1.at[pl.ds(0, 6 * 256)], send_sem.at[14])
    landed(wto_s.at[pl.ds(0, 672)], send_sem.at[5])
    landed(pp_s.at[pl.ds(0, 7)], send_sem.at[6])
    landed(em.at[pl.ds(0, 15)], send_sem.at[7])
    landed(kv3.at[half3], send_sem.at[8])
    landed(kv2.at[half3], send_sem.at[9])

    @pl.loop(0, 3)
    def _(t):
        landed(att_s.at[t, pl.ds(0, 7 * HB)], att_send.at[t])


def run_encoder(*args):
    hbm = pl.BlockSpec(memory_space=pl.ANY)
    vmem = pl.BlockSpec(memory_space=pltpu.VMEM)
    shape = jax.ShapeDtypeStruct
    return pl.pallas_call(
        encoder_kernel,
        out_shape=(
            shape((ROWS, 512), BF16),
            shape((256, ROWS), BF16),
            shape((GW, ROWS), BF16),
            shape((8, 8, ROWS), F32),
            shape((256, 384), BF16),
            shape((64, 384), BF16),
            shape((16, 384), BF16),
            shape((2048, 384), BF16),
            shape((2048, 384), BF16),
            shape((2048, 384), BF16),
            shape((16, 8, SW), F32),
            shape((48, 4 * SW), F32),
        ),
        in_specs=[hbm] * 9 + [vmem] * 2 + [pl.BlockSpec(memory_space=pltpu.SMEM)] * 2,
        out_specs=(hbm, hbm, vmem, vmem, vmem, vmem, vmem, hbm, hbm, hbm, vmem, vmem),
        scratch_shapes=[
            pltpu.VMEM((768, 588), BF16),
            pltpu.VMEM((588, TW), BF16),
            pltpu.VMEM((3, HB, TW), BF16),
            pltpu.VMEM((TW, TW), BF16),
            pltpu.VMEM((2, TW, FB), BF16),
            pltpu.VMEM((FB, TW), BF16),
            pltpu.VMEM((TW, SW), BF16),
            pltpu.VMEM((ROWS, SW), BF16),
            pltpu.VMEM((3, SW, SW), BF16),
            pltpu.VMEM((4, SW, SW), BF16),
            pltpu.VMEM((6, ROWS, 128), F32),
            pltpu.VMEM((ROWS, 512), BF16),
            pltpu.VMEM((256, ROWS), BF16),
            pltpu.VMEM((256, 384), BF16),
            pltpu.VMEM((64, 384), BF16),
            pltpu.VMEM((16, 384), BF16),
            pltpu.VMEM((768, TW), BF16),
            pltpu.VMEM((3, TW, TP), BF16),
            pltpu.VMEM((8, 8, TW), F32),
            pltpu.VMEM((1, 256), F32),
            pltpu.VMEM((8, TW), F32),
            pltpu.SemaphoreType.DMA((7,)),
            pltpu.SemaphoreType.DMA((2,)),
            pltpu.SemaphoreType.DMA((5,)),
            pltpu.SemaphoreType.DMA((15,)),
            pltpu.SemaphoreType.DMA((15,)),
            pltpu.SemaphoreType.DMA((3,)),
            pltpu.SemaphoreType.DMA((3,)),
        ],
        compiler_params=pltpu.CompilerParams(
            collective_id=0, has_side_effects=True, vmem_limit_bytes=60 * 1024 * 1024
        ),
        name="encode",
    )(*args)


def slide_kernel(
    positions,
    pattern,
    qk0,
    vt0,
    near,
    stats,
    q1,
    q2,
    q3,
    kv1,
    kv2,
    kv3,
    tokens,
    new,
    em,
    w_so,
    out,
    embed_out,
    qk0_s,
    vt0_s,
    near_s,
    stats_s,
    q1_s,
    q2_s,
    q3_s,
    kv1_s,
    kv2_s,
    kv3_s,
    tok_s,
    far_s,
    wso_s,
    sem,
):
    step = pl.program_id(0)
    place = lax.axis_index("grp") * 8 + lax.axis_index("dev")

    def weights(p):
        group = sum(jnp.where(pattern[g] == p, g, 0) for g in range(4))
        return w_so[pl.ds(pl.multiple_of(group * GW, 64), GW), :]

    @pl.when(step == 0)
    def _():
        copies = [
            pltpu.make_async_copy(src, dst, sem.at[at])
            for at, (src, dst) in enumerate(
                (
                    (q1, q1_s),
                    (q2, q2_s),
                    (q3, q3_s),
                    (kv1, kv1_s),
                    (kv2, kv2_s),
                    (kv3, kv3_s),
                    (tokens, tok_s),
                    (near, near_s),
                    (qk0, qk0_s),
                    (vt0, vt0_s),
                    (stats, stats_s),
                )
            )
        ]
        for copy in copies:
            copy.start()
        for p in range(4):
            wso_s[p * 256 : p * 256 + GW, :] = weights(p)
            wso_s[p * 256 + GW : (p + 1) * 256, :] = jnp.zeros((64, SW), BF16)
        embed_out[...] = em[pl.ds(pl.multiple_of((place // 8) * 8, 8), 8), :][0:3].astype(BF16)
        far_s[...] = jnp.zeros_like(far_s)
        for copy in copies[:7]:
            copy.wait()

        def put(ref, row, vector, columns=None):
            base = pl.multiple_of((row // 16) * 16, 16)
            width = ref.shape[1]
            block = ref[pl.ds(base, 16), :].astype(F32)
            hit = lax.broadcasted_iota(jnp.int32, (16, width), 0) == row - base
            if columns is not None:
                hit = jnp.logical_and(hit, columns)
            ref[pl.ds(base, 16), :] = jnp.where(hit, vector, block).astype(BF16)

        head16 = head_of((16, 384))

        def insert(n, found):
            pos = positions[n]
            owner = jnp.right_shift(pos, 11)
            here = jnp.bitwise_and(pos, ROWS - 1)
            local = owner == place

            @pl.when(local)
            def _():
                put(tok_s, here, em[pl.ds((n // 3) * 8 + n % 3, 1), :])

            for p, q_s, kv_s in ((1, q1_s, kv1_s), (2, q2_s, kv2_s), (3, q3_s, kv3_s)):
                bits = (0, 3, 5, 7)[p]
                member = jnp.bitwise_and(pos, DIL[p] - 1)
                within = jnp.right_shift(owner, bits) == jnp.right_shift(place, bits)
                at = jnp.right_shift(here, bits)

                @pl.when(jnp.logical_and(member < 4, within))
                def _():
                    if p == 1:
                        slot = jnp.bitwise_and(owner, 7)
                    else:
                        grp = jnp.right_shift(owner, 3)
                        of_core = jnp.right_shift(grp, 1) * 8 + jnp.bitwise_and(owner, 7)
                        many = (0, 8, 16, 64)[p]
                        slot = jnp.bitwise_and(grp, 1) * many + jnp.bitwise_and(of_core, many - 1)
                    columns = head16 == member
                    put(
                        kv_s,
                        slot * (ROWS // DIL[p]) + at,
                        new[pl.ds(n, 1), p * SW : p * SW + 384],
                        columns,
                    )

                    @pl.when(local)
                    def _():
                        put(q_s, at, new[pl.ds(n, 1), p * SW + 384 : (p + 1) * SW], columns)

            return found + jnp.where(local, 1, 0)

        found = lax.fori_loop(0, 48, insert, jnp.int32(0))

        for copy in copies[7:]:
            copy.wait()

        @pl.when(jnp.min(stats_s[4:8]) < 2.0**-60)
        def _():
            @pl.loop(0, 16)
            def _(u):
                j = u % 4
                at = pl.ds(pl.multiple_of(u // 4 * 512, 512), 512)
                q = qk0_s[at, 0:256]
                s = dot_nt(
                    qk0_s[:, 256:512], jnp.where(only_head(j, 512, True), q, jnp.zeros_like(q))
                )
                m = jnp.max(s, axis=0, keepdims=True)
                e = jnp.exp2((s - m) * SCALE).astype(BF16)
                o = dot(vt0_s[pl.ds(pl.multiple_of(j * 64, 64), 64), :], e)
                count = o[SH : SH + 1, :]
                rows = pl.ds(pl.multiple_of(j * SH, 16), SH)
                near_s[rows, at] = (o[:SH, :] / count).astype(BF16)
                stats_s[j, :, at] = jnp.broadcast_to(m, (8, 512))
                stats_s[4 + j, :, at] = jnp.broadcast_to(count, (8, 512))

        @pl.when(found > 0)
        def _():
            slots = lax.broadcasted_iota(jnp.int32, (48, 1), 0)
            lanes = lax.broadcasted_iota(jnp.int32, (1, 48), 1)
            nowhere = (jnp.full((48, 1), -1, jnp.int32), jnp.full((1, 48), -1, jnp.int32))
            places, across = lax.fori_loop(
                0,
                48,
                lambda n, held: (
                    jnp.where(slots == n, positions[n], held[0]),
                    jnp.where(lanes == n, positions[n], held[1]),
                ),
                nowhere,
            )
            hide = jnp.where(jnp.right_shift(places, 11) == place, 0.0, HIDE)
            hide = jnp.concatenate([hide] * 4, axis=0)
            hide_across = jnp.where(jnp.right_shift(across, 11) == place, 0.0, HIDE)
            lane = lax.broadcasted_iota(jnp.int32, (48, 256), 1)
            fresh_q = jnp.where(lane == GW, 1.0, new[:, 0:256]).astype(BF16)
            fresh_k = new[:, 256:512].astype(BF16)
            fresh_vt = with_ones(new[:, 512 : 512 + GW].T)

            def stacked(rows, bias):
                return jnp.concatenate(
                    [
                        jnp.where(only_head(j, 48, bias), rows, jnp.zeros_like(rows))
                        for j in range(4)
                    ],
                    axis=0,
                )

            q = stacked(fresh_q, True)
            s_old = dot_nt(q, qk0_s[:, 256:512])
            s_new = dot_nt(q, fresh_k) + hide_across
            m = jnp.maximum(
                jnp.max(s_old, axis=1, keepdims=True), jnp.max(s_new, axis=1, keepdims=True)
            )
            e_old = jnp.exp2((s_old - m) * SCALE).astype(BF16)
            e_new = jnp.exp2((s_new - m) * SCALE).astype(BF16)
            made = []
            for j in range(4):
                head_rows = slice(j * 64, (j + 1) * 64)
                of_head = slice(j * 48, (j + 1) * 48)
                o = dot_nt(vt0_s[head_rows, :], e_old[of_head]) + dot_nt(
                    fresh_vt[head_rows, :], e_new[of_head]
                )
                made.append(o[:SH, :] / o[SH : SH + 1, :])
            made = jnp.concatenate(made, axis=0).astype(BF16)
            k = stacked(fresh_k, False)

            @pl.loop(0, 4)
            def _(b):
                at = pl.ds(pl.multiple_of(b * 512, 512), 512)
                all_s = dot_nt(k, qk0_s[at, 0:256]) + hide
                joined = []
                for j in range(4):
                    s = all_s[j * 48 : (j + 1) * 48, :]
                    m_old = stats_s[j, 0:1, at]
                    m = jnp.maximum(m_old, jnp.max(s, axis=0, keepdims=True))
                    weight = stats_s[4 + j, 0:1, at] * jnp.exp2((m_old - m) * SCALE)
                    e = jnp.exp2((s - m) * SCALE).astype(BF16)
                    o = dot(fresh_vt[j * 64 : (j + 1) * 64, :], e)
                    held = near_s[j * SH : (j + 1) * SH, at].astype(F32)
                    joined.append((held * weight + o[:SH, :]) / (weight + o[SH : SH + 1, :]))
                row = lax.broadcasted_iota(jnp.int32, (48, 512), 1) + (place * ROWS + b * 512)
                hit = jnp.where(row == places, 1.0, 0.0)
                anew = dot(made, hit.astype(BF16))
                taken = jnp.max(hit, axis=0, keepdims=True) > 0.0
                near_s[:, at] = jnp.where(taken, anew, jnp.concatenate(joined, axis=0)).astype(
                    BF16
                )

        def far_heads(p, q_s, kv_s, heads):
            r = DIL[p]
            count = ROWS // r
            q = q_s[...]
            kv = kv_s[...]
            head = head_of((count, 384))
            stack = [jnp.where(head == j, q, jnp.zeros_like(q)) for j in heads]
            _, e, o = attend(jnp.concatenate(stack, axis=0), kv, kv)
            o = o[:, 0:256] / jnp.sum(e.astype(F32), axis=-1, keepdims=True)
            for at, j in enumerate(heads):
                mine = jnp.where(
                    only_head(j, count, False), o[at * count : (at + 1) * count, :], 0.0
                )
                for b in range(2):
                    far_s[2 * (p - 1) + b, pl.ds(j, count, stride=r), :] = mine[
                        :, b * 128 : (b + 1) * 128
                    ]

        for j in range(4):
            far_heads(1, q1_s, kv1_s, (j,))
        far_heads(2, q2_s, kv2_s, (0, 1, 2, 3))
        far_heads(3, q3_s, kv3_s, (0, 1, 2, 3))

    at = pl.ds(pl.multiple_of(step * 512, 512), 512)

    near_t = jnp.concatenate([near_s[:, at], jnp.zeros((64, 512), BF16)], axis=0).T
    far = jnp.concatenate([far_s[b, at, :] for b in range(6)], axis=1).astype(BF16)
    total = tok_s[at, :].astype(F32) + dot(jnp.concatenate([near_t, far], axis=1), wso_s[...])
    out[...] = total.astype(BF16)


def run_slide(*args):
    hbm = pl.BlockSpec(memory_space=pl.ANY)
    vmem = pl.BlockSpec(memory_space=pltpu.VMEM)
    return pl.pallas_call(
        slide_kernel,
        out_shape=(
            jax.ShapeDtypeStruct((ROWS, SW), BF16),
            jax.ShapeDtypeStruct((3, SW), BF16),
        ),
        grid_spec=pltpu.PrefetchScalarGridSpec(
            num_scalar_prefetch=2,
            grid=(4,),
            in_specs=[hbm] * 11 + [vmem] * 3,
            out_specs=(
                pl.BlockSpec((512, SW), lambda i, *_: (i, 0)),
                pl.BlockSpec((3, SW), lambda i, *_: (0, 0)),
            ),
            scratch_shapes=[
                pltpu.VMEM((ROWS, 512), BF16),
                pltpu.VMEM((256, ROWS), BF16),
                pltpu.VMEM((GW, ROWS), BF16),
                pltpu.VMEM((8, 8, ROWS), F32),
                pltpu.VMEM((256, 384), BF16),
                pltpu.VMEM((64, 384), BF16),
                pltpu.VMEM((16, 384), BF16),
                pltpu.VMEM((2048, 384), BF16),
                pltpu.VMEM((2048, 384), BF16),
                pltpu.VMEM((2048, 384), BF16),
                pltpu.VMEM((ROWS, SW), BF16),
                pltpu.VMEM((6, ROWS, 128), F32),
                pltpu.VMEM((1024, SW), BF16),
                pltpu.SemaphoreType.DMA((11,)),
            ],
        ),
        compiler_params=pltpu.CompilerParams(vmem_limit_bytes=56 * 1024 * 1024),
        name="slide",
    )(*args)


def shards(
    tile_patches,
    w_patch,
    w_tqkv,
    w_to,
    w_gu,
    w_down,
    tile_gain,
    w_in,
    slide_tokens,
    slide_gain,
    w_sqkv,
    w_so,
    pattern_of_group,
    new_positions,
):
    qk0, vt0, near, stats, q1, q2, q3, kv1, kv2, kv3, em, new = run_encoder(
        tile_patches,
        w_patch,
        jnp.transpose(w_tqkv, (0, 2, 1)),
        w_to,
        w_gu,
        w_down,
        w_in,
        slide_tokens,
        w_sqkv,
        tile_gain,
        slide_gain,
        new_positions,
        pattern_of_group,
    )
    slide_out, tile_embed = run_slide(
        new_positions,
        pattern_of_group,
        qk0,
        vt0,
        near,
        stats,
        q1,
        q2,
        q3,
        kv1,
        kv2,
        kv3,
        slide_tokens,
        new,
        em.reshape(128, SW),
        w_so,
    )
    return (tile_embed, slide_out)


def solution(mesh):
    placed = (
        P(("grp", "dev"), None),
        P(),
        P(None, None, "dev"),
        P("dev", None),
        P(None, None, "dev"),
        P("dev", None),
        P(),
        P(),
        P(("grp", "dev"), None),
        P(),
        P(),
        P(),
        P(),
        P(),
    )
    return jax.shard_map(
        shards,
        mesh=mesh,
        in_specs=placed,
        out_specs=(P("grp", None), P(("grp", "dev"), None)),
        check_vma=False,
    )
```

```python
import functools

import jax
import jax.numpy as jnp
from jax import lax
from jax.experimental import pallas as pl
from jax.experimental.pallas import tpu as pltpu
from jax.sharding import PartitionSpec as P

MESH = pl.DeviceIdType.MESH
BF16 = jnp.bfloat16
F32 = jnp.float32

TW = 1536
TH = 64
TP = 256
HB = 192
FB = 512
SW = 768
GW = 192
SH = 48
ROWS = 2048
DIL = (1, 8, 32, 128)
LOG2E = 1.4426950408889634
HIDE = -1e30
KEYS_AT, HALF_AT, FEED_AT, EMBED_AT = 6, 10, 12, 14
SCALE = LOG2E * SH**-0.5


def dot(a, b):
    return jnp.dot(a, b, preferred_element_type=F32)


def dot_nt(a, b):
    return lax.dot_general(a, b, (((1,), (1,)), ((), ())), preferred_element_type=F32)


def norm(v, gain):
    center = v - jnp.mean(v, axis=-1, keepdims=True)
    spread = jnp.mean(center * center, axis=-1, keepdims=True)
    return center * lax.rsqrt(spread + 1e-06) * gain


def head_of(shape):
    return (lax.broadcasted_iota(jnp.int32, shape, 1) % GW) // SH


def attend(q, keys, values):
    s = dot_nt(q, keys)
    m = jnp.max(s, axis=-1, keepdims=True)
    e = jnp.exp2((s - m) * SCALE).astype(BF16)
    return m, e, dot(e, values)


def with_ones(vt):
    tail = lax.broadcasted_iota(jnp.int32, (16, vt.shape[1]), 0) == 0
    tail = jnp.where(tail, 1.0, 0.0)
    pieces = []
    for j in range(4):
        pieces += [vt[j * SH : (j + 1) * SH, :], tail]
    return jnp.concatenate(pieces, axis=0).astype(BF16)


def only_head(j, rows, bias=False, shift=False):
    lane = lax.broadcasted_iota(jnp.int32, (rows, 256), 1)
    mine = jnp.logical_and(lane >= j * SH, lane < (j + 1) * SH)
    if bias:
        mine = jnp.logical_or(mine, lane == GW)
    if shift:
        mine = jnp.logical_or(mine, lane == GW + 1 + j)
    return mine


def encoder_kernel(
    patches,
    w_patch,
    w_tqkv,
    w_to,
    w_gu,
    w_down,
    w_in,
    tokens,
    w_sqkv,
    tgain,
    sgain,
    positions,
    pattern,
    qk0_out,
    vt0_out,
    near,
    stats,
    q1_out,
    q2_out,
    q3_out,
    kv1,
    kv2,
    kv3,
    em,
    new_out,
    patches_s,
    w_patch_s,
    w_tqkv_s,
    wto_s,
    w_gu_s,
    w_down_s,
    w_in_s,
    tok_s,
    w_raw,
    w_slide_s,
    hs,
    qk0_s,
    vt0_s,
    kvc1,
    kvc2,
    kvc3,
    x0_s,
    att_s,
    pp_s,
    largest,
    x_sum_s,
    load_sem,
    out_sem,
    own_sem,
    send_sem,
    recv_sem,
    att_send,
    att_recv,
):
    grp = lax.axis_index("grp")
    dev = lax.axis_index("dev")
    core = grp % 2
    plane = grp // 4
    chip = (grp // 2) * 8 + dev
    local16 = (grp // 2) % 2 * 8 + dev
    sibling = (grp // 2) * 2 + (1 - core)

    z = dev % 4
    side = (grp // 2) % 2 * 2 + dev // 4

    def peer8(i):
        return (grp, (dev + i) % 8)

    def peer_z(i):
        return (grp, dev // 4 * 4 + (z + i) % 4)

    def peer_y(i):
        to = (side + i) % 4
        return (plane * 4 + to // 2 * 2 + core, to % 2 * 4 + z)

    def peer_x(i):
        return ((plane + i) % 4 * 4 + grp % 4, dev)

    def peer_grp(i):
        return ((grp + i) % 16, dev)

    def load(src, dst, at):
        copy = pltpu.make_async_copy(src, dst, load_sem.at[at])
        copy.start()
        return copy

    ld_tok = load(tokens, tok_s, 0)
    ld_raw = load(w_sqkv, w_raw, 1)
    ld_patch = load(w_patch, w_patch_s, 2)
    ld_tqkv = load(w_tqkv, w_tqkv_s, 3)
    ld_gu = load(w_gu, w_gu_s, 4)
    ld_down = load(w_down, w_down_s, 5)
    ld_in = load(w_in, w_in_s, 6)

    my_patch = pl.ds(pl.multiple_of(dev * 96, 32), 96)
    half_row = pl.multiple_of(core * 96, 32)
    my_half = pl.ds(pl.multiple_of(dev * HB + core * 96, 32), 96)
    quarter = pl.ds(pl.multiple_of(plane * 384, 128), 384)
    my_shard = pl.ds(pl.multiple_of(dev * HB, 64), HB)

    barrier = pltpu.get_barrier_semaphore()

    @pl.loop(1, 8)
    def _(i):
        pl.semaphore_signal(barrier, inc=1, device_id=peer8(i), device_id_type=MESH)

    @pl.loop(1, 16)
    def _(i):
        pl.semaphore_signal(barrier, inc=1, device_id=peer_grp(i), device_id_type=MESH)

    across = (plane * 4 + (1 - side // 2) * 2 + core, (dev + 4) % 8)
    pl.semaphore_signal(barrier, inc=1, device_id=across, device_id_type=MESH)
    pl.semaphore_wait(barrier, 23)

    own_patch = pltpu.make_async_copy(patches, patches_s.at[my_patch], own_sem.at[0])
    own_patch.start()
    own_wto = pltpu.make_async_copy(w_to, wto_s.at[my_shard], own_sem.at[1])
    own_wto.start()

    def push(src, dst, at, to):
        pltpu.make_async_remote_copy(
            src_ref=src,
            dst_ref=dst,
            send_sem=send_sem.at[at],
            recv_sem=recv_sem.at[at],
            device_id=to,
            device_id_type=MESH,
        ).start()

    def landed(ref, sem):
        pltpu.make_async_copy(ref, ref, sem).wait()

    @pl.loop(1, 8)
    def _(i):
        push(patches, patches_s.at[my_patch], 0, peer8(i))

    @pl.loop(1, 8)
    def _(i):
        push(w_to.at[pl.ds(half_row, 96), quarter], wto_s.at[my_half, quarter], 1, peer8(i))

    ld_raw.wait()
    group = [
        sum(jnp.where(pattern[g] == p, g, 0) for g in range(4)) for p in range(4)
    ]

    @pl.loop(0, 3)
    def _(c):
        at = pl.ds(pl.multiple_of(c * 256, 256), 256)

        def part(index, p):
            pair = jnp.where(group[p] >= 2, w_raw[index, at, 384:], w_raw[index, at, :384])
            return jnp.where(group[p] % 2 == 1, pair[:, GW:], pair[:, :GW])

        for index in range(3):
            w_slide_s[0, at, index * 256 : (index + 1) * 256] = jnp.concatenate(
                [part(index, 0), jnp.zeros((256, 64), BF16)], axis=1
            )
        for p in range(1, 4):
            w_slide_s[p, at, :384] = jnp.concatenate([part(2, p), part(1, p)], axis=1)
            w_slide_s[p, at, 384:] = jnp.concatenate(
                [jnp.zeros((256, GW), BF16), part(0, p)], axis=1
            )

    lane128 = lax.broadcasted_iota(jnp.int32, (1, 128), 1)
    places = lax.fori_loop(
        0,
        48,
        lambda n, held: jnp.where(lane128 == n, positions[n], held),
        jnp.full((1, 128), -1, jnp.int32),
    )
    ld_tok.wait()
    first = (grp * 8 + dev) * ROWS
    source = lax.broadcasted_iota(jnp.int32, (256, 256), 0)
    target = lax.broadcasted_iota(jnp.int32, (256, 256), 1)
    to_lane = jnp.logical_and(source < GW, target == GW + 1 + source // SH)
    to_lane = jnp.where(to_lane, 1.0, 0.0).astype(BF16)
    largest[...] = jnp.zeros_like(largest)

    @pl.loop(0, 8)
    def _(c):
        at = pl.ds(pl.multiple_of(c * 256, 256), 256)
        h = norm(tok_s[at, :].astype(F32), sgain[...].reshape(1, SW))
        for b in range(6):
            hs[b, at, :] = h[:, b * 128 : (b + 1) * 128]
        y = dot(h.astype(BF16), w_slide_s[0])
        row = lax.broadcasted_iota(jnp.int32, (256, 128), 0) + (first + c * 256)
        stale = jnp.max(jnp.where(row == places, 1.0, 0.0), axis=1, keepdims=True)
        column = lax.broadcasted_iota(jnp.int32, (256, 256), 1)
        q = y[:, 0:256].astype(BF16)
        k = y[:, 256:512].astype(BF16)
        q_size = jnp.sqrt(dot((q.astype(F32) * q.astype(F32)).astype(BF16), to_lane)) * 1.02
        k_size = dot((k.astype(F32) * k.astype(F32)).astype(BF16), to_lane)
        largest[...] = jnp.maximum(largest[...], jnp.max(k_size, axis=0, keepdims=True))
        q = jnp.where(column == GW, 1.0, q.astype(F32) - q_size)
        qk0_s[at, 0:256] = q.astype(BF16)
        qk0_s[at, 256:512] = jnp.where(column == GW, stale * HIDE, k.astype(F32)).astype(BF16)
        vt0_s[:, at] = with_ones(y[:, 512 : 512 + GW].T)

    bound = (jnp.sqrt(largest[...]) * 1.02).astype(BF16)

    @pl.loop(0, 8)
    def _(c):
        at = pl.ds(pl.multiple_of(c * 256, 256), 256)
        k = qk0_s[at, 256:512]
        qk0_s[at, 256:512] = jnp.where(target > GW, bound.astype(F32), k.astype(F32)).astype(BF16)

    out0 = pltpu.make_async_copy(qk0_s, qk0_out, out_sem.at[0])
    out0.start()
    out1 = pltpu.make_async_copy(vt0_s, vt0_out, out_sem.at[1])
    out1.start()

    own_patch.wait()
    landed(patches_s.at[pl.ds(0, 672)], recv_sem.at[0])
    ld_patch.wait()
    ld_tqkv.wait()

    lanes = lax.broadcasted_iota(jnp.int32, (TP, HB), 1) // TH

    @pl.loop(0, 3)
    def _(t):
        at = pl.ds(pl.multiple_of(t * TP, TP), TP)
        @pl.when(t == 1)
        def _():
            own_wto.wait()
            landed(wto_s.at[pl.ds(0, 672), quarter], recv_sem.at[1])

            @pl.loop(1, 8)
            def _(i):
                half = pl.ds(pl.multiple_of(((dev + i) % 8) * HB + core * 96, 32), 96)

                @pl.loop(1, 4)
                def _(step):
                    push(wto_s.at[half, quarter], wto_s.at[half, quarter], 10, peer_x(step))

        x0 = dot(patches_s[at, :], w_patch_s[...]).astype(BF16)
        x0_s[at, :] = x0
        h1 = norm(x0.astype(F32), tgain[0:1, :]).astype(BF16)
        q = dot_nt(h1, w_tqkv_s[0]).astype(BF16)
        k = dot_nt(h1, w_tqkv_s[1]).astype(BF16)
        vt = dot_nt(w_tqkv_s[2], h1).astype(BF16)
        for h in range(3):
            s = dot_nt(jnp.where(lanes == h, q, jnp.zeros_like(q)), k) * (TH**-0.5)
            e = jnp.exp(s - jnp.max(s, axis=-1, keepdims=True))
            probs = (e / jnp.sum(e, axis=-1, keepdims=True)).astype(BF16)
            o = dot_nt(vt[h * TH : (h + 1) * TH, :], probs)
            rows = pl.ds(pl.multiple_of(dev * HB + h * TH, 64), TH)
            att_s[t, rows, :] = o.astype(BF16)

        @pl.loop(1, 8)
        def _(i):
            pltpu.make_async_remote_copy(
                src_ref=att_s.at[t, my_shard],
                dst_ref=att_s.at[t, my_shard],
                send_sem=att_send.at[t],
                recv_sem=att_recv.at[t],
                device_id=peer8(i),
                device_id_type=MESH,
            ).start()

    for p, kvc, q_out in ((1, kvc1, q1_out), (2, kvc2, q2_out), (3, kvc3, q3_out)):
        r = DIL[p]
        n = ROWS // r
        picked = jnp.concatenate(
            [
                jnp.concatenate([hs[b, pl.ds(j, n, stride=r), :] for b in range(6)], axis=1)
                for j in range(4)
            ],
            axis=0,
        ).astype(BF16)
        y = dot(picked, w_slide_s[p])
        head = head_of((n, SW))
        mine = jnp.zeros((n, SW), F32)
        for j in range(4):
            mine = jnp.where(head == j, y[j * n : (j + 1) * n, :], mine)
        kvc[...] = mine[:, :384].astype(BF16)
        q_out[...] = mine[:, 384:].astype(BF16)

    at1 = pl.ds(pl.multiple_of(dev * 256, 256), 256)
    at1_y = pl.ds(pl.multiple_of((dev + 4) % 8 * 256, 256), 256)
    at2 = pl.ds(pl.multiple_of((core * 16 + local16) * 64, 64), 64)
    at2_z = pl.ds(pl.multiple_of((core * 16 + local16 // 4 * 4) * 64, 256), 256)
    at3 = pl.ds(pl.multiple_of((core * 64 + chip) * 16, 16), 16)
    at3_z = pl.ds(pl.multiple_of((core * 64 + chip // 4 * 4) * 16, 64), 64)
    at3_y = pl.ds(pl.multiple_of((core * 64 + chip // 16 * 16) * 16, 256), 256)
    own1 = pltpu.make_async_copy(kvc1, kv1.at[at1], own_sem.at[2])
    own2 = pltpu.make_async_copy(kvc2, kv2.at[at2], own_sem.at[3])
    own3 = pltpu.make_async_copy(kvc3, kv3.at[at3], own_sem.at[4])
    own1.start()
    own2.start()
    own3.start()

    eight = lax.broadcasted_iota(jnp.int32, (8, 1), 0)
    half3 = pl.ds(pl.multiple_of(core * 1024, 1024), 1024)

    def feed(t, sums):
        x_sum, h_sum = sums
        at = pl.ds(pl.multiple_of(t * TP, TP), TP)
        landed(att_s.at[t, pl.ds(0, 7 * HB)], att_recv.at[t])
        att = att_s[t].T
        x1 = (x0_s[at, :].astype(F32) + dot(att, wto_s[...])).astype(BF16).astype(F32)
        h2 = norm(x1, tgain[1:2, :]).astype(BF16)
        gate = dot(h2, w_gu_s[0])
        up = dot(h2, w_gu_s[1])
        hidden = (jax.nn.silu(gate) * up).astype(BF16).astype(F32)
        x_sum = x_sum + jnp.where(eight == t, jnp.sum(x1, axis=0, keepdims=True), 0.0)
        h_sum = h_sum + jnp.where(eight == t, jnp.sum(hidden, axis=0, keepdims=True), 0.0)
        return x_sum, h_sum

    @pl.loop(0, 16)
    def _(u):
        j = u % 4
        at = pl.ds(pl.multiple_of(u // 4 * 512, 512), 512)
        q = qk0_s[at, 0:256]
        q = jnp.where(only_head(j, 512, True, True), q, jnp.zeros_like(q))
        e = jnp.exp2(dot_nt(qk0_s[:, 256:512], q) * SCALE).astype(BF16)
        o = dot(vt0_s[pl.ds(pl.multiple_of(j * 64, 64), 64), :], e)
        count = o[SH : SH + 1, :]
        near[pl.ds(pl.multiple_of(j * SH, 16), SH), at] = (o[:SH, :] / count).astype(BF16)
        lane = lax.broadcasted_iota(jnp.int32, (8, 256), 1)
        limit = jnp.where(lane == GW + 1 + j, -bound.astype(F32), 0.0).astype(BF16)
        stats[j, :, at] = dot_nt(limit, q)
        stats[4 + j, :, at] = jnp.broadcast_to(count, (8, 512))

        @pl.when(u == KEYS_AT)
        def _():
            push(kvc1, kv1.at[at1], 13, (grp, (dev + 4) % 8))

            @pl.loop(1, 4)
            def _(i):
                push(kvc3, kv3.at[at3], 2, peer_z(i))
                push(kvc2, kv2.at[at2], 11, peer_z(i))
                push(kvc1, kv1.at[at1], 14, peer_z(i))

        @pl.when(u == HALF_AT)
        def _():
            landed(wto_s.at[pl.ds(0, 672), pl.ds(0, 1152)], recv_sem.at[10])

            @pl.loop(1, 8)
            def _(i):
                half = pl.ds(pl.multiple_of(((dev + i) % 8) * HB + core * 96, 32), 96)
                push(wto_s.at[half], wto_s.at[half], 5, (sibling, dev))

        @pl.when(u == FEED_AT)
        def _():
            own3.wait()
            landed(kv3.at[pl.ds(0, 3 * 16)], recv_sem.at[2])
            own2.wait()
            landed(kv2.at[pl.ds(0, 3 * 64)], recv_sem.at[11])
            landed(kv1.at[at1_y], recv_sem.at[13])

            @pl.loop(1, 4)
            def _(i):
                push(kv3.at[at3_z], kv3.at[at3_z], 3, peer_y(i))
                push(kv2.at[at2_z], kv2.at[at2_z], 12, peer_y(i))
                push(kv1.at[at1_y], kv1.at[at1_y], 14, peer_z(i))

            landed(wto_s.at[pl.ds(0, 672)], recv_sem.at[5])
            ld_gu.wait()
            x_sum, h_sum = lax.fori_loop(
                0, 3, feed, (jnp.zeros((8, TW), F32), jnp.zeros((8, FB), F32))
            )
            x_sum_s[...] = x_sum
            ld_down.wait()
            h_mean = h_sum * (1.0 / TP)
            coarse = h_mean.astype(BF16)
            fine = (h_mean - coarse.astype(F32)).astype(BF16)
            both = jnp.concatenate([coarse.astype(F32), fine.astype(F32)], axis=0).astype(BF16)
            part = dot(both, w_down_s[...])
            pp_s[dev] = part[0:8] + part[8:16]

            @pl.loop(1, 8)
            def _(i):
                push(pp_s.at[dev], pp_s.at[dev], 6, peer8(i))

            landed(kv3.at[pl.ds(0, 3 * 64)], recv_sem.at[3])

            @pl.loop(1, 4)
            def _(i):
                push(kv3.at[at3_y], kv3.at[at3_y], 4, peer_x(i))

        @pl.when(u == EMBED_AT)
        def _():
            ld_in.wait()
            landed(pp_s.at[pl.ds(0, 7)], recv_sem.at[6])
            pooled = x_sum_s[...] * (1.0 / TP) + jnp.sum(pp_s[...], axis=0)
            normed = norm(pooled, tgain[2:3, :]).astype(BF16)
            em[grp] = dot(normed, w_in_s[...]).astype(BF16).astype(F32)

            @pl.loop(1, 16)
            def _(i):
                push(em.at[grp], em.at[grp], 7, peer_grp(i))

            landed(kv2.at[pl.ds(0, 3 * 256)], recv_sem.at[12])
            push(kv2.at[half3], kv2.at[half3], 9, (sibling, dev))

    landed(kv3.at[pl.ds(0, 3 * 256)], recv_sem.at[4])
    push(kv3.at[half3], kv3.at[half3], 8, (sibling, dev))
    landed(em.at[pl.ds(0, 15)], recv_sem.at[7])
    tile = lax.broadcasted_iota(jnp.int32, (48, 128), 0)
    slot = lax.broadcasted_iota(jnp.int32, (48, 128), 1)
    gather = jnp.where(slot == tile // 3 * 8 + tile % 3, 1.0, 0.0).astype(BF16)
    fresh = dot(gather, em[...].reshape(128, SW).astype(BF16))
    fresh = norm(fresh, sgain[...].reshape(1, SW)).astype(BF16)
    for p in range(4):
        new_out[:, p * SW : (p + 1) * SW] = dot(fresh, w_slide_s[p])

    own1.wait()
    landed(kv1.at[pl.ds(0, 6 * 256)], recv_sem.at[14])
    landed(kv3.at[half3], recv_sem.at[8])
    landed(kv2.at[half3], recv_sem.at[9])
    out0.wait()
    out1.wait()

    landed(patches_s.at[pl.ds(0, 672)], send_sem.at[0])
    landed(wto_s.at[pl.ds(0, 672), quarter], send_sem.at[1])
    landed(wto_s.at[pl.ds(0, 672), pl.ds(0, 1152)], send_sem.at[10])
    landed(kv3.at[pl.ds(0, 3 * 16)], send_sem.at[2])
    landed(kv3.at[pl.ds(0, 3 * 64)], send_sem.at[3])
    landed(kv3.at[pl.ds(0, 3 * 256)], send_sem.at[4])
    landed(kv2.at[pl.ds(0, 3 * 64)], send_sem.at[11])
    landed(kv2.at[pl.ds(0, 3 * 256)], send_sem.at[12])
    landed(kv1.at[at1_y], send_sem.at[13])
    landed(kv1.at[pl.ds(0, 6 * 256)], send_sem.at[14])
    landed(wto_s.at[pl.ds(0, 672)], send_sem.at[5])
    landed(pp_s.at[pl.ds(0, 7)], send_sem.at[6])
    landed(em.at[pl.ds(0, 15)], send_sem.at[7])
    landed(kv3.at[half3], send_sem.at[8])
    landed(kv2.at[half3], send_sem.at[9])

    @pl.loop(0, 3)
    def _(t):
        landed(att_s.at[t, pl.ds(0, 7 * HB)], att_send.at[t])


def run_encoder(*args):
    hbm = pl.BlockSpec(memory_space=pl.ANY)
    vmem = pl.BlockSpec(memory_space=pltpu.VMEM)
    shape = jax.ShapeDtypeStruct
    return pl.pallas_call(
        encoder_kernel,
        out_shape=(
            shape((ROWS, 512), BF16),
            shape((256, ROWS), BF16),
            shape((GW, ROWS), BF16),
            shape((8, 8, ROWS), F32),
            shape((256, 384), BF16),
            shape((64, 384), BF16),
            shape((16, 384), BF16),
            shape((2048, 384), BF16),
            shape((2048, 384), BF16),
            shape((2048, 384), BF16),
            shape((16, 8, SW), F32),
            shape((48, 4 * SW), F32),
        ),
        in_specs=[hbm] * 9 + [vmem] * 2 + [pl.BlockSpec(memory_space=pltpu.SMEM)] * 2,
        out_specs=(hbm, hbm, vmem, vmem, vmem, vmem, vmem, hbm, hbm, hbm, vmem, vmem),
        scratch_shapes=[
            pltpu.VMEM((768, 588), BF16),
            pltpu.VMEM((588, TW), BF16),
            pltpu.VMEM((3, HB, TW), BF16),
            pltpu.VMEM((TW, TW), BF16),
            pltpu.VMEM((2, TW, FB), BF16),
            pltpu.VMEM((FB, TW), BF16),
            pltpu.VMEM((TW, SW), BF16),
            pltpu.VMEM((ROWS, SW), BF16),
            pltpu.VMEM((3, SW, SW), BF16),
            pltpu.VMEM((4, SW, SW), BF16),
            pltpu.VMEM((6, ROWS, 128), F32),
            pltpu.VMEM((ROWS, 512), BF16),
            pltpu.VMEM((256, ROWS), BF16),
            pltpu.VMEM((256, 384), BF16),
            pltpu.VMEM((64, 384), BF16),
            pltpu.VMEM((16, 384), BF16),
            pltpu.VMEM((768, TW), BF16),
            pltpu.VMEM((3, TW, TP), BF16),
            pltpu.VMEM((8, 8, TW), F32),
            pltpu.VMEM((1, 256), F32),
            pltpu.VMEM((8, TW), F32),
            pltpu.SemaphoreType.DMA((7,)),
            pltpu.SemaphoreType.DMA((2,)),
            pltpu.SemaphoreType.DMA((5,)),
            pltpu.SemaphoreType.DMA((15,)),
            pltpu.SemaphoreType.DMA((15,)),
            pltpu.SemaphoreType.DMA((3,)),
            pltpu.SemaphoreType.DMA((3,)),
        ],
        compiler_params=pltpu.CompilerParams(
            collective_id=0, has_side_effects=True, vmem_limit_bytes=60 * 1024 * 1024
        ),
        name="encode",
    )(*args)


def slide_kernel(
    positions,
    pattern,
    qk0,
    vt0,
    near,
    stats,
    q1,
    q2,
    q3,
    kv1,
    kv2,
    kv3,
    tokens,
    new,
    em,
    w_so,
    out,
    embed_out,
    qk0_s,
    vt0_s,
    near_s,
    stats_s,
    q1_s,
    q2_s,
    q3_s,
    kv1_s,
    kv2_s,
    kv3_s,
    tok_s,
    far_s,
    wso_s,
    sem,
):
    step = pl.program_id(0)
    place = lax.axis_index("grp") * 8 + lax.axis_index("dev")

    def weights(p):
        group = sum(jnp.where(pattern[g] == p, g, 0) for g in range(4))
        return w_so[pl.ds(pl.multiple_of(group * GW, 64), GW), :]

    @pl.when(step == 0)
    def _():
        copies = [
            pltpu.make_async_copy(src, dst, sem.at[at])
            for at, (src, dst) in enumerate(
                (
                    (q1, q1_s),
                    (q2, q2_s),
                    (q3, q3_s),
                    (kv1, kv1_s),
                    (kv2, kv2_s),
                    (kv3, kv3_s),
                    (tokens, tok_s),
                    (near, near_s),
                    (qk0, qk0_s),
                    (vt0, vt0_s),
                    (stats, stats_s),
                )
            )
        ]
        for copy in copies:
            copy.start()
        for p in range(4):
            wso_s[p * 256 : p * 256 + GW, :] = weights(p)
            wso_s[p * 256 + GW : (p + 1) * 256, :] = jnp.zeros((64, SW), BF16)
        embed_out[...] = em[pl.ds(pl.multiple_of((place // 8) * 8, 8), 8), :][0:3].astype(BF16)
        far_s[...] = jnp.zeros_like(far_s)
        for copy in copies[:7]:
            copy.wait()

        def put(ref, row, vector, columns=None):
            base = pl.multiple_of((row // 16) * 16, 16)
            width = ref.shape[1]
            block = ref[pl.ds(base, 16), :].astype(F32)
            hit = lax.broadcasted_iota(jnp.int32, (16, width), 0) == row - base
            if columns is not None:
                hit = jnp.logical_and(hit, columns)
            ref[pl.ds(base, 16), :] = jnp.where(hit, vector, block).astype(BF16)

        head16 = head_of((16, 384))

        def insert(n, found):
            pos = positions[n]
            owner = jnp.right_shift(pos, 11)
            here = jnp.bitwise_and(pos, ROWS - 1)
            local = owner == place

            @pl.when(local)
            def _():
                put(tok_s, here, em[pl.ds((n // 3) * 8 + n % 3, 1), :])

            for p, q_s, kv_s in ((1, q1_s, kv1_s), (2, q2_s, kv2_s), (3, q3_s, kv3_s)):
                bits = (0, 3, 5, 7)[p]
                member = jnp.bitwise_and(pos, DIL[p] - 1)
                within = jnp.right_shift(owner, bits) == jnp.right_shift(place, bits)
                at = jnp.right_shift(here, bits)

                @pl.when(jnp.logical_and(member < 4, within))
                def _():
                    if p == 1:
                        slot = jnp.bitwise_and(owner, 7)
                    else:
                        grp = jnp.right_shift(owner, 3)
                        of_core = jnp.right_shift(grp, 1) * 8 + jnp.bitwise_and(owner, 7)
                        many = (0, 8, 16, 64)[p]
                        slot = jnp.bitwise_and(grp, 1) * many + jnp.bitwise_and(of_core, many - 1)
                    columns = head16 == member
                    put(
                        kv_s,
                        slot * (ROWS // DIL[p]) + at,
                        new[pl.ds(n, 1), p * SW : p * SW + 384],
                        columns,
                    )

                    @pl.when(local)
                    def _():
                        put(q_s, at, new[pl.ds(n, 1), p * SW + 384 : (p + 1) * SW], columns)

            return found + jnp.where(local, 1, 0)

        found = lax.fori_loop(0, 48, insert, jnp.int32(0))

        for copy in copies[7:]:
            copy.wait()

        @pl.when(jnp.min(stats_s[4:8]) < 2.0**-60)
        def _():
            @pl.loop(0, 16)
            def _(u):
                j = u % 4
                at = pl.ds(pl.multiple_of(u // 4 * 512, 512), 512)
                q = qk0_s[at, 0:256]
                s = dot_nt(
                    qk0_s[:, 256:512], jnp.where(only_head(j, 512, True), q, jnp.zeros_like(q))
                )
                m = jnp.max(s, axis=0, keepdims=True)
                e = jnp.exp2((s - m) * SCALE).astype(BF16)
                o = dot(vt0_s[pl.ds(pl.multiple_of(j * 64, 64), 64), :], e)
                count = o[SH : SH + 1, :]
                rows = pl.ds(pl.multiple_of(j * SH, 16), SH)
                near_s[rows, at] = (o[:SH, :] / count).astype(BF16)
                stats_s[j, :, at] = jnp.broadcast_to(m, (8, 512))
                stats_s[4 + j, :, at] = jnp.broadcast_to(count, (8, 512))

        @pl.when(found > 0)
        def _():
            slots = lax.broadcasted_iota(jnp.int32, (48, 1), 0)
            lanes = lax.broadcasted_iota(jnp.int32, (1, 48), 1)
            nowhere = (jnp.full((48, 1), -1, jnp.int32), jnp.full((1, 48), -1, jnp.int32))
            places, across = lax.fori_loop(
                0,
                48,
                lambda n, held: (
                    jnp.where(slots == n, positions[n], held[0]),
                    jnp.where(lanes == n, positions[n], held[1]),
                ),
                nowhere,
            )
            hide = jnp.where(jnp.right_shift(places, 11) == place, 0.0, HIDE)
            hide = jnp.concatenate([hide] * 4, axis=0)
            hide_across = jnp.where(jnp.right_shift(across, 11) == place, 0.0, HIDE)
            lane = lax.broadcasted_iota(jnp.int32, (48, 256), 1)
            fresh_q = jnp.where(lane == GW, 1.0, new[:, 0:256]).astype(BF16)
            fresh_k = new[:, 256:512].astype(BF16)
            fresh_vt = with_ones(new[:, 512 : 512 + GW].T)

            def stacked(rows, bias):
                return jnp.concatenate(
                    [
                        jnp.where(only_head(j, 48, bias), rows, jnp.zeros_like(rows))
                        for j in range(4)
                    ],
                    axis=0,
                )

            q = stacked(fresh_q, True)
            s_old = dot_nt(q, qk0_s[:, 256:512])
            s_new = dot_nt(q, fresh_k) + hide_across
            m = jnp.maximum(
                jnp.max(s_old, axis=1, keepdims=True), jnp.max(s_new, axis=1, keepdims=True)
            )
            e_old = jnp.exp2((s_old - m) * SCALE).astype(BF16)
            e_new = jnp.exp2((s_new - m) * SCALE).astype(BF16)
            made = []
            for j in range(4):
                head_rows = slice(j * 64, (j + 1) * 64)
                of_head = slice(j * 48, (j + 1) * 48)
                o = dot_nt(vt0_s[head_rows, :], e_old[of_head]) + dot_nt(
                    fresh_vt[head_rows, :], e_new[of_head]
                )
                made.append(o[:SH, :] / o[SH : SH + 1, :])
            made = jnp.concatenate(made, axis=0).astype(BF16)
            k = stacked(fresh_k, False)

            @pl.loop(0, 4)
            def _(b):
                at = pl.ds(pl.multiple_of(b * 512, 512), 512)
                all_s = dot_nt(k, qk0_s[at, 0:256]) + hide
                joined = []
                for j in range(4):
                    s = all_s[j * 48 : (j + 1) * 48, :]
                    m_old = stats_s[j, 0:1, at]
                    m = jnp.maximum(m_old, jnp.max(s, axis=0, keepdims=True))
                    weight = stats_s[4 + j, 0:1, at] * jnp.exp2((m_old - m) * SCALE)
                    e = jnp.exp2((s - m) * SCALE).astype(BF16)
                    o = dot(fresh_vt[j * 64 : (j + 1) * 64, :], e)
                    held = near_s[j * SH : (j + 1) * SH, at].astype(F32)
                    joined.append((held * weight + o[:SH, :]) / (weight + o[SH : SH + 1, :]))
                row = lax.broadcasted_iota(jnp.int32, (48, 512), 1) + (place * ROWS + b * 512)
                hit = jnp.where(row == places, 1.0, 0.0)
                anew = dot(made, hit.astype(BF16))
                taken = jnp.max(hit, axis=0, keepdims=True) > 0.0
                near_s[:, at] = jnp.where(taken, anew, jnp.concatenate(joined, axis=0)).astype(
                    BF16
                )

        def far_heads(p, q_s, kv_s, heads):
            r = DIL[p]
            count = ROWS // r
            q = q_s[...]
            kv = kv_s[...]
            head = head_of((count, 384))
            stack = [jnp.where(head == j, q, jnp.zeros_like(q)) for j in heads]
            _, e, o = attend(jnp.concatenate(stack, axis=0), kv, kv)
            o = o[:, 0:256] / jnp.sum(e.astype(F32), axis=-1, keepdims=True)
            for at, j in enumerate(heads):
                mine = jnp.where(
                    only_head(j, count, False), o[at * count : (at + 1) * count, :], 0.0
                )
                for b in range(2):
                    far_s[2 * (p - 1) + b, pl.ds(j, count, stride=r), :] = mine[
                        :, b * 128 : (b + 1) * 128
                    ]

        for j in range(4):
            far_heads(1, q1_s, kv1_s, (j,))
        far_heads(2, q2_s, kv2_s, (0, 1, 2, 3))
        far_heads(3, q3_s, kv3_s, (0, 1, 2, 3))

    at = pl.ds(pl.multiple_of(step * 512, 512), 512)

    near_t = jnp.concatenate([near_s[:, at], jnp.zeros((64, 512), BF16)], axis=0).T
    far = jnp.concatenate([far_s[b, at, :] for b in range(6)], axis=1).astype(BF16)
    total = tok_s[at, :].astype(F32) + dot(jnp.concatenate([near_t, far], axis=1), wso_s[...])
    out[...] = total.astype(BF16)


def run_slide(*args):
    hbm = pl.BlockSpec(memory_space=pl.ANY)
    vmem = pl.BlockSpec(memory_space=pltpu.VMEM)
    return pl.pallas_call(
        slide_kernel,
        out_shape=(
            jax.ShapeDtypeStruct((ROWS, SW), BF16),
            jax.ShapeDtypeStruct((3, SW), BF16),
        ),
        grid_spec=pltpu.PrefetchScalarGridSpec(
            num_scalar_prefetch=2,
            grid=(4,),
            in_specs=[hbm] * 11 + [vmem] * 3,
            out_specs=(
                pl.BlockSpec((512, SW), lambda i, *_: (i, 0)),
                pl.BlockSpec((3, SW), lambda i, *_: (0, 0)),
            ),
            scratch_shapes=[
                pltpu.VMEM((ROWS, 512), BF16),
                pltpu.VMEM((256, ROWS), BF16),
                pltpu.VMEM((GW, ROWS), BF16),
                pltpu.VMEM((8, 8, ROWS), F32),
                pltpu.VMEM((256, 384), BF16),
                pltpu.VMEM((64, 384), BF16),
                pltpu.VMEM((16, 384), BF16),
                pltpu.VMEM((2048, 384), BF16),
                pltpu.VMEM((2048, 384), BF16),
                pltpu.VMEM((2048, 384), BF16),
                pltpu.VMEM((ROWS, SW), BF16),
                pltpu.VMEM((6, ROWS, 128), F32),
                pltpu.VMEM((1024, SW), BF16),
                pltpu.SemaphoreType.DMA((11,)),
            ],
        ),
        compiler_params=pltpu.CompilerParams(vmem_limit_bytes=56 * 1024 * 1024),
        name="slide",
    )(*args)


def shards(
    tile_patches,
    w_patch,
    w_tqkv,
    w_to,
    w_gu,
    w_down,
    tile_gain,
    w_in,
    slide_tokens,
    slide_gain,
    w_sqkv,
    w_so,
    pattern_of_group,
    new_positions,
):
    qk0, vt0, near, stats, q1, q2, q3, kv1, kv2, kv3, em, new = run_encoder(
        tile_patches,
        w_patch,
        jnp.transpose(w_tqkv, (0, 2, 1)),
        w_to,
        w_gu,
        w_down,
        w_in,
        slide_tokens,
        w_sqkv,
        tile_gain,
        slide_gain,
        new_positions,
        pattern_of_group,
    )
    slide_out, tile_embed = run_slide(
        new_positions,
        pattern_of_group,
        qk0,
        vt0,
        near,
        stats,
        q1,
        q2,
        q3,
        kv1,
        kv2,
        kv3,
        slide_tokens,
        new,
        em.reshape(128, SW),
        w_so,
    )
    return (tile_embed, slide_out)


def solution(mesh):
    placed = (
        P(("grp", "dev"), None),
        P(),
        P(None, None, "dev"),
        P("dev", None),
        P(None, None, "dev"),
        P("dev", None),
        P(),
        P(),
        P(("grp", "dev"), None),
        P(),
        P(),
        P(),
        P(),
        P(),
    )
    return jax.shard_map(
        shards,
        mesh=mesh,
        in_specs=placed,
        out_specs=(P("grp", None), P(("grp", "dev"), None)),
        check_vma=False,
    )
```
